256 devices in a mesh: az: 64 (over y, x_lo, z), ht: 4 (over x_hi, core).
Axes of the slice: x: 4 (x_hi: 2, x_lo: 2; x = x_hi * 2 + x_lo), y: 4, z: 8, core: 2. Of those that a mesh axis runs over, the one named last changes fastest.
Arguments:
- state: float32 [4, 2048, 64, 256], P(None, 'az', 'ht'), may hold values from -6 to 6
- zone_id: int32 [2048, 256], P('az'), may hold values from 0 to 7
- ground_aux: float32 [2048, 256], P('az'), may hold values from -6 to 6
- resistance: float32 [8], replicated, may hold values from 0.3 to 3
- relax_rate: float32 [8], replicated, may hold values from 0.1 to 2.5
- cutoff: int32 [64], replicated, may hold values from 1 to 128, as said below
Outputs:
- filtered_state: float32 [4, 2048, 64, 256], P(None, 'az', 'ht')
The draws below stay inside these ranges and needn't reach their ends.
Inputs may be any that keep to these rules, and one draw needn't show every extreme that they name: `cutoff`: some cycle keeps exactly 128 modes.
All inputs are finite; a program needn't handle non-finite values.
Results may differ from the reference program's by a relative error of at most 0.000064.
Values sent between devices are 32-bit elements; how exact they have to be, the bound alone decides.
No kernel may reach another device: no remote copies, remote signals or barrier semaphores. Data moves between devices by JAX's collectives and lax.ppermute only.
A program may use at most 64 MiB of HBM per device.

```python
import math
import jax
import jax.numpy as jnp

NA = 2048
NI = 64
MODES = 128
ZONES = 8
NR = 256
NZ = 64


def draw_cutoff(key, part):
    first, second = jax.random.split(key)
    counts = jax.random.randint(first, (NI,), 1, MODES + 1)
    spot = jax.random.randint(second, (), 0, NI)
    return jnp.where(jnp.arange(NI) == spot, MODES, counts).astype(jnp.int32)


def set_ends(array, rng, least, largest):
    extent = array.shape
    index_at = [jax.random.randint(jax.random.fold_in(rng, axis), (), 0, extent[axis]) for axis in range(len(extent))]
    array = array.at[tuple(index_at)].set(least)
    longest = extent.index(max(extent))
    index_at[longest] = (index_at[longest] + 1) % extent[longest]
    return array.at[tuple(index_at)].set(largest)


def block_scale(own_key, shape, cuts, low, high):
    gain, own = 1.0, jax.random.fold_in(own_key, 6)
    for position, shards_of in cuts:
        steps = jnp.exp(jax.random.uniform(jax.random.fold_in(own, position), (shards_of,), jnp.float32, low / len(cuts), high / len(cuts)))
        gain = gain * jnp.repeat(steps, shape[position] // shards_of).reshape([-1 if axis == position else 1 for axis in range(len(shape))])
    return gain


def bell_draw(stream_key, dims, scale, reach, cuts=(), kind=jnp.bfloat16):
    drawn = scale * jax.random.normal(stream_key, dims, jnp.float32)
    if cuts:
        drawn = drawn * block_scale(stream_key, dims, cuts, -0.22, 0.18)
    return jnp.clip(drawn, -reach, reach).astype(kind)


def setup_inputs(seed: int = 0) -> dict:
    keys = jax.random.split(jax.random.key(seed), 7)
    return {
        "state": bell_draw(keys[0], (4, NA, NZ, NR), 1.0, 6.0, ((1, 64), (2, 4)), jnp.float32),
        "zone_id": set_ends(jax.random.randint(keys[1], (NA, NR), 0, ZONES), jax.random.fold_in(keys[1], 1), 0, ZONES - 1).astype(jnp.int32),
        "ground_aux": bell_draw(keys[2], (NA, NR), 1.0, 6.0, ((0, 64),), jnp.float32),
        "resistance": jnp.clip(jnp.exp(jax.random.uniform(keys[3], (ZONES,), jnp.float32, math.log(0.3), math.log(3.0))), 0.3, 3.0),
        "relax_rate": jnp.clip(jnp.exp(jax.random.uniform(keys[4], (ZONES,), jnp.float32, math.log(0.1), math.log(2.5))), 0.1, 2.5),
        "cutoff": draw_cutoff(jax.random.fold_in(keys[6], 71), 0),
    }


time_step = 0.4


def radial_terms(total_az, count):
    radius = total_az / (2.0 * math.pi) + jnp.arange(count, dtype=jnp.float32)
    inv_radius = 1.0 / radius
    inv_arc = (total_az / (2.0 * math.pi)) * inv_radius
    return inv_radius, inv_arc


def zone_lookup(zone_id, table):
    match = zone_id[..., None] == jnp.arange(table.shape[0], dtype=jnp.int32)
    return jnp.sum(jnp.where(match, table, jnp.zeros_like(table)), axis=-1)


def radial_diff(field):
    zero = jnp.zeros_like(field[..., :1])
    return 0.5 * (jnp.concatenate([field[..., 1:], zero], -1) - jnp.concatenate([zero, field[..., :-1]], -1))


def tendency(state, az_pad, ht_pad, inv_radius, inv_arc):
    pres, vel_r = state[0], state[1]
    theta_p = 0.5 * (az_pad[0, 2:] - az_pad[0, :-2]) * inv_arc
    theta_t = 0.5 * (az_pad[1, 2:] - az_pad[1, :-2]) * inv_arc
    height_p = 0.5 * (ht_pad[0, :, 2:] - ht_pad[0, :, :-2])
    height_z = 0.5 * (ht_pad[1, :, 2:] - ht_pad[1, :, :-2])
    rate_p = -(radial_diff(vel_r) + vel_r * inv_radius + theta_t + height_z)
    return jnp.stack([rate_p, -radial_diff(pres), -theta_p, -height_p])


def ground_ghost(state, aux, inv_resist):
    wall = (state[0, :, 0, :] - aux) * inv_resist
    return jnp.stack([state[0, :, 0, :], 2.0 * wall - state[3, :, 0, :]])[:, :, None, :]


def full_rates(state, aux, inv_resist, inv_radius, inv_arc):
    pair_t = jnp.stack([state[0], state[2]])
    az_pad = jnp.concatenate([pair_t[:, -1:], pair_t, pair_t[:, :1]], 1)
    pair_z = jnp.stack([state[0], state[3]])
    top = jnp.zeros_like(pair_z[:, :, :1])
    ht_pad = jnp.concatenate([ground_ghost(state, aux, inv_resist), pair_z, top], 2)
    return tendency(state, az_pad, ht_pad, inv_radius, inv_arc)


def reference(state, zone_id, ground_aux, resistance, relax_rate, cutoff):
    inv_radius, inv_arc = radial_terms(NA, NR)
    inv_resist = zone_lookup(zone_id, 1.0 / resistance)
    relax = zone_lookup(zone_id, relax_rate)
    first = full_rates(state, ground_aux, inv_resist, inv_radius, inv_arc)
    middle = state + time_step * first
    mid_aux = ground_aux + time_step * relax * (state[0, :, 0, :] - ground_aux)
    second = full_rates(middle, mid_aux, inv_resist, inv_radius, inv_arc)
    stepped = 0.5 * (state + middle + time_step * second)
    inner = stepped[..., :NI]
    spectrum = jnp.fft.rfft(inner, axis=1)
    keep = jnp.arange(spectrum.shape[1], dtype=jnp.int32)[:, None] < cutoff[None, :]
    spectrum = jnp.where(keep[None, :, None, :], spectrum, jnp.zeros_like(spectrum))
    filtered = jnp.fft.irfft(spectrum, n=NA, axis=1).astype(stepped.dtype)
    return jnp.concatenate([filtered, stepped[..., NI:]], -1)
```

```python
import functools
import math

import jax
import jax.numpy as jnp
import numpy as np
from jax import lax
from jax.experimental import pallas as pl
from jax.experimental.pallas import tpu as pltpu
from jax.sharding import Mesh, PartitionSpec as P

NA = 2048
NI = 64
MODES = 128
ZONES = 8
SECTORS = 64
ROWS = NA // SECTORS
HALF = ROWS // 2
HTS = 16
NR = 256
COMPS = 4
DT = 0.4

AZ = ("y", "x", "z")
SPREAD = ("y", "z", "x")
HT = ("hx", "core")


def sector_of_chunk():
    y, z, x = np.meshgrid(np.arange(4), np.arange(8), np.arange(2), indexing="ij")
    return ((y * 2 + x) * 8 + z).reshape(-1)


def mode_tables():
    azimuth = (sector_of_chunk()[: SECTORS // 2, None] * ROWS + np.arange(HALF)[None, :]).reshape(-1)
    tables = []
    for parity in range(2):
        modes = np.arange(parity, MODES, 2)
        phase = (modes[:, None] * azimuth[None, :] % NA) * (2.0 * math.pi / NA)
        turn = (modes * HALF % NA) * (2.0 * math.pi / NA)
        more = np.zeros((MODES // 2, 128))
        more[:, 0] = np.cos(turn)
        more[:, 1] = np.sin(turn)
        more[:, 2] = np.where(modes == 0, 1.0, 2.0) / NA
        tables.append((np.concatenate([np.cos(phase), np.sin(phase)], 0), more))
    waves, turns = [np.stack(t).astype(np.float32) for t in zip(*tables)]
    return (*split(waves), turns)


def split(x):
    x = x.astype(np.float32) if isinstance(x, np.ndarray) else x
    large = x.astype(jnp.bfloat16)
    return large, (x - large.astype(jnp.float32)).astype(jnp.bfloat16)


def product(a, b, dims):
    dot = functools.partial(lax.dot_general, dimension_numbers=(dims, ((), ())), preferred_element_type=jnp.float32)
    return dot(a[0], b[0]) + (dot(a[0], b[1]) + dot(a[1], b[0]))


def radial_diff(x):
    n = x.shape[-1]
    lane = lax.broadcasted_iota(jnp.int32, (1, n), 1)
    after = jnp.where(lane == NR - 1, 0.0, 0.5)
    before = jnp.where(lane == 0, 0.0, 0.5)
    return after * pltpu.roll(x, n - 1, x.ndim - 1) - before * pltpu.roll(x, 1, x.ndim - 1)


def row_diff(x, low, high):
    up = jnp.concatenate([x[1:], high], 0)
    down = jnp.concatenate([low, x[:-1]], 0)
    return 0.5 * (up - down)


def radial_rates(n):
    lane = lax.broadcasted_iota(jnp.int32, (1, n), 1).astype(jnp.float32)
    inv_r = 1.0 / (NA / (2.0 * math.pi) + lane)
    return inv_r, 0.5 * (NA / (2.0 * math.pi)) * inv_r


def plane(state, comp, height, width=NR):
    return state[comp, :, height, 0:width]


def lookup(ids, table):
    out = jnp.zeros(ids.shape, jnp.float32)
    for k in range(ZONES):
        out = jnp.where(ids == k, table[k], out)
    return out


HT_ROWS = 136
AZ_ROWS = 72


def pack_kernel(state, up, down):
    inv_r, half_arc = radial_rates(NR)
    zero = jnp.zeros((1, NR), jnp.float32)
    for out, edge, inside, sign in ((up, HTS - 1, HTS - 2, 1.0), (down, 0, 1, -1.0)):
        p, w, u, v = [plane(state, i, edge) for i in (0, 3, 1, 2)]
        p_in, w_in = plane(state, 0, inside), plane(state, 3, inside)
        out[0:32] = p
        out[32:64] = w
        turn = 2.0 * row_diff(v, zero, zero) * half_arc
        out[64:96] = p - DT * (radial_diff(u) + u * inv_r + turn - (0.5 * sign) * w_in)
        out[96:128] = w + (0.5 * DT * sign) * p_in
        out[128:129] = v[0:1]
        out[129:130] = v[ROWS - 1 : ROWS]
        out[130:HT_ROWS] = jnp.zeros((HT_ROWS - 130, NR), jnp.float32)


def ground_kernel(resistance, relax, state, zone, aux, ground):
    ids, q = zone[...], aux[...]
    p0, w0 = plane(state, 0, 0), plane(state, 3, 0)
    twice = 2.0 * (1.0 / lookup(ids, resistance))
    ground[0] = twice * (p0 - q) - w0
    ground[1] = twice
    ground[2] = q + DT * lookup(ids, relax) * (p0 - q)


def edge_kernel(flag, state, low, high, ground, to_left, to_right):
    inv_r, half_arc = radial_rates(NR)
    on_ground = flag[0] == 1
    for out, j, inside, sign, corner in ((to_right, ROWS - 1, ROWS - 2, 1.0, 129), (to_left, 0, 1, -1.0, 128)):
        p, u, v, w = [state[i, j] for i in range(4)]
        w_low = jnp.where(on_ground, ground[0, j : j + 1], low[32 + j : 33 + j])
        out[0:16] = p
        out[16:32] = v
        rate = radial_diff(u) + u * inv_r + row_diff(w, w_low, high[32 + j : 33 + j]) - sign * half_arc * state[2, inside]
        out[32:48] = p - DT * rate
        out[48:64] = v + (DT * sign) * half_arc * state[0, inside]
        out[64:65] = low[corner : corner + 1]
        out[65:66] = high[corner : corner + 1]
        out[66:AZ_ROWS] = jnp.zeros((AZ_ROWS - 66, NR), jnp.float32)


def two_stages(width, flag, state, low, high, left, right, ground, mid, ghost, emit):
    on_ground, on_top = flag[0] == 1, flag[1] == 1
    inv_r, half_arc = radial_rates(width)
    cols = slice(0, width)
    turn = DT * half_arc

    p0, p1, u0, v0, w0, w1 = [plane(state, i, k, width) for i, k in ((0, 0), (0, 1), (1, 0), (2, 0), (3, 0), (3, 1))]
    p15, w15 = plane(state, 0, HTS - 1, width), plane(state, 3, HTS - 1, width)
    bp = jnp.where(on_ground, p0, low[0:32, cols])
    bw = jnp.where(on_ground, ground[0, :, cols], low[32:64, cols])
    ghost[0], ghost[1], ghost[2], ghost[3] = bp, bw, high[0:32, cols], high[32:64, cols]

    sub = lax.broadcasted_iota(jnp.int32, (ROWS, width), 0)

    def corners(k):
        return turn * jnp.where(
            sub == 0, left[k : k + 1, cols], jnp.where(sub == ROWS - 1, -right[k : k + 1, cols], 0.0)
        )

    top_p = high[64:96, cols] + (0.5 * DT) * w15 + corners(65)
    top_w = high[96:128, cols] + (0.5 * DT) * p15
    low_p = low[64:96, cols] - (0.5 * DT) * w0 + corners(64)
    low_w = low[96:128, cols] - (0.5 * DT) * p0
    v_diff = 2.0 * row_diff(v0, left[16:17, cols], right[16:17, cols]) * half_arc
    mid_p0 = p0 - DT * (radial_diff(u0) + u0 * inv_r + v_diff + 0.5 * (w1 - bw))
    mid_w0 = w0 - (0.5 * DT) * (p1 - bp)
    ghost[4] = jnp.where(on_ground, mid_p0, low_p)
    ghost[5] = jnp.where(on_ground, ground[1, :, cols] * (mid_p0 - ground[2, :, cols]) - mid_w0, low_w)
    ghost[6] = jnp.where(on_top, 0.0, top_p)
    ghost[7] = jnp.where(on_top, 0.0, top_w)

    mid[0, 0] = left[32:48, cols] - turn * state[2, 0, :, cols]
    mid[2, 0] = left[48:64, cols] - turn * state[0, 0, :, cols]
    mid[0, ROWS + 1] = right[32:48, cols] + turn * state[2, ROWS - 1, :, cols]
    mid[2, ROWS + 1] = right[48:64, cols] + turn * state[0, ROWS - 1, :, cols]

    def rates(p, u, v_diff, p_diff, w, j, first):
        p_low, w_low, p_high, w_high = [ghost[first + i, pl.ds(j, 1)] for i in range(4)]
        return (
            radial_diff(u) + u * inv_r + v_diff * half_arc + row_diff(w, w_low, w_high),
            radial_diff(p),
            half_arc * p_diff,
            row_diff(p, p_low, p_high),
        )

    def first(j, p_diff, v_diff):
        p, u, v, w = [state[i, j, :, cols] for i in range(4)]
        for i, (s, rate) in enumerate(zip((p, u, v, w), rates(p, u, v_diff, p_diff, w, j, 0))):
            mid[i, j + 1] = s - DT * rate

    first(0, state[0, 1, :, cols] - left[0:16, cols], state[2, 1, :, cols] - left[16:32, cols])
    end = ROWS - 2
    first(ROWS - 1, right[0:16, cols] - state[0, end, :, cols], right[16:32, cols] - state[2, end, :, cols])

    @pl.loop(1, ROWS - 1, unroll=5)
    def _(j):
        first(
            j,
            state[0, j + 1, :, cols] - state[0, j - 1, :, cols],
            state[2, j + 1, :, cols] - state[2, j - 1, :, cols],
        )

    def second(j):
        p, u, v, w = [mid[i, j + 1] for i in range(4)]
        found = rates(p, u, mid[2, j + 2] - mid[2, j], mid[0, j + 2] - mid[0, j], w, j, 4)
        return [0.5 * (state[i, j, :, cols] + m - DT * r) for i, (m, r) in enumerate(zip((p, u, v, w), found))]

    @pl.loop(0, HALF, unroll=2)
    def _(l):
        emit(l, second(l), second(l + HALF))


def inner_kernel(flag, state, low, high, left, right, ground, packed, mid, ghost):
    near = lax.broadcasted_iota(jnp.int32, (HTS, 128), 1) < NI

    def emit(l, one, two):
        for i in range(COMPS):
            both = jnp.where(near, one[i], pltpu.roll(two[i], NI, 1))
            packed[pl.ds(i * HTS * HALF + l, HTS, stride=HALF), :] = both

    two_stages(128, flag, state, low, high, left, right, ground, mid, ghost, emit)


def outer_kernel(flag, state, low, high, left, right, ground, stepped, mid, ghost):
    def emit(l, one, two):
        for i in range(COMPS):
            stepped[i, l] = one[i]
            stepped[i, l + HALF] = two[i]

    two_stages(NR, flag, state, low, high, left, right, ground, mid, ghost, emit)


def filter_kernel(large, small, turn, cutoff, x_ref, o_ref):
    n = NA // 4
    first, second = x_ref[:n], x_ref[n:]
    h = MODES // 2
    mode = lax.broadcasted_iota(jnp.int32, (h, 128), 0) * 2
    near = lax.broadcasted_iota(jnp.int32, (h, 128), 1) < NI
    limit = jnp.concatenate([cutoff[...], cutoff[...]], 1)
    outs = []
    for parity in range(2):
        folded = first + second if parity == 0 else first - second
        waves = large[parity], small[parity]
        cs, sn, weight = [turn[parity, :, k : k + 1] for k in range(3)]
        coef = product(waves, split(folded), ((1,), (0,)))
        a, b = coef[:h], coef[h:]
        a_all = jnp.where(near, a, a * cs - b * sn)
        b_all = jnp.where(near, b, a * sn + b * cs)
        keep = jnp.where(mode + parity < limit, weight, 0.0)
        a_all = (a_all + pltpu.roll(a_all, NI, 1)) * keep
        b_all = (b_all + pltpu.roll(b_all, NI, 1)) * keep
        a_back = jnp.where(near, a_all, a_all * cs + b_all * sn)
        b_back = jnp.where(near, b_all, b_all * cs - a_all * sn)
        back = jnp.concatenate([a_back, b_back], 0)
        outs.append(product(waves, split(back), ((0,), (0,))))
    o_ref[:n] = outs[0] + outs[1]
    o_ref[n:] = outs[0] - outs[1]


def merge_kernel(stepped, back, out, rows, tile, beside, sems):
    near = lax.broadcasted_iota(jnp.int32, (HTS, 128), 1) < NI
    loads = [
        pltpu.make_async_copy(stepped.at[i, :, :, pl.ds(0, 128)], beside.at[i], sems.at[0, i]) for i in range(COMPS)
    ]
    for copy in loads:
        copy.start()
    for i in range(COMPS * HTS):
        rows[pl.ds(i // HTS * HTS * HALF + i % HTS, HALF, stride=HTS), :] = back[i * HALF : (i + 1) * HALF]
    stores = []
    for i in range(COMPS):
        loads[i].wait()
        for l in range(HALF):
            at = (i * HALF + l) * HTS
            both = rows[at : at + HTS]
            tile[i, l] = jnp.where(near, both, beside[i, l])
            tile[i, l + HALF] = jnp.where(near, pltpu.roll(both, NI, 1), beside[i, l + HALF])
        stores.append(pltpu.make_async_copy(tile.at[i], out.at[i, :, :, pl.ds(0, 128)], sems.at[1, i]))
        stores[i].start()
    for copy in stores:
        copy.wait()


def per_device(state, zone_id, ground_aux, resistance, relax_rate, cutoff):
    f32 = jnp.float32
    ht = lax.axis_index(HT)
    flags = jnp.stack([ht == 0, ht == 3]).astype(jnp.int32)

    vmem = pl.BlockSpec(memory_space=pltpu.VMEM)
    smem = pl.BlockSpec(memory_space=pltpu.SMEM)
    anywhere = pl.BlockSpec(memory_space=pl.ANY)

    def call(kernel, mib=8, **more):
        return pl.pallas_call(kernel, compiler_params=pltpu.CompilerParams(vmem_limit_bytes=mib * 2**20), **more)

    def shapes(*dims):
        return tuple(jax.ShapeDtypeStruct(d, f32) for d in dims)

    up, down = call(
        pack_kernel, out_shape=shapes((HT_ROWS, NR), (HT_ROWS, NR)), in_specs=[vmem], out_specs=(vmem, vmem), name="pack"
    )(state)
    low = lax.ppermute(up, HT, [(i, i + 1) for i in range(3)])
    high = lax.ppermute(down, HT, [(i + 1, i) for i in range(3)])
    ground = call(
        ground_kernel,
        out_shape=shapes((3, ROWS, NR))[0],
        in_specs=[smem] * 2 + [vmem] * 3,
        out_specs=vmem,
        name="ground",
    )(resistance, relax_rate, state, zone_id, ground_aux)
    to_left, to_right = call(
        edge_kernel,
        out_shape=shapes((AZ_ROWS, NR), (AZ_ROWS, NR)),
        in_specs=[smem] + [vmem] * 4,
        out_specs=(vmem, vmem),
        name="edge",
    )(flags, state, low, high, ground)
    left = lax.ppermute(to_right, AZ, [(i, (i + 1) % SECTORS) for i in range(SECTORS)])
    right = lax.ppermute(to_left, AZ, [((i + 1) % SECTORS, i) for i in range(SECTORS)])

    operands = (flags, state, low, high, left, right, ground)

    def scratch(width):
        return [pltpu.VMEM((COMPS, ROWS + 2, HTS, width), f32), pltpu.VMEM((8, ROWS, width), f32)]

    packed = call(
        inner_kernel,
        mib=12,
        out_shape=shapes((COMPS * HTS * HALF, 128))[0],
        in_specs=[smem] + [vmem] * 6,
        out_specs=vmem,
        scratch_shapes=scratch(128),
        cost_estimate=pl.CostEstimate(flops=10**7, bytes_accessed=6 * 10**6, transcendentals=0),
        name="inner",
    )(*operands)
    circle = lax.all_to_all(packed.reshape(SECTORS, HALF, 128), SPREAD, 0, 0, tiled=True)
    stepped = call(
        outer_kernel,
        mib=16,
        out_shape=shapes((COMPS, ROWS, HTS, NR))[0],
        in_specs=[smem] + [vmem] * 6,
        out_specs=vmem,
        scratch_shapes=scratch(NR),
        cost_estimate=pl.CostEstimate(flops=2 * 10**7, bytes_accessed=2 * 10**7, transcendentals=0),
        name="outer",
    )(*operands)
    kept = call(
        filter_kernel, out_shape=shapes((NA // 2, 128))[0], in_specs=[vmem] * 5, out_specs=vmem, name="filter"
    )(*map(jnp.asarray, mode_tables()), cutoff.reshape(1, NI), circle.reshape(NA // 2, 128))
    back = lax.all_to_all(kept.reshape(SECTORS, HALF, 128), SPREAD, 0, 0, tiled=True)
    return call(
        merge_kernel,
        out_shape=jax.ShapeDtypeStruct(stepped.shape, f32),
        in_specs=[anywhere, vmem],
        out_specs=anywhere,
        scratch_shapes=[
            pltpu.VMEM((COMPS * HTS * HALF, 128), f32),
            pltpu.VMEM((COMPS, ROWS, HTS, 128), f32),
            pltpu.VMEM((COMPS, ROWS, HTS, 128), f32),
            pltpu.SemaphoreType.DMA((2, COMPS)),
        ],
        input_output_aliases={0: 0},
        name="merge",
    )(stepped, back.reshape(COMPS * HTS * HALF, 128))


def solution(mesh):
    fine = Mesh(mesh.devices.reshape(4, 2, 8, 2, 2), AZ + HT)
    return jax.shard_map(
        per_device,
        mesh=fine,
        in_specs=(P(None, AZ, HT, None), P(AZ, None), P(AZ, None), P(), P(), P()),
        out_specs=P(None, AZ, HT, None),
        check_vma=False,
    )
```

```python
import functools
import math

import jax
import jax.numpy as jnp
import numpy as np
from jax import lax
from jax.experimental import pallas as pl
from jax.experimental.pallas import tpu as pltpu
from jax.sharding import Mesh, PartitionSpec as P

NA = 2048
NI = 64
MODES = 128
ZONES = 8
SECTORS = 64
ROWS = NA // SECTORS
HALF = ROWS // 2
LONG = HALF + 1
HTS = 16
NR = 256
COMPS = 4
DT = 0.4

AZ = ("y", "x", "z")
SPREAD = ("y", "z", "x")
HT = ("hx", "core")


def sector_of_chunk():
    y, z, x = np.meshgrid(np.arange(4), np.arange(8), np.arange(2), indexing="ij")
    return ((y * 2 + x) * 8 + z).reshape(-1)


def mode_tables():
    first = sector_of_chunk()[: SECTORS // 2, None] * ROWS
    there = (first - 1 + np.arange(LONG)[None, :]).reshape(-1)
    back = (first + np.arange(HALF)[None, :]).reshape(-1)
    tables = []
    for parity in range(2):
        modes = np.arange(parity, MODES, 2)
        waves = []
        for azimuth in (there, back):
            phase = (modes[:, None] * azimuth[None, :] % NA) * (2.0 * math.pi / NA)
            waves.append(np.concatenate([np.cos(phase), np.sin(phase)], 0))
        more = np.zeros((MODES // 2, 128))
        for k, by in enumerate((LONG, HALF)):
            turn = (modes * by % NA) * (2.0 * math.pi / NA)
            more[:, 2 * k] = np.cos(turn)
            more[:, 2 * k + 1] = np.sin(turn)
        more[:, 4] = np.where(modes == 0, 1.0, 2.0) / NA
        tables.append((*waves, more))
    there, back, turns = [np.stack(t).astype(np.float32) for t in zip(*tables)]
    return (*split(there), *split(back), turns)


def split(x):
    x = x.astype(np.float32) if isinstance(x, np.ndarray) else x
    large = x.astype(jnp.bfloat16)
    return large, (x - large.astype(jnp.float32)).astype(jnp.bfloat16)


def product(a, b, dims):
    dot = functools.partial(lax.dot_general, dimension_numbers=(dims, ((), ())), preferred_element_type=jnp.float32)
    return dot(a[0], b[0]) + (dot(a[0], b[1]) + dot(a[1], b[0]))


def radial_diff(x):
    n = x.shape[-1]
    lane = lax.broadcasted_iota(jnp.int32, (1, n), 1)
    after = jnp.where(lane == NR - 1, 0.0, 0.5)
    before = jnp.where(lane == 0, 0.0, 0.5)
    return after * pltpu.roll(x, n - 1, x.ndim - 1) - before * pltpu.roll(x, 1, x.ndim - 1)


def row_diff(x, low, high):
    up = jnp.concatenate([x[1:], high], 0)
    down = jnp.concatenate([low, x[:-1]], 0)
    return 0.5 * (up - down)


def radial_rates(n):
    lane = lax.broadcasted_iota(jnp.int32, (1, n), 1).astype(jnp.float32)
    inv_r = 1.0 / (NA / (2.0 * math.pi) + lane)
    return inv_r, 0.5 * (NA / (2.0 * math.pi)) * inv_r


def plane(state, comp, height, width=NR):
    return state[comp, :, height, 0:width]


def lookup(ids, table):
    out = jnp.zeros(ids.shape, jnp.float32)
    for k in range(ZONES):
        out = jnp.where(ids == k, table[k], out)
    return out


HT_ROWS = 136
AZ_ROWS = 64


def pack_kernel(state, up, down, to_left, to_right):
    inv_r, half_arc = radial_rates(NR)
    zero = jnp.zeros((1, NR), jnp.float32)
    for out, edge, inside, sign in ((up, HTS - 1, HTS - 2, 1.0), (down, 0, 1, -1.0)):
        p, w, u, v = [plane(state, i, edge) for i in (0, 3, 1, 2)]
        p_in, w_in = plane(state, 0, inside), plane(state, 3, inside)
        out[0:32] = p
        out[32:64] = w
        turn = 2.0 * row_diff(v, zero, zero) * half_arc
        out[64:96] = p - DT * (radial_diff(u) + u * inv_r + turn - (0.5 * sign) * w_in)
        out[96:128] = w + (0.5 * DT * sign) * p_in
        out[128:129] = v[0:1]
        out[129:130] = v[ROWS - 1 : ROWS]
        out[130:HT_ROWS] = jnp.zeros((HT_ROWS - 130, NR), jnp.float32)

    for out, j, inside, sign in ((to_right, ROWS - 1, ROWS - 2, 1.0), (to_left, 0, 1, -1.0)):
        p, u, v, w = [state[i, j] for i in range(4)]
        out[0:16] = p
        out[16:32] = v
        rate = radial_diff(u) + u * inv_r + row_diff(w, zero, zero) - sign * half_arc * state[2, inside]
        out[32:48] = p - DT * rate
        out[48:64] = v + (DT * sign) * half_arc * state[0, inside]


def ground_kernel(resistance, relax, state, zone, aux, ground):
    ids, q = zone[...], aux[...]
    p0, w0 = plane(state, 0, 0), plane(state, 3, 0)
    twice = 2.0 * (1.0 / lookup(ids, resistance))
    ground[0] = twice * (p0 - q) - w0
    ground[1] = twice
    ground[2] = q + DT * lookup(ids, relax) * (p0 - q)


def two_stages(width, flag, state, low, high, left, right, ground, mid, ghost):
    on_ground, on_top = flag[0] == 1, flag[1] == 1
    inv_r, half_arc = radial_rates(width)
    cols = slice(0, width)
    turn = DT * half_arc

    p0, p1, u0, v0, w0, w1 = [plane(state, i, k, width) for i, k in ((0, 0), (0, 1), (1, 0), (2, 0), (3, 0), (3, 1))]
    p15, w15 = plane(state, 0, HTS - 1, width), plane(state, 3, HTS - 1, width)
    bp = jnp.where(on_ground, p0, low[0:32, cols])
    bw = jnp.where(on_ground, ground[0, :, cols], low[32:64, cols])
    ghost[0], ghost[1], ghost[2], ghost[3] = bp, bw, high[0:32, cols], high[32:64, cols]

    top_p = high[64:96, cols] + (0.5 * DT) * w15
    top_w = high[96:128, cols] + (0.5 * DT) * p15
    low_p = low[64:96, cols] - (0.5 * DT) * w0
    low_w = low[96:128, cols] - (0.5 * DT) * p0
    v_diff = 2.0 * row_diff(v0, left[16:17, cols], right[16:17, cols]) * half_arc
    mid_p0 = p0 - DT * (radial_diff(u0) + u0 * inv_r + v_diff + 0.5 * (w1 - bw))
    mid_w0 = w0 - (0.5 * DT) * (p1 - bp)
    ghost[4] = jnp.where(on_ground, mid_p0, low_p)
    ghost[5] = jnp.where(on_ground, ground[1, :, cols] * (mid_p0 - ground[2, :, cols]) - mid_w0, low_w)
    ghost[6] = jnp.where(on_top, 0.0, top_p)
    ghost[7] = jnp.where(on_top, 0.0, top_w)

    mid[0, 0] = left[32:48, cols] - turn * state[2, 0, :, cols]
    mid[2, 0] = left[48:64, cols] - turn * state[0, 0, :, cols]
    mid[0, ROWS + 1] = right[32:48, cols] + turn * state[2, ROWS - 1, :, cols]
    mid[2, ROWS + 1] = right[48:64, cols] + turn * state[0, ROWS - 1, :, cols]

    def rates(p, u, v_diff, p_diff, w, j, first):
        p_low, w_low, p_high, w_high = [ghost[first + i, pl.ds(j, 1)] for i in range(4)]
        return (
            radial_diff(u) + u * inv_r + v_diff * half_arc + row_diff(w, w_low, w_high),
            radial_diff(p),
            half_arc * p_diff,
            row_diff(p, p_low, p_high),
        )

    def first(j, p_diff, v_diff):
        p, u, v, w = [state[i, j, :, cols] for i in range(4)]
        for i, (s, rate) in enumerate(zip((p, u, v, w), rates(p, u, v_diff, p_diff, w, j, 0))):
            mid[i, j + 1] = s - DT * rate

    first(0, state[0, 1, :, cols] - left[0:16, cols], state[2, 1, :, cols] - left[16:32, cols])
    end = ROWS - 2
    first(ROWS - 1, right[0:16, cols] - state[0, end, :, cols], right[16:32, cols] - state[2, end, :, cols])

    @pl.loop(1, ROWS - 1, unroll=5)
    def _(j):
        first(
            j,
            state[0, j + 1, :, cols] - state[0, j - 1, :, cols],
            state[2, j + 1, :, cols] - state[2, j - 1, :, cols],
        )

    def second(j):
        p, u, v, w = [mid[i, j + 1] for i in range(4)]
        found = rates(p, u, mid[2, j + 2] - mid[2, j], mid[0, j + 2] - mid[0, j], w, j, 4)
        return [0.5 * (state[i, j, :, cols] + m - DT * r) for i, (m, r) in enumerate(zip((p, u, v, w), found))]

    return second


def corner_weight(width):
    return (0.5 * DT) * (0.5 * DT) * radial_rates(width)[1]


def inner_kernel(flag, state, low, high, left, right, ground, packed, to_left, to_right, mid, ghost):
    near = lax.broadcasted_iota(jnp.int32, (HTS, 128), 1) < NI
    height = lax.broadcasted_iota(jnp.int32, (HTS, 128), 0)
    second = two_stages(128, flag, state, low, high, left, right, ground, mid, ghost)

    def emit(r, one, two):
        for i in range(COMPS):
            both = jnp.where(near, one[i], pltpu.roll(two[i], NI, 1))
            packed[pl.ds(i * HTS * LONG + r, HTS, stride=LONG), :] = both

    @pl.loop(0, HALF - 1, unroll=3)
    def _(l):
        emit(l + 1, second(l), second(l + LONG))

    weight = corner_weight(128)

    def beyond(row):
        at, end = 32 + row * (ROWS - 1), row * (ROWS - 1)
        w_low = jnp.where(flag[0] == 1, ground[0, end : end + 1], low[at : at + 1])
        return (w_low, high[at : at + 1]), (low[128 + row : 129 + row], high[128 + row : 129 + row])

    def owed(row, sign):
        out = [jnp.zeros((HTS, 128), jnp.float32)] * 2
        for below, above in beyond(row):
            below, above = [(by * weight) * x[:, 0:128] for by, x in ((-sign, below), (sign, above))]
            out.append(jnp.where(height == HTS - 1, above, jnp.where(height == 0, below, 0.0)))
        return out

    emit(0, owed(0, 1.0), second(HALF))
    emit(HALF, second(HALF - 1), owed(1, -1.0))

    for out, row in ((to_left, 0), (to_right, 1)):
        (w_low, w_high), (v_low, v_high) = beyond(row)
        out[...] = jnp.concatenate([w_low, w_high, v_low, v_high, jnp.zeros((4, NR), jnp.float32)], 0)


def outer_kernel(flag, state, low, high, left, right, ground, left_corner, right_corner, stepped, mid, ghost):
    second = two_stages(NR, flag, state, low, high, left, right, ground, mid, ghost)

    @pl.loop(0, ROWS, unroll=2)
    def _(j):
        for i, value in enumerate(second(j)):
            stepped[i, j] = value

    weight = corner_weight(NR)
    for j, corner, sign in ((0, left_corner, -1.0), (ROWS - 1, right_corner, 1.0)):
        for i, k in ((2, 0), (3, 2)):
            stepped[i, j, 0:1] = stepped[i, j, 0:1] - (sign * weight) * corner[k : k + 1]
            end = slice(HTS - 1, HTS)
            stepped[i, j, end] = stepped[i, j, end] + (sign * weight) * corner[k + 1 : k + 2]


def filter_kernel(there, there_small, back, back_small, turn, cutoff, x_ref, o_ref):
    n, m = NA // 4, SECTORS // 2 * LONG
    first, second = x_ref[:m], x_ref[m:]
    h = MODES // 2
    mode = lax.broadcasted_iota(jnp.int32, (h, 128), 0) * 2
    near = lax.broadcasted_iota(jnp.int32, (h, 128), 1) < NI
    limit = jnp.concatenate([cutoff[...], cutoff[...]], 1)
    outs = []
    for parity in range(2):
        folded = first + second if parity == 0 else first - second
        cs, sn, cs_back, sn_back, weight = [turn[parity, :, k : k + 1] for k in range(5)]
        coef = product((there[parity], there_small[parity]), split(folded), ((1,), (0,)))
        a, b = coef[:h], coef[h:]
        a_all = jnp.where(near, a, a * cs - b * sn)
        b_all = jnp.where(near, b, a * sn + b * cs)
        keep = jnp.where(mode + parity < limit, weight, 0.0)
        a_all = (a_all + pltpu.roll(a_all, NI, 1)) * keep
        b_all = (b_all + pltpu.roll(b_all, NI, 1)) * keep
        a_back = jnp.where(near, a_all, a_all * cs_back + b_all * sn_back)
        b_back = jnp.where(near, b_all, b_all * cs_back - a_all * sn_back)
        both = jnp.concatenate([a_back, b_back], 0)
        outs.append(product((back[parity], back_small[parity]), split(both), ((0,), (0,))))
    o_ref[:n] = outs[0] + outs[1]
    o_ref[n:] = outs[0] - outs[1]


def merge_kernel(stepped, back, out, rows, tile, beside, sems):
    near = lax.broadcasted_iota(jnp.int32, (HTS, 128), 1) < NI
    loads = [
        pltpu.make_async_copy(stepped.at[i, :, :, pl.ds(0, 128)], beside.at[i], sems.at[0, i]) for i in range(COMPS)
    ]
    for copy in loads:
        copy.start()
    for i in range(COMPS * HTS):
        rows[pl.ds(i // HTS * HTS * HALF + i % HTS, HALF, stride=HTS), :] = back[i * HALF : (i + 1) * HALF]
    stores = []
    for i in range(COMPS):
        loads[i].wait()
        for l in range(HALF):
            at = (i * HALF + l) * HTS
            both = rows[at : at + HTS]
            tile[i, l] = jnp.where(near, both, beside[i, l])
            tile[i, l + HALF] = jnp.where(near, pltpu.roll(both, NI, 1), beside[i, l + HALF])
        stores.append(pltpu.make_async_copy(tile.at[i], out.at[i, :, :, pl.ds(0, 128)], sems.at[1, i]))
        stores[i].start()
    for copy in stores:
        copy.wait()


def per_device(state, zone_id, ground_aux, resistance, relax_rate, cutoff):
    f32 = jnp.float32
    ht = lax.axis_index(HT)
    flags = jnp.stack([ht == 0, ht == 3]).astype(jnp.int32)

    vmem = pl.BlockSpec(memory_space=pltpu.VMEM)
    smem = pl.BlockSpec(memory_space=pltpu.SMEM)
    anywhere = pl.BlockSpec(memory_space=pl.ANY)

    def call(kernel, mib=8, **more):
        return pl.pallas_call(kernel, compiler_params=pltpu.CompilerParams(vmem_limit_bytes=mib * 2**20), **more)

    def shapes(*dims):
        return tuple(jax.ShapeDtypeStruct(d, f32) for d in dims)

    up, down, to_left, to_right = call(
        pack_kernel,
        out_shape=shapes((HT_ROWS, NR), (HT_ROWS, NR), (AZ_ROWS, NR), (AZ_ROWS, NR)),
        in_specs=[vmem],
        out_specs=(vmem,) * 4,
        name="pack",
    )(state)
    ground = call(
        ground_kernel,
        out_shape=shapes((3, ROWS, NR))[0],
        in_specs=[smem] * 2 + [vmem] * 3,
        out_specs=vmem,
        name="ground",
    )(resistance, relax_rate, state, zone_id, ground_aux)
    to_next, to_last = [(i, (i + 1) % SECTORS) for i in range(SECTORS)], [((i + 1) % SECTORS, i) for i in range(SECTORS)]
    low = lax.ppermute(up, HT, [(i, i + 1) for i in range(3)])
    high = lax.ppermute(down, HT, [(i + 1, i) for i in range(3)])
    left = lax.ppermute(to_right, AZ, to_next)
    right = lax.ppermute(to_left, AZ, to_last)

    operands = (flags, state, low, high, left, right, ground)

    def scratch(width):
        return [pltpu.VMEM((COMPS, ROWS + 2, HTS, width), f32), pltpu.VMEM((8, ROWS, width), f32)]

    packed, to_left, to_right = call(
        inner_kernel,
        mib=12,
        out_shape=shapes((COMPS * HTS * LONG, 128), (8, NR), (8, NR)),
        in_specs=[smem] + [vmem] * 6,
        out_specs=(vmem,) * 3,
        scratch_shapes=scratch(128),
        cost_estimate=pl.CostEstimate(flops=10**7, bytes_accessed=6 * 10**6, transcendentals=0),
        name="inner",
    )(*operands)
    circle = lax.all_to_all(packed.reshape(SECTORS, LONG, 1, 128), SPREAD, 0, 0, tiled=True)
    left_corner = lax.ppermute(to_right, AZ, to_next)
    right_corner = lax.ppermute(to_left, AZ, to_last)
    stepped = call(
        outer_kernel,
        mib=16,
        out_shape=shapes((COMPS, ROWS, HTS, NR))[0],
        in_specs=[smem] + [vmem] * 8,
        out_specs=vmem,
        scratch_shapes=scratch(NR),
        cost_estimate=pl.CostEstimate(flops=2 * 10**7, bytes_accessed=2 * 10**7, transcendentals=0),
        name="outer",
    )(*operands, left_corner, right_corner)
    kept = call(
        filter_kernel, out_shape=shapes((NA // 2, 128))[0], in_specs=[vmem] * 7, out_specs=vmem, name="filter"
    )(*map(jnp.asarray, mode_tables()), cutoff.reshape(1, NI), circle.reshape(SECTORS * LONG, 128))
    back = lax.all_to_all(kept.reshape(SECTORS, HALF, 128), SPREAD, 0, 0, tiled=True)
    return call(
        merge_kernel,
        out_shape=jax.ShapeDtypeStruct(stepped.shape, f32),
        in_specs=[anywhere, vmem],
        out_specs=anywhere,
        scratch_shapes=[
            pltpu.VMEM((COMPS * HTS * HALF, 128), f32),
            pltpu.VMEM((COMPS, ROWS, HTS, 128), f32),
            pltpu.VMEM((COMPS, ROWS, HTS, 128), f32),
            pltpu.SemaphoreType.DMA((2, COMPS)),
        ],
        input_output_aliases={0: 0},
        name="merge",
    )(stepped, back.reshape(COMPS * HTS * HALF, 128))


def solution(mesh):
    fine = Mesh(mesh.devices.reshape(4, 2, 8, 2, 2), AZ + HT)
    return jax.shard_map(
        per_device,
        mesh=fine,
        in_specs=(P(None, AZ, HT, None), P(AZ, None), P(AZ, None), P(), P(), P()),
        out_specs=P(None, AZ, HT, None),
        check_vma=False,
    )
```

```python
import functools
import math

import jax
import jax.numpy as jnp
import numpy as np
from jax import lax
from jax.experimental import pallas as pl
from jax.experimental.pallas import tpu as pltpu
from jax.sharding import Mesh, PartitionSpec as P

NA = 2048
NI = 64
MODES = 128
ZONES = 8
SECTORS = 64
ROWS = NA // SECTORS
HALF = ROWS // 2
LONG = HALF + 1
HTS = 16
NR = 256
COMPS = 4
DT = 0.4

AZ = ("y", "x", "z")
SPREAD = ("y", "z", "x")
HT = ("hx", "core")


def sector_of_chunk():
    y, z, x = np.meshgrid(np.arange(4), np.arange(8), np.arange(2), indexing="ij")
    return ((y * 2 + x) * 8 + z).reshape(-1)


def mode_tables():
    first = sector_of_chunk()[: SECTORS // 2, None] * ROWS
    there = (first - 1 + np.arange(LONG)[None, :]).reshape(-1)
    back = (first + np.arange(HALF)[None, :]).reshape(-1)
    tables = []
    for parity in range(2):
        modes = np.arange(parity, MODES, 2)
        waves = []
        for azimuth in (there, back):
            phase = (modes[:, None] * azimuth[None, :] % NA) * (2.0 * math.pi / NA)
            waves.append(np.concatenate([np.cos(phase), np.sin(phase)], 0))
        more = np.zeros((MODES // 2, 128))
        for k, by in enumerate((LONG, HALF)):
            turn = (modes * by % NA) * (2.0 * math.pi / NA)
            more[:, 2 * k] = np.cos(turn)
            more[:, 2 * k + 1] = np.sin(turn)
        more[:, 4] = np.where(modes == 0, 1.0, 2.0) / NA
        tables.append((*waves, more))
    there, back, turns = [np.stack(t).astype(np.float32) for t in zip(*tables)]
    return (*split(there), *split(back), turns)


def split(x):
    x = x.astype(np.float32) if isinstance(x, np.ndarray) else x
    large = x.astype(jnp.bfloat16)
    return large, (x - large.astype(jnp.float32)).astype(jnp.bfloat16)


def product(a, b, dims):
    dot = functools.partial(lax.dot_general, dimension_numbers=(dims, ((), ())), preferred_element_type=jnp.float32)
    return dot(a[0], b[0]) + (dot(a[0], b[1]) + dot(a[1], b[0]))


def radial_diff(x):
    n = x.shape[-1]
    lane = lax.broadcasted_iota(jnp.int32, (1, n), 1)
    after = jnp.where(lane == NR - 1, 0.0, 0.5)
    before = jnp.where(lane == 0, 0.0, 0.5)
    return after * pltpu.roll(x, n - 1, x.ndim - 1) - before * pltpu.roll(x, 1, x.ndim - 1)


def row_diff(x, low, high):
    up = jnp.concatenate([x[1:], high], 0)
    down = jnp.concatenate([low, x[:-1]], 0)
    return 0.5 * (up - down)


def radial_rates(n):
    lane = lax.broadcasted_iota(jnp.int32, (1, n), 1).astype(jnp.float32)
    inv_r = 1.0 / (NA / (2.0 * math.pi) + lane)
    return inv_r, 0.5 * (NA / (2.0 * math.pi)) * inv_r


def plane(state, comp, height, width=NR):
    return state[comp, :, height, 0:width]


def lookup(ids, table):
    out = jnp.zeros(ids.shape, jnp.float32)
    for k in range(ZONES):
        out = jnp.where(ids == k, table[k], out)
    return out


HT_ROWS = 136
AZ_ROWS = 64


def pack_kernel(flag, state, ht_first, ht_then, az_first, az_then, up, down, to_left, to_right):
    inv_r, half_arc = radial_rates(NR)
    zero = jnp.zeros((1, NR), jnp.float32)
    for out, edge, inside, sign in ((up, HTS - 1, HTS - 2, 1.0), (down, 0, 1, -1.0)):
        p, w, u, v = [plane(state, i, edge) for i in (0, 3, 1, 2)]
        p_in, w_in = plane(state, 0, inside), plane(state, 3, inside)
        out[0:32] = p
        out[32:64] = w
        turn = 2.0 * row_diff(v, zero, zero) * half_arc
        out[64:96] = p - DT * (radial_diff(u) + u * inv_r + turn - (0.5 * sign) * w_in)
        out[96:128] = w + (0.5 * DT * sign) * p_in
        out[128:129] = v[0:1]
        out[129:130] = v[ROWS - 1 : ROWS]
        out[130:HT_ROWS] = jnp.zeros((HT_ROWS - 130, NR), jnp.float32)

    for out, j, inside, sign in ((to_right, ROWS - 1, ROWS - 2, 1.0), (to_left, 0, 1, -1.0)):
        p, u, v, w = [state[i, j] for i in range(4)]
        out[0:16] = p
        out[16:32] = v
        rate = radial_diff(u) + u * inv_r + row_diff(w, zero, zero) - sign * half_arc * state[2, inside]
        out[32:48] = p - DT * rate
        out[48:64] = v + (DT * sign) * half_arc * state[0, inside]

    for odd, one, two, ahead, behind in (
        (flag[2] == 1, ht_first, ht_then, up, down),
        (flag[3] == 1, az_first, az_then, to_right, to_left),
    ):
        one[...] = jnp.where(odd, behind[...], ahead[...])
        two[...] = jnp.where(odd, ahead[...], behind[...])


def ground_kernel(resistance, relax, state, zone, aux, ground):
    ids, q = zone[...], aux[...]
    p0, w0 = plane(state, 0, 0), plane(state, 3, 0)
    twice = 2.0 * (1.0 / lookup(ids, resistance))
    ground[0] = twice * (p0 - q) - w0
    ground[1] = twice
    ground[2] = q + DT * lookup(ids, relax) * (p0 - q)


def unswap(flag, place, first, then, behind, ahead):
    behind[...] = jnp.where(flag[place] == 1, first[...], then[...])
    ahead[...] = jnp.where(flag[place] == 1, then[...], first[...])


def two_stages(width, flag, state, low, high, left, right, ground, mid, ghost):
    on_ground, on_top = flag[0] == 1, flag[1] == 1
    inv_r, half_arc = radial_rates(width)
    cols = slice(0, width)
    turn = DT * half_arc

    p0, p1, u0, v0, w0, w1 = [plane(state, i, k, width) for i, k in ((0, 0), (0, 1), (1, 0), (2, 0), (3, 0), (3, 1))]
    p15, w15 = plane(state, 0, HTS - 1, width), plane(state, 3, HTS - 1, width)
    bp = jnp.where(on_ground, p0, low[0:32, cols])
    bw = jnp.where(on_ground, ground[0, :, cols], low[32:64, cols])
    ghost[0], ghost[1], ghost[2], ghost[3] = bp, bw, high[0:32, cols], high[32:64, cols]

    top_p = high[64:96, cols] + (0.5 * DT) * w15
    top_w = high[96:128, cols] + (0.5 * DT) * p15
    low_p = low[64:96, cols] - (0.5 * DT) * w0
    low_w = low[96:128, cols] - (0.5 * DT) * p0
    v_diff = 2.0 * row_diff(v0, left[16:17, cols], right[16:17, cols]) * half_arc
    mid_p0 = p0 - DT * (radial_diff(u0) + u0 * inv_r + v_diff + 0.5 * (w1 - bw))
    mid_w0 = w0 - (0.5 * DT) * (p1 - bp)
    ghost[4] = jnp.where(on_ground, mid_p0, low_p)
    ghost[5] = jnp.where(on_ground, ground[1, :, cols] * (mid_p0 - ground[2, :, cols]) - mid_w0, low_w)
    ghost[6] = jnp.where(on_top, 0.0, top_p)
    ghost[7] = jnp.where(on_top, 0.0, top_w)

    mid[0, 0] = left[32:48, cols] - turn * state[2, 0, :, cols]
    mid[2, 0] = left[48:64, cols] - turn * state[0, 0, :, cols]
    mid[0, ROWS + 1] = right[32:48, cols] + turn * state[2, ROWS - 1, :, cols]
    mid[2, ROWS + 1] = right[48:64, cols] + turn * state[0, ROWS - 1, :, cols]

    def rates(p, u, v_diff, p_diff, w, j, first):
        p_low, w_low, p_high, w_high = [ghost[first + i, pl.ds(j, 1)] for i in range(4)]
        return (
            radial_diff(u) + u * inv_r + v_diff * half_arc + row_diff(w, w_low, w_high),
            radial_diff(p),
            half_arc * p_diff,
            row_diff(p, p_low, p_high),
        )

    def first(j, p_diff, v_diff):
        p, u, v, w = [state[i, j, :, cols] for i in range(4)]
        for i, (s, rate) in enumerate(zip((p, u, v, w), rates(p, u, v_diff, p_diff, w, j, 0))):
            mid[i, j + 1] = s - DT * rate

    first(0, state[0, 1, :, cols] - left[0:16, cols], state[2, 1, :, cols] - left[16:32, cols])
    end = ROWS - 2
    first(ROWS - 1, right[0:16, cols] - state[0, end, :, cols], right[16:32, cols] - state[2, end, :, cols])

    @pl.loop(1, ROWS - 1, unroll=5)
    def _(j):
        first(
            j,
            state[0, j + 1, :, cols] - state[0, j - 1, :, cols],
            state[2, j + 1, :, cols] - state[2, j - 1, :, cols],
        )

    def second(j):
        p, u, v, w = [mid[i, j + 1] for i in range(4)]
        found = rates(p, u, mid[2, j + 2] - mid[2, j], mid[0, j + 2] - mid[0, j], w, j, 4)
        return [0.5 * (state[i, j, :, cols] + m - DT * r) for i, (m, r) in enumerate(zip((p, u, v, w), found))]

    return second


def corner_weight(width):
    return (0.5 * DT) * (0.5 * DT) * radial_rates(width)[1]


def inner_kernel(
    flag, state, ht_first, ht_then, az_first, az_then, ground, packed, low, high, left, right, to_left, to_right, mid, ghost
):
    unswap(flag, 2, ht_first, ht_then, low, high)
    unswap(flag, 3, az_first, az_then, left, right)
    near = lax.broadcasted_iota(jnp.int32, (HTS, 128), 1) < NI
    height = lax.broadcasted_iota(jnp.int32, (HTS, 128), 0)
    second = two_stages(128, flag, state, low, high, left, right, ground, mid, ghost)

    def emit(r, one, two):
        for i in range(COMPS):
            both = jnp.where(near, one[i], pltpu.roll(two[i], NI, 1))
            packed[pl.ds(i * HTS * LONG + r, HTS, stride=LONG), :] = both

    @pl.loop(0, HALF - 1, unroll=3)
    def _(l):
        emit(l + 1, second(l), second(l + LONG))

    weight = corner_weight(128)

    def beyond(row):
        at, end = 32 + row * (ROWS - 1), row * (ROWS - 1)
        w_low = jnp.where(flag[0] == 1, ground[0, end : end + 1], low[at : at + 1])
        return (w_low, high[at : at + 1]), (low[128 + row : 129 + row], high[128 + row : 129 + row])

    def owed(row, sign):
        out = [jnp.zeros((HTS, 128), jnp.float32)] * 2
        for below, above in beyond(row):
            below, above = [(by * weight) * x[:, 0:128] for by, x in ((-sign, below), (sign, above))]
            out.append(jnp.where(height == HTS - 1, above, jnp.where(height == 0, below, 0.0)))
        return out

    emit(0, owed(0, 1.0), second(HALF))
    emit(HALF, second(HALF - 1), owed(1, -1.0))

    for out, row in ((to_left, 0), (to_right, 1)):
        (w_low, w_high), (v_low, v_high) = beyond(row)
        out[...] = jnp.concatenate([w_low, w_high, v_low, v_high, jnp.zeros((4, NR), jnp.float32)], 0)


def outer_kernel(flag, state, low, high, left, right, ground, stepped, mid, ghost):
    second = two_stages(NR, flag, state, low, high, left, right, ground, mid, ghost)

    @pl.loop(0, ROWS, unroll=2)
    def _(j):
        for i, value in enumerate(second(j)):
            stepped[i, j] = value


def filter_kernel(there, there_small, back, back_small, turn, cutoff, x_ref, o_ref):
    n, m = NA // 4, SECTORS // 2 * LONG
    first, second = x_ref[:m], x_ref[m:]
    h = MODES // 2
    mode = lax.broadcasted_iota(jnp.int32, (h, 128), 0) * 2
    near = lax.broadcasted_iota(jnp.int32, (h, 128), 1) < NI
    limit = jnp.concatenate([cutoff[...], cutoff[...]], 1)
    outs = []
    for parity in range(2):
        folded = first + second if parity == 0 else first - second
        cs, sn, cs_back, sn_back, weight = [turn[parity, :, k : k + 1] for k in range(5)]
        coef = product((there[parity], there_small[parity]), split(folded), ((1,), (0,)))
        a, b = coef[:h], coef[h:]
        a_all = jnp.where(near, a, a * cs - b * sn)
        b_all = jnp.where(near, b, a * sn + b * cs)
        keep = jnp.where(mode + parity < limit, weight, 0.0)
        a_all = (a_all + pltpu.roll(a_all, NI, 1)) * keep
        b_all = (b_all + pltpu.roll(b_all, NI, 1)) * keep
        a_back = jnp.where(near, a_all, a_all * cs_back + b_all * sn_back)
        b_back = jnp.where(near, b_all, b_all * cs_back - a_all * sn_back)
        both = jnp.concatenate([a_back, b_back], 0)
        outs.append(product((back[parity], back_small[parity]), split(both), ((0,), (0,))))
    o_ref[:n] = outs[0] + outs[1]
    o_ref[n:] = outs[0] - outs[1]


def merge_kernel(stepped, back, left_corner, right_corner, out, rows, tile, beside, edges, sems, edge_sems):
    near = lax.broadcasted_iota(jnp.int32, (HTS, 128), 1) < NI
    height = lax.broadcasted_iota(jnp.int32, (HTS, NR), 0)
    loads = [
        pltpu.make_async_copy(stepped.at[i, :, :, pl.ds(0, 128)], beside.at[i], sems.at[0, i]) for i in range(COMPS)
    ]
    places = [(k, i, j) for k, (i, j) in enumerate(((2, 0), (2, ROWS - 1), (3, 0), (3, ROWS - 1)))]
    edge_loads = [
        pltpu.make_async_copy(stepped.at[i, j, :, pl.ds(128, 128)], edges.at[k], edge_sems.at[0, k]) for k, i, j in places
    ]
    for copy in loads + edge_loads:
        copy.start()

    weight = corner_weight(NR)
    owed = {}
    for k, i, j in places:
        corner, sign = (left_corner, -1.0) if j == 0 else (right_corner, 1.0)
        at = 2 * (i - 2)
        below, above = (-sign * weight) * corner[at : at + 1], (sign * weight) * corner[at + 1 : at + 2]
        owed[i, j] = jnp.where(height == HTS - 1, above, jnp.where(height == 0, below, 0.0))

    for i in range(COMPS * HTS):
        rows[pl.ds(i // HTS * HTS * HALF + i % HTS, HALF, stride=HTS), :] = back[i * HALF : (i + 1) * HALF]
    stores = []
    for i in range(COMPS):
        loads[i].wait()
        for j in (0, ROWS - 1):
            if i >= 2:
                beside[i, j] = beside[i, j] + owed[i, j][:, 0:128]
        for l in range(HALF):
            at = (i * HALF + l) * HTS
            both = rows[at : at + HTS]
            tile[i, l] = jnp.where(near, both, beside[i, l])
            tile[i, l + HALF] = jnp.where(near, pltpu.roll(both, NI, 1), beside[i, l + HALF])
        stores.append(pltpu.make_async_copy(tile.at[i], out.at[i, :, :, pl.ds(0, 128)], sems.at[1, i]))
        stores[i].start()
    for k, i, j in places:
        edge_loads[k].wait()
        edges[k] = edges[k] + owed[i, j][:, 128:NR]
        stores.append(pltpu.make_async_copy(edges.at[k], out.at[i, j, :, pl.ds(128, 128)], edge_sems.at[1, k]))
        stores[-1].start()
    for copy in stores:
        copy.wait()


def per_device(state, zone_id, ground_aux, resistance, relax_rate, cutoff):
    f32 = jnp.float32
    ht = lax.axis_index(HT)
    flags = jnp.stack([ht == 0, ht == 3, lax.axis_index("core") == 1, lax.axis_index("z") % 2 == 1]).astype(jnp.int32)

    vmem = pl.BlockSpec(memory_space=pltpu.VMEM)
    smem = pl.BlockSpec(memory_space=pltpu.SMEM)
    anywhere = pl.BlockSpec(memory_space=pl.ANY)

    def call(kernel, mib=8, **more):
        return pl.pallas_call(kernel, compiler_params=pltpu.CompilerParams(vmem_limit_bytes=mib * 2**20), **more)

    def shapes(*dims):
        return tuple(jax.ShapeDtypeStruct(d, f32) for d in dims)

    ht_message, az_message = (HT_ROWS, NR), (AZ_ROWS, NR)
    ht_first, ht_then, az_first, az_then = call(
        pack_kernel,
        out_shape=shapes(ht_message, ht_message, az_message, az_message),
        in_specs=[smem, vmem],
        out_specs=(vmem,) * 4,
        scratch_shapes=[pltpu.VMEM(m, f32) for m in (ht_message, ht_message, az_message, az_message)],
        name="pack",
    )(flags, state)
    ground = call(
        ground_kernel,
        out_shape=shapes((3, ROWS, NR))[0],
        in_specs=[smem] * 2 + [vmem] * 3,
        out_specs=vmem,
        name="ground",
    )(resistance, relax_rate, state, zone_id, ground_aux)
    def swap(x, axes, size, start, closed):
        pairs = [(i % size, (i + 1) % size) for i in range(start, size if closed else size - 1, 2)]
        return lax.ppermute(x, axes, pairs + [(b, a) for a, b in pairs])

    swaps = (
        swap(ht_first, HT, 4, 0, False),
        swap(ht_then, HT, 4, 1, False),
        swap(az_first, AZ, SECTORS, 0, True),
        swap(az_then, AZ, SECTORS, 1, True),
    )

    def scratch(width):
        return [pltpu.VMEM((COMPS, ROWS + 2, HTS, width), f32), pltpu.VMEM((8, ROWS, width), f32)]

    packed, low, high, left, right, to_left, to_right = call(
        inner_kernel,
        mib=12,
        out_shape=shapes(
            (COMPS * HTS * LONG, 128), ht_message, ht_message, az_message, az_message, (8, NR), (8, NR)
        ),
        in_specs=[smem] + [vmem] * 6,
        out_specs=(vmem,) * 7,
        scratch_shapes=scratch(128),
        cost_estimate=pl.CostEstimate(flops=10**7, bytes_accessed=6 * 10**6, transcendentals=0),
        name="inner",
    )(flags, state, *swaps, ground)
    circle = lax.all_to_all(packed.reshape(SECTORS, LONG, 1, 128), SPREAD, 0, 0, tiled=True)
    left_corner = lax.ppermute(to_right, AZ, [(i, (i + 1) % SECTORS) for i in range(SECTORS)])
    right_corner = lax.ppermute(to_left, AZ, [((i + 1) % SECTORS, i) for i in range(SECTORS)])
    stepped = call(
        outer_kernel,
        mib=16,
        out_shape=shapes((COMPS, ROWS, HTS, NR))[0],
        in_specs=[smem] + [vmem] * 6,
        out_specs=vmem,
        scratch_shapes=scratch(NR),
        cost_estimate=pl.CostEstimate(flops=2 * 10**7, bytes_accessed=2 * 10**7, transcendentals=0),
        name="outer",
    )(flags, state, low, high, left, right, ground)
    kept = call(
        filter_kernel, out_shape=shapes((NA // 2, 128))[0], in_specs=[vmem] * 7, out_specs=vmem, name="filter"
    )(*map(jnp.asarray, mode_tables()), cutoff.reshape(1, NI), circle.reshape(SECTORS * LONG, 128))
    back = lax.all_to_all(kept.reshape(SECTORS, HALF, 128), SPREAD, 0, 0, tiled=True)
    return call(
        merge_kernel,
        out_shape=jax.ShapeDtypeStruct(stepped.shape, f32),
        in_specs=[anywhere] + [vmem] * 3,
        out_specs=anywhere,
        scratch_shapes=[
            pltpu.VMEM((COMPS * HTS * HALF, 128), f32),
            pltpu.VMEM((COMPS, ROWS, HTS, 128), f32),
            pltpu.VMEM((COMPS, ROWS, HTS, 128), f32),
            pltpu.VMEM((4, HTS, 128), f32),
            pltpu.SemaphoreType.DMA((2, COMPS)),
            pltpu.SemaphoreType.DMA((2, 4)),
        ],
        input_output_aliases={0: 0},
        name="merge",
    )(stepped, back.reshape(COMPS * HTS * HALF, 128), left_corner, right_corner)


def solution(mesh):
    fine = Mesh(mesh.devices.reshape(4, 2, 8, 2, 2), AZ + HT)
    return jax.shard_map(
        per_device,
        mesh=fine,
        in_specs=(P(None, AZ, HT, None), P(AZ, None), P(AZ, None), P(), P(), P()),
        out_specs=P(None, AZ, HT, None),
        check_vma=False,
    )
```

```python
import functools
import math

import jax
import jax.numpy as jnp
import numpy as np
from jax import lax
from jax.experimental import pallas as pl
from jax.experimental.pallas import tpu as pltpu
from jax.sharding import Mesh, PartitionSpec as P

NA = 2048
NI = 64
MODES = 128
ZONES = 8
SECTORS = 64
ROWS = NA // SECTORS
HALF = ROWS // 2
LONG = HALF + 1
HTS = 16
NR = 256
COMPS = 4
DT = 0.4

AZ = ("y", "x", "z")
SPREAD = ("y", "z", "x")
HT = ("hx", "core")


def sector_of_chunk():
    y, z, x = np.meshgrid(np.arange(4), np.arange(8), np.arange(2), indexing="ij")
    return ((y * 2 + x) * 8 + z).reshape(-1)


def mode_tables():
    first = sector_of_chunk()[: SECTORS // 2, None] * ROWS
    there = (first - 1 + np.arange(LONG)[None, :]).reshape(-1)
    back = (first + np.arange(HALF)[None, :]).reshape(-1)
    tables = []
    for parity in range(2):
        modes = np.arange(parity, MODES, 2)
        waves = []
        for azimuth in (there, back):
            phase = (modes[:, None] * azimuth[None, :] % NA) * (2.0 * math.pi / NA)
            waves.append(np.concatenate([np.cos(phase), np.sin(phase)], 0))
        more = np.zeros((MODES // 2, 128))
        for k, by in enumerate((LONG, HALF)):
            turn = (modes * by % NA) * (2.0 * math.pi / NA)
            more[:, 2 * k] = np.cos(turn)
            more[:, 2 * k + 1] = np.sin(turn)
        more[:, 4] = np.where(modes == 0, 1.0, 2.0) / NA
        tables.append((*waves, more))
    there, back, turns = [np.stack(t).astype(np.float32) for t in zip(*tables)]
    return (*split(there), *split(back), turns)


def split(x):
    x = x.astype(np.float32) if isinstance(x, np.ndarray) else x
    large = x.astype(jnp.bfloat16)
    return large, (x - large.astype(jnp.float32)).astype(jnp.bfloat16)


def product(a, b, dims):
    dot = functools.partial(lax.dot_general, dimension_numbers=(dims, ((), ())), preferred_element_type=jnp.float32)
    return dot(a[0], b[0]) + (dot(a[0], b[1]) + dot(a[1], b[0]))


def radial_diff(x):
    n = x.shape[-1]
    lane = lax.broadcasted_iota(jnp.int32, (1, n), 1)
    after = jnp.where(lane == NR - 1, 0.0, 0.5)
    before = jnp.where(lane == 0, 0.0, 0.5)
    return after * pltpu.roll(x, n - 1, x.ndim - 1) - before * pltpu.roll(x, 1, x.ndim - 1)


def row_diff(x, low, high):
    up = jnp.concatenate([x[1:], high], 0)
    down = jnp.concatenate([low, x[:-1]], 0)
    return 0.5 * (up - down)


def radial_rates(n):
    lane = lax.broadcasted_iota(jnp.int32, (1, n), 1).astype(jnp.float32)
    inv_r = 1.0 / (NA / (2.0 * math.pi) + lane)
    return inv_r, 0.5 * (NA / (2.0 * math.pi)) * inv_r


def plane(state, comp, height, width=NR):
    return state[comp, :, height, 0:width]


def lookup(ids, table):
    out = jnp.zeros(ids.shape, jnp.float32)
    for k in range(ZONES):
        out = jnp.where(ids == k, table[k], out)
    return out


def odd_slab():
    return lax.axis_index("core") == 1


def odd_sector():
    return lax.rem(lax.axis_index("z"), 2) == 1


def lowest_slab():
    return lax.axis_index("hx") * 2 + lax.axis_index("core") == 0


def highest_slab():
    return lax.axis_index("hx") * 2 + lax.axis_index("core") == 3


HT_ROWS = 136
AZ_ROWS = 64


def pack_kernel(state, az_then, ht_then, az_first, ht_first, up, down, to_left, to_right):
    inv_r, half_arc = radial_rates(NR)
    zero = jnp.zeros((1, NR), jnp.float32)
    for out, edge, inside, sign in ((up, HTS - 1, HTS - 2, 1.0), (down, 0, 1, -1.0)):
        p, w, u, v = [plane(state, i, edge) for i in (0, 3, 1, 2)]
        p_in, w_in = plane(state, 0, inside), plane(state, 3, inside)
        out[0:32] = p
        out[32:64] = w
        turn = 2.0 * row_diff(v, zero, zero) * half_arc
        out[64:96] = p - DT * (radial_diff(u) + u * inv_r + turn - (0.5 * sign) * w_in)
        out[96:128] = w + (0.5 * DT * sign) * p_in
        out[128:129] = v[0:1]
        out[129:130] = v[ROWS - 1 : ROWS]
        out[130:HT_ROWS] = jnp.zeros((HT_ROWS - 130, NR), jnp.float32)

    for out, j, inside, sign in ((to_right, ROWS - 1, ROWS - 2, 1.0), (to_left, 0, 1, -1.0)):
        p, u, v, w = [state[i, j] for i in range(4)]
        out[0:16] = p
        out[16:32] = v
        rate = radial_diff(u) + u * inv_r + row_diff(w, zero, zero) - sign * half_arc * state[2, inside]
        out[32:48] = p - DT * rate
        out[48:64] = v + (DT * sign) * half_arc * state[0, inside]

    for odd, one, two, ahead, behind in (
        (odd_slab(), ht_first, ht_then, up, down),
        (odd_sector(), az_first, az_then, to_right, to_left),
    ):
        one[...] = jnp.where(odd, behind[...], ahead[...])
        two[...] = jnp.where(odd, ahead[...], behind[...])


def ground_kernel(resistance, relax, state, zone, aux, ground):
    ids, q = zone[...], aux[...]
    p0, w0 = plane(state, 0, 0), plane(state, 3, 0)
    twice = 2.0 * (1.0 / lookup(ids, resistance))
    ground[0] = twice * (p0 - q) - w0
    ground[1] = twice
    ground[2] = q + DT * lookup(ids, relax) * (p0 - q)


def unswap(odd, first, then, behind, ahead):
    behind[...] = jnp.where(odd, first[...], then[...])
    ahead[...] = jnp.where(odd, then[...], first[...])


def two_stages(width, state, low, high, left, right, ground, mid, ghost):
    on_ground, on_top = lowest_slab(), highest_slab()
    inv_r, half_arc = radial_rates(width)
    cols = slice(0, width)
    turn = DT * half_arc

    p0, p1, u0, v0, w0, w1 = [plane(state, i, k, width) for i, k in ((0, 0), (0, 1), (1, 0), (2, 0), (3, 0), (3, 1))]
    p15, w15 = plane(state, 0, HTS - 1, width), plane(state, 3, HTS - 1, width)
    bp = jnp.where(on_ground, p0, low[0:32, cols])
    bw = jnp.where(on_ground, ground[0, :, cols], low[32:64, cols])
    ghost[0], ghost[1], ghost[2], ghost[3] = bp, bw, high[0:32, cols], high[32:64, cols]

    top_p = high[64:96, cols] + (0.5 * DT) * w15
    top_w = high[96:128, cols] + (0.5 * DT) * p15
    low_p = low[64:96, cols] - (0.5 * DT) * w0
    low_w = low[96:128, cols] - (0.5 * DT) * p0
    v_diff = 2.0 * row_diff(v0, left[16:17, cols], right[16:17, cols]) * half_arc
    mid_p0 = p0 - DT * (radial_diff(u0) + u0 * inv_r + v_diff + 0.5 * (w1 - bw))
    mid_w0 = w0 - (0.5 * DT) * (p1 - bp)
    ghost[4] = jnp.where(on_ground, mid_p0, low_p)
    ghost[5] = jnp.where(on_ground, ground[1, :, cols] * (mid_p0 - ground[2, :, cols]) - mid_w0, low_w)
    ghost[6] = jnp.where(on_top, 0.0, top_p)
    ghost[7] = jnp.where(on_top, 0.0, top_w)

    mid[0, 0] = left[32:48, cols] - turn * state[2, 0, :, cols]
    mid[2, 0] = left[48:64, cols] - turn * state[0, 0, :, cols]
    mid[0, ROWS + 1] = right[32:48, cols] + turn * state[2, ROWS - 1, :, cols]
    mid[2, ROWS + 1] = right[48:64, cols] + turn * state[0, ROWS - 1, :, cols]

    def rates(p, u, v_diff, p_diff, w, j, first):
        p_low, w_low, p_high, w_high = [ghost[first + i, pl.ds(j, 1)] for i in range(4)]
        return (
            radial_diff(u) + u * inv_r + v_diff * half_arc + row_diff(w, w_low, w_high),
            radial_diff(p),
            half_arc * p_diff,
            row_diff(p, p_low, p_high),
        )

    def first(j, p_diff, v_diff):
        p, u, v, w = [state[i, j, :, cols] for i in range(4)]
        for i, (s, rate) in enumerate(zip((p, u, v, w), rates(p, u, v_diff, p_diff, w, j, 0))):
            mid[i, j + 1] = s - DT * rate

    first(0, state[0, 1, :, cols] - left[0:16, cols], state[2, 1, :, cols] - left[16:32, cols])
    end = ROWS - 2
    first(ROWS - 1, right[0:16, cols] - state[0, end, :, cols], right[16:32, cols] - state[2, end, :, cols])

    @pl.loop(1, ROWS - 1, unroll=5)
    def _(j):
        first(
            j,
            state[0, j + 1, :, cols] - state[0, j - 1, :, cols],
            state[2, j + 1, :, cols] - state[2, j - 1, :, cols],
        )

    def second(j):
        p, u, v, w = [mid[i, j + 1] for i in range(4)]
        found = rates(p, u, mid[2, j + 2] - mid[2, j], mid[0, j + 2] - mid[0, j], w, j, 4)
        return [0.5 * (state[i, j, :, cols] + m - DT * r) for i, (m, r) in enumerate(zip((p, u, v, w), found))]

    return second


def corner_weight(width):
    return (0.5 * DT) * (0.5 * DT) * radial_rates(width)[1]


def inner_kernel(
    state, az_then, ht_then, az_first, ht_first, ground, packed, low, high, left, right, to_left, to_right, mid, ghost
):
    unswap(odd_slab(), ht_first, ht_then, low, high)
    unswap(odd_sector(), az_first, az_then, left, right)
    near = lax.broadcasted_iota(jnp.int32, (HTS, 128), 1) < NI
    height = lax.broadcasted_iota(jnp.int32, (HTS, 128), 0)
    second = two_stages(128, state, low, high, left, right, ground, mid, ghost)

    def emit(r, one, two):
        for i in range(COMPS):
            both = jnp.where(near, one[i], pltpu.roll(two[i], NI, 1))
            packed[pl.ds(i * HTS * LONG + r, HTS, stride=LONG), :] = both

    @pl.loop(0, HALF - 1, unroll=3)
    def _(l):
        emit(l + 1, second(l), second(l + LONG))

    weight = corner_weight(128)

    def beyond(row):
        at, end = 32 + row * (ROWS - 1), row * (ROWS - 1)
        w_low = jnp.where(lowest_slab(), ground[0, end : end + 1], low[at : at + 1])
        return (w_low, high[at : at + 1]), (low[128 + row : 129 + row], high[128 + row : 129 + row])

    def owed(row, sign):
        out = [jnp.zeros((HTS, 128), jnp.float32)] * 2
        for below, above in beyond(row):
            below, above = [(by * weight) * x[:, 0:128] for by, x in ((-sign, below), (sign, above))]
            out.append(jnp.where(height == HTS - 1, above, jnp.where(height == 0, below, 0.0)))
        return out

    emit(0, owed(0, 1.0), second(HALF))
    emit(HALF, second(HALF - 1), owed(1, -1.0))

    for out, row in ((to_left, 0), (to_right, 1)):
        (w_low, w_high), (v_low, v_high) = beyond(row)
        out[...] = jnp.concatenate([w_low, w_high, v_low, v_high, jnp.zeros((4, NR), jnp.float32)], 0)


def outer_kernel(state, low, high, left, right, ground, stepped, mid, ghost):
    second = two_stages(NR, state, low, high, left, right, ground, mid, ghost)

    @pl.loop(0, ROWS, unroll=2)
    def _(j):
        for i, value in enumerate(second(j)):
            stepped[i, j] = value


def filter_kernel(there, there_small, back, back_small, turn, cutoff, x_ref, o_ref):
    n, m = NA // 4, SECTORS // 2 * LONG
    first, second = x_ref[:m], x_ref[m:]
    h = MODES // 2
    mode = lax.broadcasted_iota(jnp.int32, (h, 128), 0) * 2
    near = lax.broadcasted_iota(jnp.int32, (h, 128), 1) < NI
    limit = jnp.concatenate([cutoff[...], cutoff[...]], 1)
    outs = []
    for parity in range(2):
        folded = first + second if parity == 0 else first - second
        cs, sn, cs_back, sn_back, weight = [turn[parity, :, k : k + 1] for k in range(5)]
        coef = product((there[parity], there_small[parity]), split(folded), ((1,), (0,)))
        a, b = coef[:h], coef[h:]
        a_all = jnp.where(near, a, a * cs - b * sn)
        b_all = jnp.where(near, b, a * sn + b * cs)
        keep = jnp.where(mode + parity < limit, weight, 0.0)
        a_all = (a_all + pltpu.roll(a_all, NI, 1)) * keep
        b_all = (b_all + pltpu.roll(b_all, NI, 1)) * keep
        a_back = jnp.where(near, a_all, a_all * cs_back + b_all * sn_back)
        b_back = jnp.where(near, b_all, b_all * cs_back - a_all * sn_back)
        both = jnp.concatenate([a_back, b_back], 0)
        outs.append(product((back[parity], back_small[parity]), split(both), ((0,), (0,))))
    o_ref[:n] = outs[0] + outs[1]
    o_ref[n:] = outs[0] - outs[1]


def merge_kernel(stepped, back, left_corner, right_corner, out, rows, tile, beside, edges, sems, edge_sems):
    near = lax.broadcasted_iota(jnp.int32, (HTS, 128), 1) < NI
    height = lax.broadcasted_iota(jnp.int32, (HTS, NR), 0)
    loads = [
        pltpu.make_async_copy(stepped.at[i, :, :, pl.ds(0, 128)], beside.at[i], sems.at[0, i]) for i in range(COMPS)
    ]
    places = [(k, i, j) for k, (i, j) in enumerate(((2, 0), (2, ROWS - 1), (3, 0), (3, ROWS - 1)))]
    edge_loads = [
        pltpu.make_async_copy(stepped.at[i, j, :, pl.ds(128, 128)], edges.at[k], edge_sems.at[0, k]) for k, i, j in places
    ]
    for copy in loads + edge_loads:
        copy.start()

    weight = corner_weight(NR)
    owed = {}
    for k, i, j in places:
        corner, sign = (left_corner, -1.0) if j == 0 else (right_corner, 1.0)
        at = 2 * (i - 2)
        below, above = (-sign * weight) * corner[at : at + 1], (sign * weight) * corner[at + 1 : at + 2]
        owed[i, j] = jnp.where(height == HTS - 1, above, jnp.where(height == 0, below, 0.0))

    for i in range(COMPS * HTS):
        rows[pl.ds(i // HTS * HTS * HALF + i % HTS, HALF, stride=HTS), :] = back[i * HALF : (i + 1) * HALF]
    stores = []
    for i in range(COMPS):
        loads[i].wait()
        for j in (0, ROWS - 1):
            if i >= 2:
                beside[i, j] = beside[i, j] + owed[i, j][:, 0:128]
        for l in range(HALF):
            at = (i * HALF + l) * HTS
            both = rows[at : at + HTS]
            tile[i, l] = jnp.where(near, both, beside[i, l])
            tile[i, l + HALF] = jnp.where(near, pltpu.roll(both, NI, 1), beside[i, l + HALF])
        stores.append(pltpu.make_async_copy(tile.at[i], out.at[i, :, :, pl.ds(0, 128)], sems.at[1, i]))
        stores[i].start()
    for k, i, j in places:
        edge_loads[k].wait()
        edges[k] = edges[k] + owed[i, j][:, 128:NR]
        stores.append(pltpu.make_async_copy(edges.at[k], out.at[i, j, :, pl.ds(128, 128)], edge_sems.at[1, k]))
        stores[-1].start()
    for copy in stores:
        copy.wait()


def per_device(state, zone_id, ground_aux, resistance, relax_rate, cutoff):
    f32 = jnp.float32
    vmem = pl.BlockSpec(memory_space=pltpu.VMEM)
    smem = pl.BlockSpec(memory_space=pltpu.SMEM)
    anywhere = pl.BlockSpec(memory_space=pl.ANY)

    def call(kernel, mib=8, **more):
        return pl.pallas_call(kernel, compiler_params=pltpu.CompilerParams(vmem_limit_bytes=mib * 2**20), **more)

    def shapes(*dims):
        return tuple(jax.ShapeDtypeStruct(d, f32) for d in dims)

    ht_message, az_message = (HT_ROWS, NR), (AZ_ROWS, NR)
    az_then, ht_then, az_first, ht_first = call(
        pack_kernel,
        out_shape=shapes(az_message, ht_message, az_message, ht_message),
        in_specs=[vmem],
        out_specs=(vmem,) * 4,
        scratch_shapes=[pltpu.VMEM(m, f32) for m in (ht_message, ht_message, az_message, az_message)],
        name="pack",
    )(state)
    ground = call(
        ground_kernel,
        out_shape=shapes((3, ROWS, NR))[0],
        in_specs=[smem] * 2 + [vmem] * 3,
        out_specs=vmem,
        name="ground",
    )(resistance, relax_rate, state, zone_id, ground_aux)
    def swap(x, axes, size, start, closed):
        pairs = [(i % size, (i + 1) % size) for i in range(start, size if closed else size - 1, 2)]
        return lax.ppermute(x, axes, pairs + [(b, a) for a, b in pairs])

    az_then = swap(az_then, AZ, SECTORS, 1, True)
    ht_then = swap(ht_then, HT, 4, 1, False)
    az_first = swap(az_first, AZ, SECTORS, 0, True)
    ht_first = swap(ht_first, HT, 4, 0, False)

    def scratch(width):
        return [pltpu.VMEM((COMPS, ROWS + 2, HTS, width), f32), pltpu.VMEM((8, ROWS, width), f32)]

    packed, low, high, left, right, to_left, to_right = call(
        inner_kernel,
        mib=12,
        out_shape=shapes(
            (COMPS * HTS * LONG, 128), ht_message, ht_message, az_message, az_message, (8, NR), (8, NR)
        ),
        in_specs=[vmem] * 6,
        out_specs=(vmem,) * 7,
        scratch_shapes=scratch(128),
        cost_estimate=pl.CostEstimate(flops=10**7, bytes_accessed=6 * 10**6, transcendentals=0),
        name="inner",
    )(state, az_then, ht_then, az_first, ht_first, ground)
    circle = lax.all_to_all(packed.reshape(SECTORS, LONG, 1, 128), SPREAD, 0, 0, tiled=True)
    left_corner = lax.ppermute(to_right, AZ, [(i, (i + 1) % SECTORS) for i in range(SECTORS)])
    right_corner = lax.ppermute(to_left, AZ, [((i + 1) % SECTORS, i) for i in range(SECTORS)])
    stepped = call(
        outer_kernel,
        mib=16,
        out_shape=shapes((COMPS, ROWS, HTS, NR))[0],
        in_specs=[vmem] * 6,
        out_specs=vmem,
        scratch_shapes=scratch(NR),
        cost_estimate=pl.CostEstimate(flops=2 * 10**7, bytes_accessed=2 * 10**7, transcendentals=0),
        name="outer",
    )(state, low, high, left, right, ground)
    kept = call(
        filter_kernel, out_shape=shapes((NA // 2, 128))[0], in_specs=[vmem] * 7, out_specs=vmem, name="filter"
    )(*map(jnp.asarray, mode_tables()), cutoff.reshape(1, NI), circle.reshape(SECTORS * LONG, 128))
    back = lax.all_to_all(kept.reshape(SECTORS, HALF, 128), SPREAD, 0, 0, tiled=True)
    return call(
        merge_kernel,
        out_shape=jax.ShapeDtypeStruct(stepped.shape, f32),
        in_specs=[anywhere] + [vmem] * 3,
        out_specs=anywhere,
        scratch_shapes=[
            pltpu.VMEM((COMPS * HTS * HALF, 128), f32),
            pltpu.VMEM((COMPS, ROWS, HTS, 128), f32),
            pltpu.VMEM((COMPS, ROWS, HTS, 128), f32),
            pltpu.VMEM((4, HTS, 128), f32),
            pltpu.SemaphoreType.DMA((2, COMPS)),
            pltpu.SemaphoreType.DMA((2, 4)),
        ],
        input_output_aliases={0: 0},
        name="merge",
    )(stepped, back.reshape(COMPS * HTS * HALF, 128), left_corner, right_corner)


def solution(mesh):
    fine = Mesh(mesh.devices.reshape(4, 2, 8, 2, 2), AZ + HT)
    return jax.shard_map(
        per_device,
        mesh=fine,
        in_specs=(P(None, AZ, HT, None), P(AZ, None), P(AZ, None), P(), P(), P()),
        out_specs=P(None, AZ, HT, None),
        check_vma=False,
    )
```

```python
import functools
import math

import jax
import jax.numpy as jnp
import numpy as np
from jax import lax
from jax.experimental import pallas as pl
from jax.experimental.pallas import tpu as pltpu
from jax.sharding import Mesh, PartitionSpec as P

NA = 2048
NI = 64
MODES = 128
ZONES = 8
SECTORS = 64
ROWS = NA // SECTORS
HALF = ROWS // 2
LONG = HALF + 1
HTS = 16
NR = 256
COMPS = 4
DT = 0.4

AZ = ("y", "x", "z")
SPREAD = ("z", "y")
PEERS = 32
SETS = COMPS * HTS // PEERS
HT = ("hx", "core")


def mode_tables():
    z, y = np.meshgrid(np.arange(8), np.arange(2), indexing="ij")
    first = (y * 16 + z).reshape(-1, 1) * ROWS
    there = (first - 1 + np.arange(LONG)[None, :]).reshape(-1)
    back = (first + np.arange(HALF)[None, :]).reshape(-1)
    tables, turns = [], np.zeros((2, 2, MODES // 2, 128), np.float32)
    for parity in range(2):
        modes = np.arange(parity, MODES, 2)
        waves = []
        for azimuth in (there, back):
            phase = (modes[:, None] * azimuth[None, :] % NA) * (2.0 * math.pi / NA)
            waves.append(np.concatenate([np.cos(phase), np.sin(phase)], 0))
        for x in range(2):
            for k, by in enumerate((0, LONG, 0, HALF)):
                turn = (modes * (by + x * 8 * ROWS) % NA) * (2.0 * math.pi / NA)
                turns[x, parity, :, 2 * k] = np.cos(turn)
                turns[x, parity, :, 2 * k + 1] = np.sin(turn)
            turns[x, parity, :, 8] = np.where(modes == 0, 1.0, 2.0) / NA
        tables.append(waves)
    there, back = [np.stack(t).astype(np.float32) for t in zip(*tables)]
    return split(there), split(back), turns


def split(x):
    x = x.astype(np.float32) if isinstance(x, np.ndarray) else x
    large = x.astype(jnp.bfloat16)
    return large, (x - large.astype(jnp.float32)).astype(jnp.bfloat16)


def product(a, b, dims):
    dot = functools.partial(lax.dot_general, dimension_numbers=(dims, ((), ())), preferred_element_type=jnp.float32)
    return dot(a[0], b[0]) + (dot(a[0], b[1]) + dot(a[1], b[0]))


def radial_diff(x):
    n = x.shape[-1]
    lane = lax.broadcasted_iota(jnp.int32, (1, n), 1)
    after = jnp.where(lane == NR - 1, 0.0, 0.5)
    before = jnp.where(lane == 0, 0.0, 0.5)
    return after * pltpu.roll(x, n - 1, x.ndim - 1) - before * pltpu.roll(x, 1, x.ndim - 1)


def row_diff(x, low, high):
    up = jnp.concatenate([x[1:], high], 0)
    down = jnp.concatenate([low, x[:-1]], 0)
    return 0.5 * (up - down)


def radial_rates(n):
    lane = lax.broadcasted_iota(jnp.int32, (1, n), 1).astype(jnp.float32)
    inv_r = 1.0 / (NA / (2.0 * math.pi) + lane)
    return inv_r, 0.5 * (NA / (2.0 * math.pi)) * inv_r


def plane(state, comp, height, width=NR):
    return state[comp, :, height, 0:width]


def lookup(ids, table):
    out = jnp.zeros(ids.shape, jnp.float32)
    for k in range(ZONES):
        out = jnp.where(ids == k, table[k], out)
    return out


def odd_slab():
    return lax.axis_index("core") == 1


def odd_sector():
    return lax.rem(lax.axis_index("z"), 2) == 1


def lowest_slab():
    return lax.axis_index("hx") * 2 + lax.axis_index("core") == 0


def highest_slab():
    return lax.axis_index("hx") * 2 + lax.axis_index("core") == 3


HT_ROWS = 136
AZ_ROWS = 64
AZ_LONG = 144


def pack_kernel(state, az_then, ht_then, az_first, ht_first, up, down, to_left, to_right):
    inv_r, half_arc = radial_rates(NR)
    zero = jnp.zeros((1, NR), jnp.float32)
    for out, edge, inside, sign in ((up, HTS - 1, HTS - 2, 1.0), (down, 0, 1, -1.0)):
        p, w, u, v = [plane(state, i, edge) for i in (0, 3, 1, 2)]
        p_in, w_in = plane(state, 0, inside), plane(state, 3, inside)
        out[0:32] = p
        out[32:64] = w
        turn = 2.0 * row_diff(v, zero, zero) * half_arc
        out[64:96] = p - DT * (radial_diff(u) + u * inv_r + turn - (0.5 * sign) * w_in)
        out[96:128] = w + (0.5 * DT * sign) * p_in
        out[128:129] = v[0:1]
        out[129:130] = v[ROWS - 1 : ROWS]
        out[130:HT_ROWS] = jnp.zeros((HT_ROWS - 130, NR), jnp.float32)

    for out, j, inside, sign in ((to_right, ROWS - 1, ROWS - 2, 1.0), (to_left, 0, 1, -1.0)):
        p, u, v, w = [state[i, j] for i in range(4)]
        out[0:16] = p
        out[16:32] = v
        rate = radial_diff(u) + u * inv_r + row_diff(w, zero, zero) - sign * half_arc * state[2, inside]
        out[32:48] = p - DT * rate
        out[48:64] = v + (DT * sign) * half_arc * state[0, inside]

    for odd, one, two, ahead, behind in (
        (odd_slab(), ht_first, ht_then, up, down),
        (odd_sector(), az_first, az_then.at[0:AZ_ROWS], to_right, to_left),
    ):
        one[...] = jnp.where(odd, behind[...], ahead[...])
        two[...] = jnp.where(odd, ahead[...], behind[...])
    az_then[AZ_ROWS:AZ_LONG] = jnp.zeros((AZ_LONG - AZ_ROWS, NR), jnp.float32)


def ground_kernel(resistance, relax, state, zone, aux, ground):
    ids, q = zone[...], aux[...]
    p0, w0 = plane(state, 0, 0), plane(state, 3, 0)
    twice = 2.0 * (1.0 / lookup(ids, resistance))
    ground[0] = twice * (p0 - q) - w0
    ground[1] = twice
    ground[2] = q + DT * lookup(ids, relax) * (p0 - q)


def unswap(odd, first, then, behind, ahead):
    behind[...] = jnp.where(odd, first[...], then[...])
    ahead[...] = jnp.where(odd, then[...], first[...])


def two_stages(width, state, low, high, left, right, ground, mid, ghost):
    on_ground, on_top = lowest_slab(), highest_slab()
    inv_r, half_arc = radial_rates(width)
    cols = slice(0, width)
    turn = DT * half_arc

    p0, p1, u0, v0, w0, w1 = [plane(state, i, k, width) for i, k in ((0, 0), (0, 1), (1, 0), (2, 0), (3, 0), (3, 1))]
    p15, w15 = plane(state, 0, HTS - 1, width), plane(state, 3, HTS - 1, width)
    bp = jnp.where(on_ground, p0, low[0:32, cols])
    bw = jnp.where(on_ground, ground[0, :, cols], low[32:64, cols])
    ghost[0], ghost[1], ghost[2], ghost[3] = bp, bw, high[0:32, cols], high[32:64, cols]

    top_p = high[64:96, cols] + (0.5 * DT) * w15
    top_w = high[96:128, cols] + (0.5 * DT) * p15
    low_p = low[64:96, cols] - (0.5 * DT) * w0
    low_w = low[96:128, cols] - (0.5 * DT) * p0
    v_diff = 2.0 * row_diff(v0, left[16:17, cols], right[16:17, cols]) * half_arc
    mid_p0 = p0 - DT * (radial_diff(u0) + u0 * inv_r + v_diff + 0.5 * (w1 - bw))
    mid_w0 = w0 - (0.5 * DT) * (p1 - bp)
    ghost[4] = jnp.where(on_ground, mid_p0, low_p)
    ghost[5] = jnp.where(on_ground, ground[1, :, cols] * (mid_p0 - ground[2, :, cols]) - mid_w0, low_w)
    ghost[6] = jnp.where(on_top, 0.0, top_p)
    ghost[7] = jnp.where(on_top, 0.0, top_w)

    mid[0, 0] = left[32:48, cols] - turn * state[2, 0, :, cols]
    mid[2, 0] = left[48:64, cols] - turn * state[0, 0, :, cols]
    mid[0, ROWS + 1] = right[32:48, cols] + turn * state[2, ROWS - 1, :, cols]
    mid[2, ROWS + 1] = right[48:64, cols] + turn * state[0, ROWS - 1, :, cols]

    def rates(p, u, v_diff, p_diff, w, j, first):
        p_low, w_low, p_high, w_high = [ghost[first + i, pl.ds(j, 1)] for i in range(4)]
        return (
            radial_diff(u) + u * inv_r + v_diff * half_arc + row_diff(w, w_low, w_high),
            radial_diff(p),
            half_arc * p_diff,
            row_diff(p, p_low, p_high),
        )

    def first(j, p_diff, v_diff):
        p, u, v, w = [state[i, j, :, cols] for i in range(4)]
        for i, (s, rate) in enumerate(zip((p, u, v, w), rates(p, u, v_diff, p_diff, w, j, 0))):
            mid[i, j + 1] = s - DT * rate

    first(0, state[0, 1, :, cols] - left[0:16, cols], state[2, 1, :, cols] - left[16:32, cols])
    end = ROWS - 2
    first(ROWS - 1, right[0:16, cols] - state[0, end, :, cols], right[16:32, cols] - state[2, end, :, cols])

    @pl.loop(1, ROWS - 1, unroll=5)
    def _(j):
        first(
            j,
            state[0, j + 1, :, cols] - state[0, j - 1, :, cols],
            state[2, j + 1, :, cols] - state[2, j - 1, :, cols],
        )

    def second(j):
        p, u, v, w = [mid[i, j + 1] for i in range(4)]
        found = rates(p, u, mid[2, j + 2] - mid[2, j], mid[0, j + 2] - mid[0, j], w, j, 4)
        return [0.5 * (state[i, j, :, cols] + m - DT * r) for i, (m, r) in enumerate(zip((p, u, v, w), found))]

    return second


def corner_weight(width):
    return (0.5 * DT) * (0.5 * DT) * radial_rates(width)[1]


def inner_kernel(
    state, az_then, ht_then, az_first, ht_first, ground, packed, low, high, left, right, to_left, to_right, mid, ghost
):
    unswap(odd_slab(), ht_first, ht_then, low, high)
    unswap(odd_sector(), az_first, az_then.at[0:AZ_ROWS], left, right)
    near = lax.broadcasted_iota(jnp.int32, (HTS, 128), 1) < NI
    height = lax.broadcasted_iota(jnp.int32, (HTS, 128), 0)
    second = two_stages(128, state, low, high, left, right, ground, mid, ghost)

    def emit(r, one, two):
        for i in range(COMPS):
            both = jnp.where(near, one[i], pltpu.roll(two[i], NI, 1))
            packed[pl.ds(i * HTS * LONG + r, HTS, stride=LONG), :] = both

    @pl.loop(0, HALF - 1, unroll=3)
    def _(l):
        emit(l + 1, second(l), second(l + LONG))

    weight = corner_weight(128)

    def beyond(row):
        at, end = 32 + row * (ROWS - 1), row * (ROWS - 1)
        w_low = jnp.where(lowest_slab(), ground[0, end : end + 1], low[at : at + 1])
        return (w_low, high[at : at + 1]), (low[128 + row : 129 + row], high[128 + row : 129 + row])

    def owed(row, sign):
        out = [jnp.zeros((HTS, 128), jnp.float32)] * 2
        for below, above in beyond(row):
            below, above = [(by * weight) * x[:, 0:128] for by, x in ((-sign, below), (sign, above))]
            out.append(jnp.where(height == HTS - 1, above, jnp.where(height == 0, below, 0.0)))
        return out

    emit(0, owed(0, 1.0), second(HALF))
    emit(HALF, second(HALF - 1), owed(1, -1.0))

    for out, row in ((to_left, 0), (to_right, 1)):
        (w_low, w_high), (v_low, v_high) = beyond(row)
        out[...] = jnp.concatenate([w_low, w_high, v_low, v_high, jnp.zeros((4, NR), jnp.float32)], 0)


def outer_kernel(state, low, high, left, right, ground, stepped, mid, ghost):
    second = two_stages(NR, state, low, high, left, right, ground, mid, ghost)

    @pl.loop(0, ROWS, unroll=2)
    def _(j):
        for i, value in enumerate(second(j)):
            stepped[i, j] = value


def turns_of(turn, x, parity, way):
    near = lax.broadcasted_iota(jnp.int32, (MODES // 2, 128), 1) < NI
    return [
        jnp.where(near, turn[x, parity, :, k : k + 1], turn[x, parity, :, k + 2 : k + 3])
        for k in (4 * way, 4 * way + 1)
    ]


def analysis_kernel(wave, wave_small, turn, circle, sums, folded):
    for z in range(8):
        for y in range(2):
            for q in range(SETS):
                one, two = [circle[pl.ds(((4 * z + k) * SETS + q) * LONG, LONG), :] for k in (y, y + 2)]
                at = pl.ds((2 * z + y) * LONG, LONG)
                folded[0, q, at, :] = one + two
                folded[1, q, at, :] = one - two
    x = lax.axis_index("x")
    h = MODES // 2
    near = lax.broadcasted_iota(jnp.int32, (h, 128), 1) < NI
    for parity in range(2):
        cs, sn = turns_of(turn, x, parity, 0)
        found = []
        for q in range(SETS):
            coef = product((wave[parity], wave_small[parity]), split(folded[parity, q]), ((1,), (0,)))
            a, b = coef[:h], coef[h:]
            found.append([t + pltpu.roll(t, NI, 1) for t in (a * cs - b * sn, a * sn + b * cs)])
        for k in range(2):
            at = (2 * parity + k) * h
            sums[at : at + h] = jnp.where(near, found[0][k], found[1][k])


def synthesis_kernel(wave, wave_small, turn, cutoff, mine, other, out):
    x = lax.axis_index("x")
    h = MODES // 2
    mode = lax.broadcasted_iota(jnp.int32, (h, 128), 0) * 2
    near = lax.broadcasted_iota(jnp.int32, (h, 128), 1) < NI
    limit = jnp.concatenate([cutoff[...], cutoff[...]], 1)
    parts = []
    for parity in range(2):
        cs, sn = turns_of(turn, x, parity, 1)
        keep = jnp.where(mode + parity < limit, turn[x, parity, :, 8:9], 0.0)
        a, b = [
            (mine[at : at + h] + other[at : at + h]) * keep for at in (2 * parity * h, (2 * parity + 1) * h)
        ]
        a_far, b_far = pltpu.roll(a, NI, 1), pltpu.roll(b, NI, 1)
        for q in range(SETS):
            a_all, b_all = [jnp.where(near == (q == 0), t, far) for t, far in ((a, a_far), (b, b_far))]
            both = jnp.concatenate([a_all * cs + b_all * sn, b_all * cs - a_all * sn], 0)
            parts.append(product((wave[parity], wave_small[parity]), split(both), ((0,), (0,))))
    for q in range(SETS):
        even, odd = parts[q], parts[SETS + q]
        for z in range(8):
            for y in range(2):
                at = slice((2 * z + y) * HALF, (2 * z + y + 1) * HALF)
                for k, value in ((y, even[at] + odd[at]), (y + 2, even[at] - odd[at])):
                    to = ((4 * z + k) * SETS + q) * HALF
                    out[to : to + HALF] = value


def merge_kernel(stepped, back, left_corner, right_corner, out, rows, tile, beside, edges, sems, edge_sems):
    near = lax.broadcasted_iota(jnp.int32, (HTS, 128), 1) < NI
    height = lax.broadcasted_iota(jnp.int32, (HTS, NR), 0)
    loads = [
        pltpu.make_async_copy(stepped.at[i, :, :, pl.ds(0, 128)], beside.at[i], sems.at[0, i]) for i in range(COMPS)
    ]
    places = [(k, i, j) for k, (i, j) in enumerate(((2, 0), (2, ROWS - 1), (3, 0), (3, ROWS - 1)))]
    edge_loads = [
        pltpu.make_async_copy(stepped.at[i, j, :, pl.ds(128, 128)], edges.at[k], edge_sems.at[0, k]) for k, i, j in places
    ]
    for copy in loads + edge_loads:
        copy.start()

    weight = corner_weight(NR)
    owed = {}
    for k, i, j in places:
        corner, sign = (left_corner, -1.0) if j == 0 else (right_corner, 1.0)
        at = 2 * (i - 2)
        below, above = (-sign * weight) * corner[at : at + 1], (sign * weight) * corner[at + 1 : at + 2]
        owed[i, j] = jnp.where(height == HTS - 1, above, jnp.where(height == 0, below, 0.0))

    for i in range(COMPS * HTS):
        rows[pl.ds(i // HTS * HTS * HALF + i % HTS, HALF, stride=HTS), :] = back[i * HALF : (i + 1) * HALF]
    stores = []
    for i in range(COMPS):
        loads[i].wait()
        for j in (0, ROWS - 1):
            if i >= 2:
                beside[i, j] = beside[i, j] + owed[i, j][:, 0:128]
        for l in range(HALF):
            at = (i * HALF + l) * HTS
            both = rows[at : at + HTS]
            tile[i, l] = jnp.where(near, both, beside[i, l])
            tile[i, l + HALF] = jnp.where(near, pltpu.roll(both, NI, 1), beside[i, l + HALF])
        stores.append(pltpu.make_async_copy(tile.at[i], out.at[i, :, :, pl.ds(0, 128)], sems.at[1, i]))
        stores[i].start()
    for k, i, j in places:
        edge_loads[k].wait()
        edges[k] = edges[k] + owed[i, j][:, 128:NR]
        stores.append(pltpu.make_async_copy(edges.at[k], out.at[i, j, :, pl.ds(128, 128)], edge_sems.at[1, k]))
        stores[-1].start()
    for copy in stores:
        copy.wait()


def per_device(state, zone_id, ground_aux, resistance, relax_rate, cutoff):
    f32 = jnp.float32
    vmem = pl.BlockSpec(memory_space=pltpu.VMEM)
    smem = pl.BlockSpec(memory_space=pltpu.SMEM)
    anywhere = pl.BlockSpec(memory_space=pl.ANY)

    def call(kernel, mib=8, **more):
        return pl.pallas_call(kernel, compiler_params=pltpu.CompilerParams(vmem_limit_bytes=mib * 2**20), **more)

    def shapes(*dims):
        return tuple(jax.ShapeDtypeStruct(d, f32) for d in dims)

    ht_message, az_message = (HT_ROWS, NR), (AZ_ROWS, NR)
    az_then, ht_then, az_first, ht_first = call(
        pack_kernel,
        out_shape=shapes((AZ_LONG, NR), ht_message, az_message, ht_message),
        in_specs=[vmem],
        out_specs=(vmem,) * 4,
        scratch_shapes=[pltpu.VMEM(m, f32) for m in (ht_message, ht_message, az_message, az_message)],
        name="pack",
    )(state)
    ground = call(
        ground_kernel,
        out_shape=shapes((3, ROWS, NR))[0],
        in_specs=[smem] * 2 + [vmem] * 3,
        out_specs=vmem,
        name="ground",
    )(resistance, relax_rate, state, zone_id, ground_aux)
    def swap(x, axes, size, start, closed):
        pairs = [(i % size, (i + 1) % size) for i in range(start, size if closed else size - 1, 2)]
        return lax.ppermute(x, axes, pairs + [(b, a) for a, b in pairs])

    az_then = swap(az_then, AZ, SECTORS, 1, True)
    ht_then = swap(ht_then, HT, 4, 1, False)
    az_first = swap(az_first, AZ, SECTORS, 0, True)
    ht_first = swap(ht_first, HT, 4, 0, False)

    def scratch(width):
        return [pltpu.VMEM((COMPS, ROWS + 2, HTS, width), f32), pltpu.VMEM((8, ROWS, width), f32)]

    packed, low, high, left, right, to_left, to_right = call(
        inner_kernel,
        mib=12,
        out_shape=shapes(
            (COMPS * HTS * LONG, 128), ht_message, ht_message, az_message, az_message, (8, NR), (8, NR)
        ),
        in_specs=[vmem] * 6,
        out_specs=(vmem,) * 7,
        scratch_shapes=scratch(128),
        cost_estimate=pl.CostEstimate(flops=10**7, bytes_accessed=6 * 10**6, transcendentals=0),
        name="inner",
    )(state, az_then, ht_then, az_first, ht_first, ground)
    circle = lax.all_to_all(packed.reshape(PEERS, SETS * LONG, 1, 128), SPREAD, 0, 0, tiled=True)
    left_corner = lax.ppermute(to_right, AZ, [(i, (i + 1) % SECTORS) for i in range(SECTORS)])
    right_corner = lax.ppermute(to_left, AZ, [((i + 1) % SECTORS, i) for i in range(SECTORS)])
    stepped = call(
        outer_kernel,
        mib=16,
        out_shape=shapes((COMPS, ROWS, HTS, NR))[0],
        in_specs=[vmem] * 6,
        out_specs=vmem,
        scratch_shapes=scratch(NR),
        cost_estimate=pl.CostEstimate(flops=2 * 10**7, bytes_accessed=2 * 10**7, transcendentals=0),
        name="outer",
    )(state, low, high, left, right, ground)
    there, back, turns = jax.tree.map(jnp.asarray, mode_tables())
    sums = call(
        analysis_kernel,
        out_shape=shapes((2 * MODES, 128))[0],
        in_specs=[vmem] * 4,
        out_specs=vmem,
        scratch_shapes=[pltpu.VMEM((2, SETS, PEERS // 2 * LONG, 128), f32)],
        name="analysis",
    )(*there, turns, circle.reshape(PEERS * SETS * LONG, 128))
    other = lax.ppermute(sums, "x", [(0, 1), (1, 0)])
    kept = call(
        synthesis_kernel,
        out_shape=shapes((PEERS * SETS * HALF, 128))[0],
        in_specs=[vmem] * 6,
        out_specs=vmem,
        name="synthesis",
    )(*back, turns, cutoff.reshape(1, NI), sums, other)
    back = lax.all_to_all(kept.reshape(PEERS, SETS * HALF, 128), SPREAD, 0, 0, tiled=True)
    return call(
        merge_kernel,
        out_shape=jax.ShapeDtypeStruct(stepped.shape, f32),
        in_specs=[anywhere] + [vmem] * 3,
        out_specs=anywhere,
        scratch_shapes=[
            pltpu.VMEM((COMPS * HTS * HALF, 128), f32),
            pltpu.VMEM((COMPS, ROWS, HTS, 128), f32),
            pltpu.VMEM((COMPS, ROWS, HTS, 128), f32),
            pltpu.VMEM((4, HTS, 128), f32),
            pltpu.SemaphoreType.DMA((2, COMPS)),
            pltpu.SemaphoreType.DMA((2, 4)),
        ],
        input_output_aliases={0: 0},
        name="merge",
    )(stepped, back.reshape(COMPS * HTS * HALF, 128), left_corner, right_corner)


def solution(mesh):
    fine = Mesh(mesh.devices.reshape(4, 2, 8, 2, 2), AZ + HT)
    return jax.shard_map(
        per_device,
        mesh=fine,
        in_specs=(P(None, AZ, HT, None), P(AZ, None), P(AZ, None), P(), P(), P()),
        out_specs=P(None, AZ, HT, None),
        check_vma=False,
    )
```

```python
import functools
import math

import jax
import jax.numpy as jnp
import numpy as np
from jax import lax
from jax.experimental import pallas as pl
from jax.experimental.pallas import tpu as pltpu
from jax.sharding import Mesh, PartitionSpec as P

NA = 2048
NI = 64
MODES = 128
ZONES = 8
SECTORS = 64
ROWS = NA // SECTORS
HALF = ROWS // 2
LONG = HALF + 2
TURN_AT = SECTORS // 2 * LONG
HTS = 16
NR = 256
COMPS = 4
DT = 0.4

AZ = ("y", "x", "z")
SPREAD = ("y", "z", "x")
HT = ("hx", "core")


def sector_of_chunk():
    y, z, x = np.meshgrid(np.arange(4), np.arange(8), np.arange(2), indexing="ij")
    return ((y * 2 + x) * 8 + z).reshape(-1)


def mode_tables():
    first = sector_of_chunk()[: SECTORS // 2, None] * ROWS
    azimuth = (first - 2 + np.arange(LONG)[None, :]).reshape(-1)
    out = np.zeros((2, 2, MODES, TURN_AT + 64), jnp.bfloat16)
    for parity in range(2):
        modes = np.arange(parity, MODES, 2)
        phase = (modes[:, None] * azimuth[None, :] % NA) * (2.0 * math.pi / NA)
        out[0, parity, :, :TURN_AT], out[1, parity, :, :TURN_AT] = split(np.concatenate([np.cos(phase), np.sin(phase)], 0))
        turn = (modes * LONG % NA) * (2.0 * math.pi / NA)
        for k, value in enumerate((np.cos(turn), np.sin(turn))):
            rest = value.astype(np.float32)
            for part in range(3):
                large = rest.astype(jnp.bfloat16)
                out[0, parity, : MODES // 2, TURN_AT + 3 * k + part] = large
                rest = rest - large.astype(np.float32)
        out[0, parity, : MODES // 2, TURN_AT + 6] = np.where(modes == 0, 1.0, 2.0) / NA
    return out


def split(x):
    x = x.astype(np.float32) if isinstance(x, np.ndarray) else x
    large = x.astype(jnp.bfloat16)
    return large, (x - large.astype(jnp.float32)).astype(jnp.bfloat16)


def product(a, b, dims):
    dot = functools.partial(lax.dot_general, dimension_numbers=(dims, ((), ())), preferred_element_type=jnp.float32)
    return dot(a[0], b[0]) + (dot(a[0], b[1]) + dot(a[1], b[0]))


def radial_diff(x):
    n = x.shape[-1]
    lane = lax.broadcasted_iota(jnp.int32, (1, n), 1)
    after = jnp.where(lane == NR - 1, 0.0, 0.5)
    before = jnp.where(lane == 0, 0.0, 0.5)
    return after * pltpu.roll(x, n - 1, x.ndim - 1) - before * pltpu.roll(x, 1, x.ndim - 1)


def row_diff(x, low, high):
    up = jnp.concatenate([x[1:], high], 0)
    down = jnp.concatenate([low, x[:-1]], 0)
    return 0.5 * (up - down)


def radial_rates(n):
    lane = lax.broadcasted_iota(jnp.int32, (1, n), 1).astype(jnp.float32)
    inv_r = 1.0 / (NA / (2.0 * math.pi) + lane)
    return inv_r, 0.5 * (NA / (2.0 * math.pi)) * inv_r


def plane(state, comp, height, width=NR):
    return state[comp, :, height, 0:width]


def lookup(ids, table):
    out = jnp.zeros(ids.shape, jnp.float32)
    for k in range(ZONES):
        out = jnp.where(ids == k, table[k], out)
    return out


def odd_slab():
    return lax.axis_index("core") == 1


def odd_sector():
    return lax.rem(lax.axis_index("z"), 2) == 1


def lowest_slab():
    return lax.axis_index("hx") * 2 + lax.axis_index("core") == 0


def highest_slab():
    return lax.axis_index("hx") * 2 + lax.axis_index("core") == 3


HT_ROWS = 136
AZ_ROWS = 72
AZ_AHEAD = 288


def pack_kernel(state, to_right, ht_then, ht_first, up, down):
    inv_r, half_arc = radial_rates(NR)
    zero = jnp.zeros((1, NR), jnp.float32)
    for out, edge, inside, sign in ((up, HTS - 1, HTS - 2, 1.0), (down, 0, 1, -1.0)):
        p, w, u, v = [plane(state, i, edge) for i in (0, 3, 1, 2)]
        p_in, w_in = plane(state, 0, inside), plane(state, 3, inside)
        out[0:32] = p
        out[32:64] = w
        turn = 2.0 * row_diff(v, zero, zero) * half_arc
        out[64:96] = p - DT * (radial_diff(u) + u * inv_r + turn - (0.5 * sign) * w_in)
        out[96:128] = w + (0.5 * DT * sign) * p_in
        out[128:129] = v[0:1]
        out[129:130] = v[ROWS - 1 : ROWS]
        out[130:HT_ROWS] = jnp.zeros((HT_ROWS - 130, NR), jnp.float32)
    odd = odd_slab()
    ht_first[...] = jnp.where(odd, down[...], up[...])
    ht_then[...] = jnp.where(odd, up[...], down[...])

    no_row = jnp.zeros((1, 128), jnp.float32)
    edge_message(to_right, state, ROWS - 1, ROWS - 2, 1.0, no_row, no_row)
    to_right[64:AZ_AHEAD] = jnp.zeros((AZ_AHEAD - 64, 128), jnp.float32)


def edge_message(out, state, j, inside, sign, w_low, w_high):
    width = w_low.shape[1]
    inv_r, half_arc = radial_rates(width)
    p, u, v, w = [state[i, j, :, 0:width] for i in range(4)]
    v_in, p_in = state[2, inside, :, 0:width], state[0, inside, :, 0:width]
    out[0:16] = p
    out[16:32] = v
    out[32:48] = p - DT * (radial_diff(u) + u * inv_r + row_diff(w, w_low, w_high) - sign * half_arc * v_in)
    out[48:64] = v + (DT * sign) * half_arc * p_in


def ground_kernel(resistance, relax, state, zone, aux, ground):
    ids, q = zone[...], aux[...]
    p0, w0 = plane(state, 0, 0), plane(state, 3, 0)
    twice = 2.0 * (1.0 / lookup(ids, resistance))
    ground[0] = twice * (p0 - q) - w0
    ground[1] = twice
    ground[2] = q + DT * lookup(ids, relax) * (p0 - q)


def unswap(odd, first, then, behind, ahead):
    behind[...] = jnp.where(odd, first[...], then[...])
    ahead[...] = jnp.where(odd, then[...], first[...])


def two_stages(width, state, low, high, left, right, ground, mid, ghost):
    on_ground, on_top = lowest_slab(), highest_slab()
    inv_r, half_arc = radial_rates(width)
    cols = slice(0, width)
    turn = DT * half_arc

    def beyond(a, b):
        return jnp.zeros((b - a, width), jnp.float32) if right is None else right[a:b, cols]

    def corners(k):
        if right is None:
            return 0.0
        sub = lax.broadcasted_iota(jnp.int32, (ROWS, width), 0)
        last = jnp.where(sub == ROWS - 1, -right[k : k + 1, cols], 0.0)
        return turn * jnp.where(sub == 0, left[k : k + 1, cols], last)

    p0, p1, u0, v0, w0, w1 = [plane(state, i, k, width) for i, k in ((0, 0), (0, 1), (1, 0), (2, 0), (3, 0), (3, 1))]
    p15, w15 = plane(state, 0, HTS - 1, width), plane(state, 3, HTS - 1, width)
    bp = jnp.where(on_ground, p0, low[0:32, cols])
    bw = jnp.where(on_ground, ground[0, :, cols], low[32:64, cols])
    ghost[0], ghost[1], ghost[2], ghost[3] = bp, bw, high[0:32, cols], high[32:64, cols]

    top_p = high[64:96, cols] + (0.5 * DT) * w15 + corners(65)
    top_w = high[96:128, cols] + (0.5 * DT) * p15
    low_p = low[64:96, cols] - (0.5 * DT) * w0 + corners(64)
    low_w = low[96:128, cols] - (0.5 * DT) * p0
    v_diff = 2.0 * row_diff(v0, left[16:17, cols], beyond(16, 17)) * half_arc
    mid_p0 = p0 - DT * (radial_diff(u0) + u0 * inv_r + v_diff + 0.5 * (w1 - bw))
    mid_w0 = w0 - (0.5 * DT) * (p1 - bp)
    ghost[4] = jnp.where(on_ground, mid_p0, low_p)
    ghost[5] = jnp.where(on_ground, ground[1, :, cols] * (mid_p0 - ground[2, :, cols]) - mid_w0, low_w)
    ghost[6] = jnp.where(on_top, 0.0, top_p)
    ghost[7] = jnp.where(on_top, 0.0, top_w)

    mid[0, 0] = left[32:48, cols] - turn * state[2, 0, :, cols]
    mid[2, 0] = left[48:64, cols] - turn * state[0, 0, :, cols]
    mid[0, ROWS + 1] = beyond(32, 48) + turn * state[2, ROWS - 1, :, cols]
    mid[2, ROWS + 1] = beyond(48, 64) + turn * state[0, ROWS - 1, :, cols]

    def rates(p, u, v_diff, p_diff, w, j, first):
        p_low, w_low, p_high, w_high = [ghost[first + i, pl.ds(j, 1)] for i in range(4)]
        return (
            radial_diff(u) + u * inv_r + v_diff * half_arc + row_diff(w, w_low, w_high),
            radial_diff(p),
            half_arc * p_diff,
            row_diff(p, p_low, p_high),
        )

    def first(j, p_diff, v_diff):
        p, u, v, w = [state[i, j, :, cols] for i in range(4)]
        for i, (s, rate) in enumerate(zip((p, u, v, w), rates(p, u, v_diff, p_diff, w, j, 0))):
            mid[i, j + 1] = s - DT * rate

    first(0, state[0, 1, :, cols] - left[0:16, cols], state[2, 1, :, cols] - left[16:32, cols])
    end = ROWS - 2
    first(ROWS - 1, beyond(0, 16) - state[0, end, :, cols], beyond(16, 32) - state[2, end, :, cols])

    @pl.loop(1, ROWS - 1, unroll=5)
    def _(j):
        first(
            j,
            state[0, j + 1, :, cols] - state[0, j - 1, :, cols],
            state[2, j + 1, :, cols] - state[2, j - 1, :, cols],
        )

    def second(j):
        p, u, v, w = [mid[i, j + 1] for i in range(4)]
        found = rates(p, u, mid[2, j + 2] - mid[2, j], mid[0, j + 2] - mid[0, j], w, j, 4)
        return [0.5 * (state[i, j, :, cols] + m - DT * r) for i, (m, r) in enumerate(zip((p, u, v, w), found))]

    return second


def corner_weight(width):
    return (0.5 * DT) * (0.5 * DT) * radial_rates(width)[1]


def inner_kernel(state, left, ht_then, ht_first, ground, packed, low, high, mid, ghost):
    unswap(odd_slab(), ht_first, ht_then, low, high)
    near = lax.broadcasted_iota(jnp.int32, (HTS, 128), 1) < NI
    height = lax.broadcasted_iota(jnp.int32, (HTS, 128), 0)
    second = two_stages(128, state, low, high, left, None, ground, mid, ghost)
    on_ground = lowest_slab()

    def emit(r, one, two):
        for i in range(COMPS):
            both = jnp.where(near, one[i], pltpu.roll(two[i], NI, 1))
            packed[pl.ds(i * HTS * LONG + r, HTS, stride=LONG), :] = both

    @pl.loop(0, HALF - 2, unroll=2)
    def _(l):
        emit(l + 2, second(l), second(l + LONG))

    turn = DT * radial_rates(128)[1]
    none = jnp.zeros((HTS, 128), jnp.float32)

    p0, v0 = state[0, 0, :, 0:128], state[2, 0, :, 0:128]
    own_p, own_v = mid[0, 1] - turn * left[16:32], mid[2, 1] - turn * left[0:16]
    far_p = -turn * v0
    far_low = jnp.where(on_ground, far_p[0:1], -turn * low[128:129, 0:128])
    far_high = -turn * high[128:129, 0:128]
    last = [
        0.5 * (far_p - turn * own_v),
        (-0.5 * DT) * radial_diff(far_p),
        (-0.5 * turn) * (p0 + own_p),
        (-0.5 * DT) * row_diff(far_p, far_low, far_high),
    ]
    before = [0.5 * turn * turn * p0, none, 0.5 * turn * turn * v0, none]

    weight = 0.5 * DT * turn * 0.5

    end = ROWS - 1
    at_ground = jnp.logical_and(on_ground, height == 0)
    owed = [jnp.where(at_ground, ground[1, end : end + 1, 0:128], 0.0), none]
    factor = jnp.where(at_ground, (-0.25 * DT) * turn * v0, 0.0)
    for below, above in ((w_below(low, ground, end), high[32 + end : 33 + end]), (low[129:130], high[129:130])):
        below, above = weight * below[:, 0:128], -weight * above[:, 0:128]
        owed.append(jnp.where(height == HTS - 1, above, jnp.where(height == 0, below, 0.0)))

    emit(0, before, second(HALF))
    emit(1, last, second(HALF + 1))
    emit(HALF, second(HALF - 2), owed)
    emit(HALF + 1, second(HALF - 1), [factor] + [none] * 3)


def w_below(low, ground, j):
    return jnp.where(lowest_slab(), ground[0, j : j + 1], low[32 + j : 33 + j])


def edge_kernel(state, ht_then, ht_first, ground, after, to_left, to_right, low, high):
    unswap(odd_slab(), ht_first, ht_then, low, high)
    end = ROWS - 1
    for out, j, inside, sign, corner in ((to_right, end, end - 1, 1.0, 129), (to_left, 0, 1, -1.0, 128)):
        edge_message(out, state, j, inside, sign, w_below(low, ground, j), high[32 + j : 33 + j])
        out[64:65] = low[corner : corner + 1]
        out[65:66] = high[corner : corner + 1]
        out[66:AZ_ROWS] = jnp.zeros((AZ_ROWS - 66, NR), jnp.float32)


def outer_kernel(state, ht_then, ht_first, left, right, ground, stepped, low, high, mid, ghost):
    unswap(odd_slab(), ht_first, ht_then, low, high)
    second = two_stages(NR, state, low, high, left, right, ground, mid, ghost)

    @pl.loop(0, ROWS, unroll=2)
    def _(j):
        for i, value in enumerate(second(j)):
            stepped[i, j] = value


def ground_terms(circle):
    near = lax.broadcasted_iota(jnp.int32, (1, 128), 1) < NI
    sectors = sector_of_chunk().tolist()

    def row(chunk, r):
        return pl.ds(chunk * LONG + r, 1)

    for k, sector in enumerate(sectors):
        last = sectors.index((sector - 1) % SECTORS)
        term = circle[row(last, HALF), :] * circle[row(k, HALF + 1), :]
        circle[row(k, 1), :] = circle[row(k, 1), :] + jnp.where(near, pltpu.roll(term, NI, 1), 0.0)
    for k in range(SECTORS):
        for r in (HALF, HALF + 1):
            circle[row(k, r), :] = jnp.where(near, circle[row(k, r), :], 0.0)


def filter_kernel(table, cutoff, x_ref, left, right, o_ref, circle):
    m = SECTORS // 2 * LONG
    circle[...] = x_ref[...]

    @pl.when(lax.axis_index("y") * 16 + lax.axis_index("z") * 2 + lax.axis_index("x") == 0)
    def _():
        ground_terms(circle)

    first, second = circle[:m], circle[m:]
    h = MODES // 2
    mode = lax.broadcasted_iota(jnp.int32, (h, 128), 0) * 2
    near = lax.broadcasted_iota(jnp.int32, (h, 128), 1) < NI
    limit = jnp.concatenate([cutoff[...], cutoff[...]], 1)
    outs = []
    for parity in range(2):
        folded = first + second if parity == 0 else first - second
        waves = table[0, parity, :, :TURN_AT], table[1, parity, :, :TURN_AT]
        parts = table[0, parity, :h, TURN_AT : TURN_AT + 64].astype(jnp.float32)
        cs, sn = [parts[:, k : k + 1] + parts[:, k + 1 : k + 2] + parts[:, k + 2 : k + 3] for k in (0, 3)]
        weight = parts[:, 6:7]
        coef = product(waves, split(folded), ((1,), (0,)))
        a, b = coef[:h], coef[h:]
        a_all = jnp.where(near, a, a * cs - b * sn)
        b_all = jnp.where(near, b, a * sn + b * cs)
        keep = jnp.where(mode + parity < limit, weight, 0.0)
        a_all = (a_all + pltpu.roll(a_all, NI, 1)) * keep
        b_all = (b_all + pltpu.roll(b_all, NI, 1)) * keep
        a_back = jnp.where(near, a_all, a_all * cs + b_all * sn)
        b_back = jnp.where(near, b_all, b_all * cs - a_all * sn)
        both = jnp.concatenate([a_back, b_back], 0)
        outs.append(product(waves, split(both), ((0,), (0,))))
    for half in range(2):
        circle[half * m : (half + 1) * m] = outs[0] + outs[1] if half == 0 else outs[0] - outs[1]
    row_near = lax.broadcasted_iota(jnp.int32, (HALF, 128), 1) < NI
    for k in range(SECTORS):
        at = k * LONG
        o_ref[k * HALF : (k + 1) * HALF] = jnp.where(
            row_near, circle[at + 2 : at + 2 + HALF], circle[at : at + HALF]
        )


def merge_kernel(stepped, back, out, rows, tile, beside, sems):
    near = lax.broadcasted_iota(jnp.int32, (HTS, 128), 1) < NI
    loads = [
        pltpu.make_async_copy(stepped.at[i, :, :, pl.ds(0, 128)], beside.at[i], sems.at[0, i]) for i in range(COMPS)
    ]
    for copy in loads:
        copy.start()
    for i in range(COMPS * HTS):
        rows[pl.ds(i // HTS * HTS * HALF + i % HTS, HALF, stride=HTS), :] = back[i * HALF : (i + 1) * HALF]
    stores = []
    for i in range(COMPS):
        loads[i].wait()
        for l in range(HALF):
            at = (i * HALF + l) * HTS
            both = rows[at : at + HTS]
            tile[i, l] = jnp.where(near, both, beside[i, l])
            tile[i, l + HALF] = jnp.where(near, pltpu.roll(both, NI, 1), beside[i, l + HALF])
        stores.append(pltpu.make_async_copy(tile.at[i], out.at[i, :, :, pl.ds(0, 128)], sems.at[1, i]))
        stores[i].start()
    for copy in stores:
        copy.wait()


def per_device(state, zone_id, ground_aux, resistance, relax_rate, cutoff):
    f32 = jnp.float32
    vmem = pl.BlockSpec(memory_space=pltpu.VMEM)
    smem = pl.BlockSpec(memory_space=pltpu.SMEM)
    anywhere = pl.BlockSpec(memory_space=pl.ANY)

    def call(kernel, mib=8, **more):
        return pl.pallas_call(kernel, compiler_params=pltpu.CompilerParams(vmem_limit_bytes=mib * 2**20), **more)

    def shapes(*dims):
        return tuple(jax.ShapeDtypeStruct(d, f32) for d in dims)

    ht_message, az_message = (HT_ROWS, NR), (AZ_ROWS, NR)
    to_right, ht_then, ht_first = call(
        pack_kernel,
        out_shape=shapes((AZ_AHEAD, 128), ht_message, ht_message),
        in_specs=[vmem],
        out_specs=(vmem,) * 3,
        scratch_shapes=[pltpu.VMEM(ht_message, f32)] * 2,
        name="pack",
    )(state)
    ground = call(
        ground_kernel,
        out_shape=shapes((3, ROWS, NR))[0],
        in_specs=[smem] * 2 + [vmem] * 3,
        out_specs=vmem,
        name="ground",
    )(resistance, relax_rate, state, zone_id, ground_aux)
    def swap(x, start):
        pairs = [(i, i + 1) for i in range(start, 3, 2)]
        return lax.ppermute(x, HT, pairs + [(b, a) for a, b in pairs])

    rightward = [(i, (i + 1) % SECTORS) for i in range(SECTORS)]
    leftward = [(b, a) for a, b in rightward]
    ahead = lax.ppermute(to_right, AZ, rightward)
    ht_then, ht_first = swap(ht_then, 1), swap(ht_first, 0)

    def scratch(width):
        return [pltpu.VMEM((COMPS, ROWS + 2, HTS, width), f32), pltpu.VMEM((8, ROWS, width), f32)]

    halos = [pltpu.VMEM(ht_message, f32)] * 2
    packed = call(
        inner_kernel,
        mib=12,
        out_shape=shapes((COMPS * HTS * LONG, 128))[0],
        in_specs=[vmem] * 5,
        out_specs=vmem,
        scratch_shapes=halos + scratch(128),
        cost_estimate=pl.CostEstimate(flops=10**7, bytes_accessed=6 * 10**6, transcendentals=0),
        name="inner",
    )(state, ahead, ht_then, ht_first, ground)
    to_left, to_right = call(
        edge_kernel,
        out_shape=shapes(az_message, az_message),
        in_specs=[vmem] * 4 + [anywhere],
        out_specs=(vmem,) * 2,
        scratch_shapes=halos,
        name="edge",
    )(state, ht_then, ht_first, ground, packed)
    circle = lax.all_to_all(packed.reshape(SECTORS, LONG, 1, 128), SPREAD, 0, 0, tiled=True)
    left = lax.ppermute(to_right, AZ, rightward)
    right = lax.ppermute(to_left, AZ, leftward)
    stepped = call(
        outer_kernel,
        mib=16,
        out_shape=shapes((COMPS, ROWS, HTS, NR))[0],
        in_specs=[vmem] * 6,
        out_specs=vmem,
        scratch_shapes=halos + scratch(NR),
        cost_estimate=pl.CostEstimate(flops=2 * 10**7, bytes_accessed=2 * 10**7, transcendentals=0),
        name="outer",
    )(state, ht_then, ht_first, left, right, ground)
    kept = call(
        filter_kernel,
        out_shape=shapes((NA // 2, 128))[0],
        in_specs=[vmem] * 3 + [anywhere] * 2,
        out_specs=vmem,
        scratch_shapes=[pltpu.VMEM((SECTORS * LONG, 128), f32)],
        name="filter",
    )(jnp.asarray(mode_tables()), cutoff.reshape(1, NI), circle.reshape(SECTORS * LONG, 128), left, right)
    back = lax.all_to_all(kept.reshape(SECTORS, HALF, 128), SPREAD, 0, 0, tiled=True)
    return call(
        merge_kernel,
        out_shape=jax.ShapeDtypeStruct(stepped.shape, f32),
        in_specs=[anywhere, vmem],
        out_specs=anywhere,
        scratch_shapes=[
            pltpu.VMEM((COMPS * HTS * HALF, 128), f32),
            pltpu.VMEM((COMPS, ROWS, HTS, 128), f32),
            pltpu.VMEM((COMPS, ROWS, HTS, 128), f32),
            pltpu.SemaphoreType.DMA((2, COMPS)),
        ],
        input_output_aliases={0: 0},
        name="merge",
    )(stepped, back.reshape(COMPS * HTS * HALF, 128))


def solution(mesh):
    fine = Mesh(mesh.devices.reshape(4, 2, 8, 2, 2), AZ + HT)
    return jax.shard_map(
        per_device,
        mesh=fine,
        in_specs=(P(None, AZ, HT, None), P(AZ, None), P(AZ, None), P(), P(), P()),
        out_specs=P(None, AZ, HT, None),
        check_vma=False,
    )
```

```python
import functools
import math

import jax
import jax.numpy as jnp
import numpy as np
from jax import lax
from jax.experimental import pallas as pl
from jax.experimental.pallas import tpu as pltpu
from jax.sharding import Mesh, PartitionSpec as P

NA = 2048
NI = 64
MODES = 128
ZONES = 8
SECTORS = 64
ROWS = NA // SECTORS
HALF = ROWS // 2
LONG = HALF + 2
TURN_AT = SECTORS // 2 * LONG
HTS = 16
NR = 256
COMPS = 4
DT = 0.4

AZ = ("y", "x", "z")
SPREAD = ("y", "z", "x")
HT = ("hx", "core")


def sector_of_chunk():
    y, z, x = np.meshgrid(np.arange(4), np.arange(8), np.arange(2), indexing="ij")
    return ((y * 2 + x) * 8 + z).reshape(-1)


def mode_tables():
    first = sector_of_chunk()[: SECTORS // 2, None] * ROWS
    azimuth = (first - 2 + np.arange(LONG)[None, :]).reshape(-1)
    out = np.zeros((2, 2, MODES, TURN_AT + 64), jnp.bfloat16)
    for parity in range(2):
        modes = np.arange(parity, MODES, 2)
        phase = (modes[:, None] * azimuth[None, :] % NA) * (2.0 * math.pi / NA)
        out[0, parity, :, :TURN_AT], out[1, parity, :, :TURN_AT] = split(np.concatenate([np.cos(phase), np.sin(phase)], 0))
        turn = (modes * LONG % NA) * (2.0 * math.pi / NA)
        for k, value in enumerate((np.cos(turn), np.sin(turn))):
            rest = value.astype(np.float32)
            for part in range(3):
                large = rest.astype(jnp.bfloat16)
                out[0, parity, : MODES // 2, TURN_AT + 3 * k + part] = large
                rest = rest - large.astype(np.float32)
        out[0, parity, : MODES // 2, TURN_AT + 6] = np.where(modes == 0, 1.0, 2.0) / NA
    return out


def split(x):
    x = x.astype(np.float32) if isinstance(x, np.ndarray) else x
    large = x.astype(jnp.bfloat16)
    return large, (x - large.astype(jnp.float32)).astype(jnp.bfloat16)


def product(a, b, dims):
    dot = functools.partial(lax.dot_general, dimension_numbers=(dims, ((), ())), preferred_element_type=jnp.float32)
    return dot(a[0], b[0]) + (dot(a[0], b[1]) + dot(a[1], b[0]))


def radial_diff(x):
    n = x.shape[-1]
    lane = lax.broadcasted_iota(jnp.int32, (1, n), 1)
    after = jnp.where(lane == NR - 1, 0.0, 0.5)
    before = jnp.where(lane == 0, 0.0, 0.5)
    return after * pltpu.roll(x, n - 1, x.ndim - 1) - before * pltpu.roll(x, 1, x.ndim - 1)


def row_diff(x, low, high):
    up = jnp.concatenate([x[1:], high], 0)
    down = jnp.concatenate([low, x[:-1]], 0)
    return 0.5 * (up - down)


def radial_rates(n):
    lane = lax.broadcasted_iota(jnp.int32, (1, n), 1).astype(jnp.float32)
    inv_r = 1.0 / (NA / (2.0 * math.pi) + lane)
    return inv_r, 0.5 * (NA / (2.0 * math.pi)) * inv_r


def plane(state, comp, height, width=NR):
    return state[comp, :, height, 0:width]


def lookup(ids, table):
    out = jnp.zeros(ids.shape, jnp.float32)
    for k in range(ZONES):
        out = jnp.where(ids == k, table[k], out)
    return out


def odd_slab():
    return lax.axis_index("core") == 1


def odd_sector():
    return lax.rem(lax.axis_index("z"), 2) == 1


def lowest_slab():
    return lax.axis_index("hx") * 2 + lax.axis_index("core") == 0


def highest_slab():
    return lax.axis_index("hx") * 2 + lax.axis_index("core") == 3


HT_ROWS = 136
AZ_ROWS = 64


def pack_kernel(state, to_right, to_left, ht_then, ht_first, up, down):
    inv_r, half_arc = radial_rates(NR)
    zero = jnp.zeros((1, NR), jnp.float32)
    for out, edge, inside, sign in ((up, HTS - 1, HTS - 2, 1.0), (down, 0, 1, -1.0)):
        p, w, u, v = [plane(state, i, edge) for i in (0, 3, 1, 2)]
        p_in, w_in = plane(state, 0, inside), plane(state, 3, inside)
        out[0:32] = p
        out[32:64] = w
        turn = 2.0 * row_diff(v, zero, zero) * half_arc
        out[64:96] = p - DT * (radial_diff(u) + u * inv_r + turn - (0.5 * sign) * w_in)
        out[96:128] = w + (0.5 * DT * sign) * p_in
        out[128:129] = v[0:1]
        out[129:130] = v[ROWS - 1 : ROWS]
        out[130:HT_ROWS] = jnp.zeros((HT_ROWS - 130, NR), jnp.float32)
    odd = odd_slab()
    ht_first[...] = jnp.where(odd, down[...], up[...])
    ht_then[...] = jnp.where(odd, up[...], down[...])

    edge_message(to_right, state, ROWS - 1, ROWS - 2, 1.0, zero, zero)
    edge_message(to_left, state, 0, 1, -1.0, zero, zero)


def edge_message(out, state, j, inside, sign, w_low, w_high):
    width = w_low.shape[1]
    inv_r, half_arc = radial_rates(width)
    p, u, v, w = [state[i, j, :, 0:width] for i in range(4)]
    v_in, p_in = state[2, inside, :, 0:width], state[0, inside, :, 0:width]
    out[0:16] = p
    out[16:32] = v
    out[32:48] = p - DT * (radial_diff(u) + u * inv_r + row_diff(w, w_low, w_high) - sign * half_arc * v_in)
    out[48:64] = v + (DT * sign) * half_arc * p_in


def ground_kernel(resistance, relax, state, zone, aux, ground):
    ids, q = zone[...], aux[...]
    p0, w0 = plane(state, 0, 0), plane(state, 3, 0)
    twice = 2.0 * (1.0 / lookup(ids, resistance))
    ground[0] = twice * (p0 - q) - w0
    ground[1] = twice
    ground[2] = q + DT * lookup(ids, relax) * (p0 - q)


def unswap(odd, first, then, behind, ahead):
    behind[...] = jnp.where(odd, first[...], then[...])
    ahead[...] = jnp.where(odd, then[...], first[...])


def two_stages(width, state, low, high, left, ground, mid, ghost):
    on_ground, on_top = lowest_slab(), highest_slab()
    inv_r, half_arc = radial_rates(width)
    cols = slice(0, width)
    turn = DT * half_arc

    def beyond(a, b):
        return jnp.zeros((b - a, width), jnp.float32)

    p0, p1, u0, v0, w0, w1 = [plane(state, i, k, width) for i, k in ((0, 0), (0, 1), (1, 0), (2, 0), (3, 0), (3, 1))]
    p15, w15 = plane(state, 0, HTS - 1, width), plane(state, 3, HTS - 1, width)
    bp = jnp.where(on_ground, p0, low[0:32, cols])
    bw = jnp.where(on_ground, ground[0, :, cols], low[32:64, cols])
    ghost[0], ghost[1], ghost[2], ghost[3] = bp, bw, high[0:32, cols], high[32:64, cols]

    top_p = high[64:96, cols] + (0.5 * DT) * w15
    top_w = high[96:128, cols] + (0.5 * DT) * p15
    low_p = low[64:96, cols] - (0.5 * DT) * w0
    low_w = low[96:128, cols] - (0.5 * DT) * p0
    v_diff = 2.0 * row_diff(v0, left[16:17, cols], beyond(16, 17)) * half_arc
    mid_p0 = p0 - DT * (radial_diff(u0) + u0 * inv_r + v_diff + 0.5 * (w1 - bw))
    mid_w0 = w0 - (0.5 * DT) * (p1 - bp)
    ghost[4] = jnp.where(on_ground, mid_p0, low_p)
    ghost[5] = jnp.where(on_ground, ground[1, :, cols] * (mid_p0 - ground[2, :, cols]) - mid_w0, low_w)
    ghost[6] = jnp.where(on_top, 0.0, top_p)
    ghost[7] = jnp.where(on_top, 0.0, top_w)

    mid[0, 0] = left[32:48, cols] - turn * state[2, 0, :, cols]
    mid[2, 0] = left[48:64, cols] - turn * state[0, 0, :, cols]
    mid[0, ROWS + 1] = beyond(32, 48) + turn * state[2, ROWS - 1, :, cols]
    mid[2, ROWS + 1] = beyond(48, 64) + turn * state[0, ROWS - 1, :, cols]

    def rates(p, u, v_diff, p_diff, w, j, first):
        p_low, w_low, p_high, w_high = [ghost[first + i, pl.ds(j, 1)] for i in range(4)]
        return (
            radial_diff(u) + u * inv_r + v_diff * half_arc + row_diff(w, w_low, w_high),
            radial_diff(p),
            half_arc * p_diff,
            row_diff(p, p_low, p_high),
        )

    def first(j, p_diff, v_diff):
        p, u, v, w = [state[i, j, :, cols] for i in range(4)]
        for i, (s, rate) in enumerate(zip((p, u, v, w), rates(p, u, v_diff, p_diff, w, j, 0))):
            mid[i, j + 1] = s - DT * rate

    first(0, state[0, 1, :, cols] - left[0:16, cols], state[2, 1, :, cols] - left[16:32, cols])
    end = ROWS - 2
    first(ROWS - 1, beyond(0, 16) - state[0, end, :, cols], beyond(16, 32) - state[2, end, :, cols])

    @pl.loop(1, ROWS - 1, unroll=5)
    def _(j):
        first(
            j,
            state[0, j + 1, :, cols] - state[0, j - 1, :, cols],
            state[2, j + 1, :, cols] - state[2, j - 1, :, cols],
        )

    def second(j):
        p, u, v, w = [mid[i, j + 1] for i in range(4)]
        found = rates(p, u, mid[2, j + 2] - mid[2, j], mid[0, j + 2] - mid[0, j], w, j, 4)
        return [0.5 * (state[i, j, :, cols] + m - DT * r) for i, (m, r) in enumerate(zip((p, u, v, w), found))]

    return second


def corner_weight(width):
    return (0.5 * DT) * (0.5 * DT) * radial_rates(width)[1]


def corner_weight(width):
    return (0.5 * DT) * (0.5 * DT) * radial_rates(width)[1]


def inner_kernel(
    state, left, ht_then, ht_first, ground, packed, left_corner, right_corner, low, high, mid, ghost
):
    unswap(odd_slab(), ht_first, ht_then, low, high)
    near = lax.broadcasted_iota(jnp.int32, (HTS, 128), 1) < NI
    height = lax.broadcasted_iota(jnp.int32, (HTS, 128), 0)
    second = two_stages(128, state, low, high, left, ground, mid, ghost)
    on_ground = lowest_slab()

    def emit(r, one, two):
        for i in range(COMPS):
            both = jnp.where(near, one[i], pltpu.roll(two[i], NI, 1))
            packed[pl.ds(i * HTS * LONG + r, HTS, stride=LONG), :] = both

    @pl.loop(0, HALF - 2, unroll=2)
    def _(l):
        emit(l + 2, second(l), second(l + LONG))

    turn = DT * radial_rates(128)[1]
    none = jnp.zeros((HTS, 128), jnp.float32)

    p0, v0 = state[0, 0, :, 0:128], state[2, 0, :, 0:128]
    own_p, own_v = mid[0, 1] - turn * left[16:32, 0:128], mid[2, 1] - turn * left[0:16, 0:128]
    far_p = -turn * v0
    far_low = jnp.where(on_ground, far_p[0:1], -turn * low[128:129, 0:128])
    far_high = -turn * high[128:129, 0:128]
    last = [
        0.5 * (far_p - turn * own_v),
        (-0.5 * DT) * radial_diff(far_p),
        (-0.5 * turn) * (p0 + own_p),
        (-0.5 * DT) * row_diff(far_p, far_low, far_high),
    ]
    before = [0.5 * turn * turn * p0, none, 0.5 * turn * turn * v0, none]

    weight = corner_weight(128)

    end = ROWS - 1
    at_ground = jnp.logical_and(on_ground, height == 0)
    owed = [jnp.where(at_ground, ground[1, end : end + 1, 0:128], 0.0), none]
    factor = jnp.where(at_ground, (-0.25 * DT) * turn * v0, 0.0)
    for below, above in ((w_below(low, ground, end), high[32 + end : 33 + end]), (low[129:130], high[129:130])):
        below, above = weight * below[:, 0:128], -weight * above[:, 0:128]
        owed.append(jnp.where(height == HTS - 1, above, jnp.where(height == 0, below, 0.0)))

    emit(0, before, second(HALF))
    emit(1, last, second(HALF + 1))
    emit(HALF, second(HALF - 2), owed)
    emit(HALF + 1, second(HALF - 1), [factor] + [none] * 3)

    for out, j, corner in ((left_corner, 0, 128), (right_corner, end, 129)):
        rows = [w_below(low, ground, j), high[32 + j : 33 + j], low[corner : corner + 1], high[corner : corner + 1]]
        out[...] = jnp.concatenate(rows + [jnp.zeros((4, NR), jnp.float32)], 0)


def w_below(low, ground, j):
    return jnp.where(lowest_slab(), ground[0, j : j + 1], low[32 + j : 33 + j])


def outer_kernel(state, ht_then, ht_first, left, ground, stepped, low, high, mid, ghost):
    unswap(odd_slab(), ht_first, ht_then, low, high)
    second = two_stages(NR, state, low, high, left, ground, mid, ghost)

    @pl.loop(0, ROWS, unroll=2)
    def _(j):
        for i, value in enumerate(second(j)):
            stepped[i, j] = value


def ground_terms(circle):
    near = lax.broadcasted_iota(jnp.int32, (1, 128), 1) < NI
    sectors = sector_of_chunk().tolist()

    def row(chunk, r):
        return pl.ds(chunk * LONG + r, 1)

    for k, sector in enumerate(sectors):
        last = sectors.index((sector - 1) % SECTORS)
        term = circle[row(last, HALF), :] * circle[row(k, HALF + 1), :]
        circle[row(k, 1), :] = circle[row(k, 1), :] + jnp.where(near, pltpu.roll(term, NI, 1), 0.0)
    for k in range(SECTORS):
        for r in (HALF, HALF + 1):
            circle[row(k, r), :] = jnp.where(near, circle[row(k, r), :], 0.0)


def filter_kernel(table, cutoff, x_ref, o_ref, circle):
    m = SECTORS // 2 * LONG
    circle[...] = x_ref[...]

    @pl.when(lax.axis_index("y") * 16 + lax.axis_index("z") * 2 + lax.axis_index("x") == 0)
    def _():
        ground_terms(circle)

    first, second = circle[:m], circle[m:]
    h = MODES // 2
    mode = lax.broadcasted_iota(jnp.int32, (h, 128), 0) * 2
    near = lax.broadcasted_iota(jnp.int32, (h, 128), 1) < NI
    limit = jnp.concatenate([cutoff[...], cutoff[...]], 1)
    outs = []
    for parity in range(2):
        folded = first + second if parity == 0 else first - second
        waves = table[0, parity, :, :TURN_AT], table[1, parity, :, :TURN_AT]
        parts = table[0, parity, :h, TURN_AT : TURN_AT + 64].astype(jnp.float32)
        cs, sn = [parts[:, k : k + 1] + parts[:, k + 1 : k + 2] + parts[:, k + 2 : k + 3] for k in (0, 3)]
        weight = parts[:, 6:7]
        coef = product(waves, split(folded), ((1,), (0,)))
        a, b = coef[:h], coef[h:]
        a_all = jnp.where(near, a, a * cs - b * sn)
        b_all = jnp.where(near, b, a * sn + b * cs)
        keep = jnp.where(mode + parity < limit, weight, 0.0)
        a_all = (a_all + pltpu.roll(a_all, NI, 1)) * keep
        b_all = (b_all + pltpu.roll(b_all, NI, 1)) * keep
        a_back = jnp.where(near, a_all, a_all * cs + b_all * sn)
        b_back = jnp.where(near, b_all, b_all * cs - a_all * sn)
        both = jnp.concatenate([a_back, b_back], 0)
        outs.append(product(waves, split(both), ((0,), (0,))))
    for half in range(2):
        circle[half * m : (half + 1) * m] = outs[0] + outs[1] if half == 0 else outs[0] - outs[1]
    row_near = lax.broadcasted_iota(jnp.int32, (HALF, 128), 1) < NI
    for k in range(SECTORS):
        at = k * LONG
        o_ref[k * HALF : (k + 1) * HALF] = jnp.where(
            row_near, circle[at + 2 : at + 2 + HALF], circle[at : at + HALF]
        )


def edge_terms(right, left_corner, right_corner, ground):
    height = lax.broadcasted_iota(jnp.int32, (HTS, NR), 0)
    half_arc = radial_rates(NR)[1]
    turn, weight = DT * half_arc, corner_weight(NR)
    on_ground = lowest_slab()
    end = ROWS - 1
    p, v, mid_p, mid_v = [right[16 * i : 16 * i + 16] for i in range(4)]
    far_p = -turn * v
    wall = (0.25 * DT) * ground[1, end : end + 1] * far_p
    far_low = jnp.where(on_ground, far_p[0:1], 0.0)
    terms = {
        (0, end): 0.5 * (far_p - turn * mid_v) + jnp.where(jnp.logical_and(on_ground, height == 0), wall, 0.0),
        (1, end): (-0.5 * DT) * radial_diff(far_p),
        (2, end): (-0.5 * turn) * (p + mid_p),
        (3, end): (-0.5 * DT) * row_diff(far_p, far_low, jnp.zeros((1, NR), jnp.float32)),
        (0, end - 1): 0.5 * turn * turn * p,
        (2, end - 1): 0.5 * turn * turn * v,
        (2, 0): 0.0,
        (3, 0): 0.0,
    }
    for i, j in ((2, 0), (2, end), (3, 0), (3, end)):
        corner, sign = (left_corner, -1.0) if j == 0 else (right_corner, 1.0)
        at = 2 * (i - 2)
        below, above = (-sign * weight) * corner[at : at + 1], (sign * weight) * corner[at + 1 : at + 2]
        corner_term = jnp.where(height == HTS - 1, above, jnp.where(height == 0, below, 0.0))
        terms[i, j] = terms[i, j] + corner_term
    return terms


EDGE_PLACES = 8


def merge_kernel(
    stepped, back, right, left_corner, right_corner, ground, out, rows, tile, beside, edges, sems, edge_sems
):
    near = lax.broadcasted_iota(jnp.int32, (HTS, 128), 1) < NI
    loads = [
        pltpu.make_async_copy(stepped.at[i, :, :, pl.ds(0, 128)], beside.at[i], sems.at[0, i]) for i in range(COMPS)
    ]
    for copy in loads:
        copy.start()
    owed = edge_terms(right, left_corner, right_corner, ground)
    places = [(k, i, j) for k, (i, j) in enumerate(owed)]
    edge_loads = [
        pltpu.make_async_copy(stepped.at[i, j, :, pl.ds(128, 128)], edges.at[k], edge_sems.at[0, k]) for k, i, j in places
    ]
    for copy in edge_loads:
        copy.start()

    for i in range(COMPS * HTS):
        rows[pl.ds(i // HTS * HTS * HALF + i % HTS, HALF, stride=HTS), :] = back[i * HALF : (i + 1) * HALF]
    stores = []
    for i in range(COMPS):
        loads[i].wait()
        for k, comp, j in places:
            if comp == i:
                beside[i, j] = beside[i, j] + owed[i, j][:, 0:128]
        for l in range(HALF):
            at = (i * HALF + l) * HTS
            both = rows[at : at + HTS]
            tile[i, l] = jnp.where(near, both, beside[i, l])
            tile[i, l + HALF] = jnp.where(near, pltpu.roll(both, NI, 1), beside[i, l + HALF])
        stores.append(pltpu.make_async_copy(tile.at[i], out.at[i, :, :, pl.ds(0, 128)], sems.at[1, i]))
        stores[i].start()
    for k, i, j in places:
        edge_loads[k].wait()
        edges[k] = edges[k] + owed[i, j][:, 128:NR]
        stores.append(pltpu.make_async_copy(edges.at[k], out.at[i, j, :, pl.ds(128, 128)], edge_sems.at[1, k]))
        stores[-1].start()
    for copy in stores:
        copy.wait()


def per_device(state, zone_id, ground_aux, resistance, relax_rate, cutoff):
    f32 = jnp.float32
    vmem = pl.BlockSpec(memory_space=pltpu.VMEM)
    smem = pl.BlockSpec(memory_space=pltpu.SMEM)
    anywhere = pl.BlockSpec(memory_space=pl.ANY)

    def call(kernel, mib=8, **more):
        return pl.pallas_call(kernel, compiler_params=pltpu.CompilerParams(vmem_limit_bytes=mib * 2**20), **more)

    def shapes(*dims):
        return tuple(jax.ShapeDtypeStruct(d, f32) for d in dims)

    ht_message, az_message = (HT_ROWS, NR), (AZ_ROWS, NR)
    to_right, to_left, ht_then, ht_first = call(
        pack_kernel,
        out_shape=shapes(az_message, az_message, ht_message, ht_message),
        in_specs=[vmem],
        out_specs=(vmem,) * 4,
        scratch_shapes=[pltpu.VMEM(ht_message, f32)] * 2,
        name="pack",
    )(state)
    ground = call(
        ground_kernel,
        out_shape=shapes((3, ROWS, NR))[0],
        in_specs=[smem] * 2 + [vmem] * 3,
        out_specs=vmem,
        name="ground",
    )(resistance, relax_rate, state, zone_id, ground_aux)
    def swap(x, start):
        pairs = [(i, i + 1) for i in range(start, 3, 2)]
        return lax.ppermute(x, HT, pairs + [(b, a) for a, b in pairs])

    rightward = [(i, (i + 1) % SECTORS) for i in range(SECTORS)]
    leftward = [(b, a) for a, b in rightward]
    left, right = lax.ppermute(to_right, AZ, rightward), lax.ppermute(to_left, AZ, leftward)
    ht_then, ht_first = swap(ht_then, 1), swap(ht_first, 0)

    def scratch(width):
        return [pltpu.VMEM((COMPS, ROWS + 2, HTS, width), f32), pltpu.VMEM((8, ROWS, width), f32)]

    halos = [pltpu.VMEM(ht_message, f32)] * 2
    packed, to_left, to_right = call(
        inner_kernel,
        mib=12,
        out_shape=shapes((COMPS * HTS * LONG, 128), (8, NR), (8, NR)),
        in_specs=[vmem] * 5,
        out_specs=(vmem,) * 3,
        scratch_shapes=halos + scratch(128),
        cost_estimate=pl.CostEstimate(flops=10**7, bytes_accessed=6 * 10**6, transcendentals=0),
        name="inner",
    )(state, left, ht_then, ht_first, ground)
    circle = lax.all_to_all(packed.reshape(SECTORS, LONG, 1, 128), SPREAD, 0, 0, tiled=True)
    left_corner, right_corner = lax.ppermute(to_right, AZ, rightward), lax.ppermute(to_left, AZ, leftward)
    stepped = call(
        outer_kernel,
        mib=16,
        out_shape=shapes((COMPS, ROWS, HTS, NR))[0],
        in_specs=[vmem] * 5,
        out_specs=vmem,
        scratch_shapes=halos + scratch(NR),
        cost_estimate=pl.CostEstimate(flops=2 * 10**7, bytes_accessed=2 * 10**7, transcendentals=0),
        name="outer",
    )(state, ht_then, ht_first, left, ground)
    kept = call(
        filter_kernel,
        out_shape=shapes((NA // 2, 128))[0],
        in_specs=[vmem] * 3,
        out_specs=vmem,
        scratch_shapes=[pltpu.VMEM((SECTORS * LONG, 128), f32)],
        name="filter",
    )(jnp.asarray(mode_tables()), cutoff.reshape(1, NI), circle.reshape(SECTORS * LONG, 128))
    back = lax.all_to_all(kept.reshape(SECTORS, HALF, 128), SPREAD, 0, 0, tiled=True)
    return call(
        merge_kernel,
        out_shape=jax.ShapeDtypeStruct(stepped.shape, f32),
        in_specs=[anywhere] + [vmem] * 5,
        out_specs=anywhere,
        scratch_shapes=[
            pltpu.VMEM((COMPS * HTS * HALF, 128), f32),
            pltpu.VMEM((COMPS, ROWS, HTS, 128), f32),
            pltpu.VMEM((COMPS, ROWS, HTS, 128), f32),
            pltpu.VMEM((EDGE_PLACES, HTS, 128), f32),
            pltpu.SemaphoreType.DMA((2, COMPS)),
            pltpu.SemaphoreType.DMA((2, EDGE_PLACES)),
        ],
        input_output_aliases={0: 0},
        name="merge",
    )(stepped, back.reshape(COMPS * HTS * HALF, 128), right, left_corner, right_corner, ground)


def solution(mesh):
    fine = Mesh(mesh.devices.reshape(4, 2, 8, 2, 2), AZ + HT)
    return jax.shard_map(
        per_device,
        mesh=fine,
        in_specs=(P(None, AZ, HT, None), P(AZ, None), P(AZ, None), P(), P(), P()),
        out_specs=P(None, AZ, HT, None),
        check_vma=False,
    )
```

```python
import functools
import math

import jax
import jax.numpy as jnp
import numpy as np
from jax import lax
from jax.experimental import pallas as pl
from jax.experimental.pallas import tpu as pltpu
from jax.sharding import Mesh, PartitionSpec as P

NA = 2048
NI = 64
MODES = 128
ZONES = 8
SECTORS = 64
ROWS = NA // SECTORS
HALF = ROWS // 2
LONG = HALF + 2
HTS = 16
NR = 256
COMPS = 4
DT = 0.4

AZ = ("y", "x", "z")
SPREAD = ("z", "y")
PEERS = 32
SETS = COMPS * HTS // PEERS
HT = ("hx", "core")


def mode_tables():
    z, y = np.meshgrid(np.arange(8), np.arange(2), indexing="ij")
    first = (y * 16 + z).reshape(-1, 1) * ROWS
    there = (first - 2 + np.arange(LONG)[None, :]).reshape(-1)
    back = (first + np.arange(HALF)[None, :]).reshape(-1)
    tables, turns = [], np.zeros((2, 2, MODES // 2, 128), np.float32)
    for parity in range(2):
        modes = np.arange(parity, MODES, 2)
        waves = []
        for azimuth in (there, back):
            phase = (modes[:, None] * azimuth[None, :] % NA) * (2.0 * math.pi / NA)
            waves.append(np.concatenate([np.cos(phase), np.sin(phase)], 0))
        for x in range(2):
            for k, by in enumerate((0, LONG, 0, HALF)):
                turn = (modes * (by + x * 8 * ROWS) % NA) * (2.0 * math.pi / NA)
                turns[x, parity, :, 2 * k] = np.cos(turn)
                turns[x, parity, :, 2 * k + 1] = np.sin(turn)
            turns[x, parity, :, 8] = np.where(modes == 0, 1.0, 2.0) / NA
        tables.append(waves)
    there, back = [np.stack(t).astype(np.float32) for t in zip(*tables)]
    return split(there), split(back), turns


def split(x):
    x = x.astype(np.float32) if isinstance(x, np.ndarray) else x
    large = x.astype(jnp.bfloat16)
    return large, (x - large.astype(jnp.float32)).astype(jnp.bfloat16)


def product(a, b, dims):
    dot = functools.partial(lax.dot_general, dimension_numbers=(dims, ((), ())), preferred_element_type=jnp.float32)
    return dot(a[0], b[0]) + (dot(a[0], b[1]) + dot(a[1], b[0]))


def radial_diff(x):
    n = x.shape[-1]
    lane = lax.broadcasted_iota(jnp.int32, (1, n), 1)
    after = jnp.where(lane == NR - 1, 0.0, 0.5)
    before = jnp.where(lane == 0, 0.0, 0.5)
    return after * pltpu.roll(x, n - 1, x.ndim - 1) - before * pltpu.roll(x, 1, x.ndim - 1)


def row_diff(x, low, high):
    up = jnp.concatenate([x[1:], high], 0)
    down = jnp.concatenate([low, x[:-1]], 0)
    return 0.5 * (up - down)


def radial_rates(n):
    lane = lax.broadcasted_iota(jnp.int32, (1, n), 1).astype(jnp.float32)
    inv_r = 1.0 / (NA / (2.0 * math.pi) + lane)
    return inv_r, 0.5 * (NA / (2.0 * math.pi)) * inv_r


def plane(state, comp, height, width=NR):
    return state[comp, :, height, 0:width]


def lookup(ids, table):
    out = jnp.zeros(ids.shape, jnp.float32)
    for k in range(ZONES):
        out = jnp.where(ids == k, table[k], out)
    return out


def odd_slab():
    return lax.axis_index("core") == 1


def odd_sector():
    return lax.rem(lax.axis_index("z"), 2) == 1


def lowest_slab():
    return lax.axis_index("hx") * 2 + lax.axis_index("core") == 0


def highest_slab():
    return lax.axis_index("hx") * 2 + lax.axis_index("core") == 3


HT_ROWS = 136
AZ_ROWS = 72


def pack_kernel(state, ht_then, ht_first, up, down):
    inv_r, half_arc = radial_rates(NR)
    zero = jnp.zeros((1, NR), jnp.float32)
    for out, edge, inside, sign in ((up, HTS - 1, HTS - 2, 1.0), (down, 0, 1, -1.0)):
        p, w, u, v = [plane(state, i, edge) for i in (0, 3, 1, 2)]
        p_in, w_in = plane(state, 0, inside), plane(state, 3, inside)
        out[0:32] = p
        out[32:64] = w
        turn = 2.0 * row_diff(v, zero, zero) * half_arc
        out[64:96] = p - DT * (radial_diff(u) + u * inv_r + turn - (0.5 * sign) * w_in)
        out[96:128] = w + (0.5 * DT * sign) * p_in
        out[128:129] = v[0:1]
        out[129:130] = v[ROWS - 1 : ROWS]
        out[130:HT_ROWS] = jnp.zeros((HT_ROWS - 130, NR), jnp.float32)
    odd = odd_slab()
    ht_first[...] = jnp.where(odd, down[...], up[...])
    ht_then[...] = jnp.where(odd, up[...], down[...])


def pack_az_kernel(state, zone, resistance, after, to_right, to_left):
    zero = jnp.zeros((1, NR), jnp.float32)
    edge_message(to_right, state, ROWS - 1, ROWS - 2, 1.0, zero, zero)
    edge_message(to_left, state, 0, 1, -1.0, zero, zero)
    ids, found = zone[ROWS - 1 : ROWS], zero
    for k in range(ZONES):
        found = jnp.where(ids == k, 2.0 * (1.0 / resistance[0:1, k : k + 1]), found)
    to_right[64:65] = found
    to_right[65:AZ_ROWS] = jnp.zeros((AZ_ROWS - 65, NR), jnp.float32)
    to_left[64:AZ_ROWS] = jnp.zeros((AZ_ROWS - 64, NR), jnp.float32)


def edge_message(out, state, j, inside, sign, w_low, w_high):
    width = w_low.shape[1]
    inv_r, half_arc = radial_rates(width)
    p, u, v, w = [state[i, j, :, 0:width] for i in range(4)]
    v_in, p_in = state[2, inside, :, 0:width], state[0, inside, :, 0:width]
    out[0:16] = p
    out[16:32] = v
    out[32:48] = p - DT * (radial_diff(u) + u * inv_r + row_diff(w, w_low, w_high) - sign * half_arc * v_in)
    out[48:64] = v + (DT * sign) * half_arc * p_in


def ground_kernel(resistance, relax, state, zone, aux, ground):
    ids, q = zone[...], aux[...]
    p0, w0 = plane(state, 0, 0), plane(state, 3, 0)
    twice = 2.0 * (1.0 / lookup(ids, resistance))
    ground[0] = twice * (p0 - q) - w0
    ground[1] = twice
    ground[2] = q + DT * lookup(ids, relax) * (p0 - q)


def unswap(odd, first, then, behind, ahead):
    behind[...] = jnp.where(odd, first[...], then[...])
    ahead[...] = jnp.where(odd, then[...], first[...])


def two_stages(width, state, low, high, left, ground, mid, ghost):
    on_ground, on_top = lowest_slab(), highest_slab()
    inv_r, half_arc = radial_rates(width)
    cols = slice(0, width)
    turn = DT * half_arc

    def beyond(a, b):
        return jnp.zeros((b - a, width), jnp.float32)

    p0, p1, u0, v0, w0, w1 = [plane(state, i, k, width) for i, k in ((0, 0), (0, 1), (1, 0), (2, 0), (3, 0), (3, 1))]
    p15, w15 = plane(state, 0, HTS - 1, width), plane(state, 3, HTS - 1, width)
    bp = jnp.where(on_ground, p0, low[0:32, cols])
    bw = jnp.where(on_ground, ground[0, :, cols], low[32:64, cols])
    ghost[0], ghost[1], ghost[2], ghost[3] = bp, bw, high[0:32, cols], high[32:64, cols]

    top_p = high[64:96, cols] + (0.5 * DT) * w15
    top_w = high[96:128, cols] + (0.5 * DT) * p15
    low_p = low[64:96, cols] - (0.5 * DT) * w0
    low_w = low[96:128, cols] - (0.5 * DT) * p0
    v_diff = 2.0 * row_diff(v0, left[16:17, cols], beyond(16, 17)) * half_arc
    mid_p0 = p0 - DT * (radial_diff(u0) + u0 * inv_r + v_diff + 0.5 * (w1 - bw))
    mid_w0 = w0 - (0.5 * DT) * (p1 - bp)
    ghost[4] = jnp.where(on_ground, mid_p0, low_p)
    ghost[5] = jnp.where(on_ground, ground[1, :, cols] * (mid_p0 - ground[2, :, cols]) - mid_w0, low_w)
    ghost[6] = jnp.where(on_top, 0.0, top_p)
    ghost[7] = jnp.where(on_top, 0.0, top_w)

    mid[0, 0] = left[32:48, cols] - turn * state[2, 0, :, cols]
    mid[2, 0] = left[48:64, cols] - turn * state[0, 0, :, cols]
    mid[0, ROWS + 1] = beyond(32, 48) + turn * state[2, ROWS - 1, :, cols]
    mid[2, ROWS + 1] = beyond(48, 64) + turn * state[0, ROWS - 1, :, cols]

    def rates(p, u, v_diff, p_diff, w, j, first):
        p_low, w_low, p_high, w_high = [ghost[first + i, pl.ds(j, 1)] for i in range(4)]
        return (
            radial_diff(u) + u * inv_r + v_diff * half_arc + row_diff(w, w_low, w_high),
            radial_diff(p),
            half_arc * p_diff,
            row_diff(p, p_low, p_high),
        )

    def first(j, p_diff, v_diff):
        p, u, v, w = [state[i, j, :, cols] for i in range(4)]
        for i, (s, rate) in enumerate(zip((p, u, v, w), rates(p, u, v_diff, p_diff, w, j, 0))):
            mid[i, j + 1] = s - DT * rate

    first(0, state[0, 1, :, cols] - left[0:16, cols], state[2, 1, :, cols] - left[16:32, cols])
    end = ROWS - 2
    first(ROWS - 1, beyond(0, 16) - state[0, end, :, cols], beyond(16, 32) - state[2, end, :, cols])

    @pl.loop(1, ROWS - 1, unroll=5)
    def _(j):
        first(
            j,
            state[0, j + 1, :, cols] - state[0, j - 1, :, cols],
            state[2, j + 1, :, cols] - state[2, j - 1, :, cols],
        )

    def second(j):
        p, u, v, w = [mid[i, j + 1] for i in range(4)]
        found = rates(p, u, mid[2, j + 2] - mid[2, j], mid[0, j + 2] - mid[0, j], w, j, 4)
        return [0.5 * (state[i, j, :, cols] + m - DT * r) for i, (m, r) in enumerate(zip((p, u, v, w), found))]

    return second


def corner_weight(width):
    return (0.5 * DT) * (0.5 * DT) * radial_rates(width)[1]


def corner_weight(width):
    return (0.5 * DT) * (0.5 * DT) * radial_rates(width)[1]


def inner_kernel(
    state, left, ht_then, ht_first, ground, packed, left_corner, right_corner, low, high, mid, ghost
):
    unswap(odd_slab(), ht_first, ht_then, low, high)
    near = lax.broadcasted_iota(jnp.int32, (HTS, 128), 1) < NI
    height = lax.broadcasted_iota(jnp.int32, (HTS, 128), 0)
    second = two_stages(128, state, low, high, left, ground, mid, ghost)
    on_ground = lowest_slab()

    def emit(r, one, two):
        for i in range(COMPS):
            both = jnp.where(near, one[i], pltpu.roll(two[i], NI, 1))
            packed[pl.ds(i * HTS * LONG + r, HTS, stride=LONG), :] = both

    @pl.loop(0, HALF - 2, unroll=2)
    def _(l):
        emit(l + 2, second(l), second(l + LONG))

    turn = DT * radial_rates(128)[1]
    none = jnp.zeros((HTS, 128), jnp.float32)

    p0, v0 = state[0, 0, :, 0:128], state[2, 0, :, 0:128]
    own_p, own_v = mid[0, 1] - turn * left[16:32, 0:128], mid[2, 1] - turn * left[0:16, 0:128]
    far_p = -turn * v0
    wall = jnp.where(jnp.logical_and(on_ground, height == 0), (0.25 * DT) * left[64:65, 0:128] * far_p, 0.0)
    far_low = jnp.where(on_ground, far_p[0:1], -turn * low[128:129, 0:128])
    far_high = -turn * high[128:129, 0:128]
    last = [
        0.5 * (far_p - turn * own_v) + wall,
        (-0.5 * DT) * radial_diff(far_p),
        (-0.5 * turn) * (p0 + own_p),
        (-0.5 * DT) * row_diff(far_p, far_low, far_high),
    ]
    before = [0.5 * turn * turn * p0, none, 0.5 * turn * turn * v0, none]

    weight = corner_weight(128)

    end = ROWS - 1
    owed = [none, none]
    for below, above in ((w_below(low, ground, end), high[32 + end : 33 + end]), (low[129:130], high[129:130])):
        below, above = weight * below[:, 0:128], -weight * above[:, 0:128]
        owed.append(jnp.where(height == HTS - 1, above, jnp.where(height == 0, below, 0.0)))

    emit(0, before, second(HALF))
    emit(1, last, second(HALF + 1))
    emit(HALF, second(HALF - 2), owed)
    emit(HALF + 1, second(HALF - 1), [none] * COMPS)

    for out, j, corner in ((left_corner, 0, 128), (right_corner, end, 129)):
        rows = [w_below(low, ground, j), high[32 + j : 33 + j], low[corner : corner + 1], high[corner : corner + 1]]
        out[...] = jnp.concatenate(rows + [jnp.zeros((4, NR), jnp.float32)], 0)


def w_below(low, ground, j):
    return jnp.where(lowest_slab(), ground[0, j : j + 1], low[32 + j : 33 + j])


def outer_kernel(state, ht_then, ht_first, left, ground, stepped, low, high, mid, ghost):
    unswap(odd_slab(), ht_first, ht_then, low, high)
    second = two_stages(NR, state, low, high, left, ground, mid, ghost)

    @pl.loop(0, ROWS, unroll=2)
    def _(j):
        for i, value in enumerate(second(j)):
            stepped[i, j] = value


def turns_of(turn, x, parity, way):
    near = lax.broadcasted_iota(jnp.int32, (MODES // 2, 128), 1) < NI
    return [
        jnp.where(near, turn[x, parity, :, k : k + 1], turn[x, parity, :, k + 2 : k + 3])
        for k in (4 * way, 4 * way + 1)
    ]


def analysis_kernel(wave, wave_small, turn, circle, sums, folded):
    for z in range(8):
        for y in range(2):
            for q in range(SETS):
                one, two = [circle[pl.ds(((4 * z + k) * SETS + q) * LONG, LONG), :] for k in (y, y + 2)]
                at = pl.ds((2 * z + y) * LONG, LONG)
                folded[0, q, at, :] = one + two
                folded[1, q, at, :] = one - two
    x = lax.axis_index("x")
    h = MODES // 2
    near = lax.broadcasted_iota(jnp.int32, (h, 128), 1) < NI
    for parity in range(2):
        cs, sn = turns_of(turn, x, parity, 0)
        found = []
        for q in range(SETS):
            coef = product((wave[parity], wave_small[parity]), split(folded[parity, q]), ((1,), (0,)))
            a, b = coef[:h], coef[h:]
            found.append([t + pltpu.roll(t, NI, 1) for t in (a * cs - b * sn, a * sn + b * cs)])
        for k in range(2):
            at = (2 * parity + k) * h
            sums[at : at + h] = jnp.where(near, found[0][k], found[1][k])


def synthesis_kernel(wave, wave_small, turn, cutoff, mine, other, out):
    x = lax.axis_index("x")
    h = MODES // 2
    mode = lax.broadcasted_iota(jnp.int32, (h, 128), 0) * 2
    near = lax.broadcasted_iota(jnp.int32, (h, 128), 1) < NI
    limit = jnp.concatenate([cutoff[...], cutoff[...]], 1)
    parts = []
    for parity in range(2):
        cs, sn = turns_of(turn, x, parity, 1)
        keep = jnp.where(mode + parity < limit, turn[x, parity, :, 8:9], 0.0)
        a, b = [
            (mine[at : at + h] + other[at : at + h]) * keep for at in (2 * parity * h, (2 * parity + 1) * h)
        ]
        a_far, b_far = pltpu.roll(a, NI, 1), pltpu.roll(b, NI, 1)
        for q in range(SETS):
            a_all, b_all = [jnp.where(near == (q == 0), t, far) for t, far in ((a, a_far), (b, b_far))]
            both = jnp.concatenate([a_all * cs + b_all * sn, b_all * cs - a_all * sn], 0)
            parts.append(product((wave[parity], wave_small[parity]), split(both), ((0,), (0,))))
    for q in range(SETS):
        even, odd = parts[q], parts[SETS + q]
        for z in range(8):
            for y in range(2):
                at = slice((2 * z + y) * HALF, (2 * z + y + 1) * HALF)
                for k, value in ((y, even[at] + odd[at]), (y + 2, even[at] - odd[at])):
                    to = ((4 * z + k) * SETS + q) * HALF
                    out[to : to + HALF] = value


def edge_terms(right, left_corner, right_corner, ground):
    height = lax.broadcasted_iota(jnp.int32, (HTS, NR), 0)
    half_arc = radial_rates(NR)[1]
    turn, weight = DT * half_arc, corner_weight(NR)
    on_ground = lowest_slab()
    end = ROWS - 1
    p, v, mid_p, mid_v = [right[16 * i : 16 * i + 16] for i in range(4)]
    far_p = -turn * v
    wall = (0.25 * DT) * ground[1, end : end + 1] * far_p
    far_low = jnp.where(on_ground, far_p[0:1], 0.0)
    terms = {
        (0, end): 0.5 * (far_p - turn * mid_v) + jnp.where(jnp.logical_and(on_ground, height == 0), wall, 0.0),
        (1, end): (-0.5 * DT) * radial_diff(far_p),
        (2, end): (-0.5 * turn) * (p + mid_p),
        (3, end): (-0.5 * DT) * row_diff(far_p, far_low, jnp.zeros((1, NR), jnp.float32)),
        (0, end - 1): 0.5 * turn * turn * p,
        (2, end - 1): 0.5 * turn * turn * v,
        (2, 0): 0.0,
        (3, 0): 0.0,
    }
    for i, j in ((2, 0), (2, end), (3, 0), (3, end)):
        corner, sign = (left_corner, -1.0) if j == 0 else (right_corner, 1.0)
        at = 2 * (i - 2)
        below, above = (-sign * weight) * corner[at : at + 1], (sign * weight) * corner[at + 1 : at + 2]
        corner_term = jnp.where(height == HTS - 1, above, jnp.where(height == 0, below, 0.0))
        terms[i, j] = terms[i, j] + corner_term
    return terms


EDGE_PLACES = 8


def merge_kernel(
    stepped, back, right, left_corner, right_corner, ground, out, rows, tile, beside, edges, sems, edge_sems
):
    near = lax.broadcasted_iota(jnp.int32, (HTS, 128), 1) < NI
    loads = [
        pltpu.make_async_copy(stepped.at[i, :, :, pl.ds(0, 128)], beside.at[i], sems.at[0, i]) for i in range(COMPS)
    ]
    for copy in loads:
        copy.start()
    owed = edge_terms(right, left_corner, right_corner, ground)
    places = [(k, i, j) for k, (i, j) in enumerate(owed)]
    edge_loads = [
        pltpu.make_async_copy(stepped.at[i, j, :, pl.ds(128, 128)], edges.at[k], edge_sems.at[0, k]) for k, i, j in places
    ]
    for copy in edge_loads:
        copy.start()

    for i in range(COMPS * HTS):
        rows[pl.ds(i // HTS * HTS * HALF + i % HTS, HALF, stride=HTS), :] = back[i * HALF : (i + 1) * HALF]
    stores = []
    for i in range(COMPS):
        loads[i].wait()
        for k, comp, j in places:
            if comp == i:
                beside[i, j] = beside[i, j] + owed[i, j][:, 0:128]
        for l in range(HALF):
            at = (i * HALF + l) * HTS
            both = rows[at : at + HTS]
            tile[i, l] = jnp.where(near, both, beside[i, l])
            tile[i, l + HALF] = jnp.where(near, pltpu.roll(both, NI, 1), beside[i, l + HALF])
        stores.append(pltpu.make_async_copy(tile.at[i], out.at[i, :, :, pl.ds(0, 128)], sems.at[1, i]))
        stores[i].start()
    for k, i, j in places:
        edge_loads[k].wait()
        edges[k] = edges[k] + owed[i, j][:, 128:NR]
        stores.append(pltpu.make_async_copy(edges.at[k], out.at[i, j, :, pl.ds(128, 128)], edge_sems.at[1, k]))
        stores[-1].start()
    for copy in stores:
        copy.wait()


def per_device(state, zone_id, ground_aux, resistance, relax_rate, cutoff):
    f32 = jnp.float32
    vmem = pl.BlockSpec(memory_space=pltpu.VMEM)
    smem = pl.BlockSpec(memory_space=pltpu.SMEM)
    anywhere = pl.BlockSpec(memory_space=pl.ANY)

    def call(kernel, mib=8, **more):
        return pl.pallas_call(kernel, compiler_params=pltpu.CompilerParams(vmem_limit_bytes=mib * 2**20), **more)

    def shapes(*dims):
        return tuple(jax.ShapeDtypeStruct(d, f32) for d in dims)

    ht_message, az_message = (HT_ROWS, NR), (AZ_ROWS, NR)
    ht_then, ht_first = call(
        pack_kernel,
        out_shape=shapes(ht_message, ht_message),
        in_specs=[vmem],
        out_specs=(vmem,) * 2,
        scratch_shapes=[pltpu.VMEM(ht_message, f32)] * 2,
        name="pack",
    )(state)
    to_right, to_left = call(
        pack_az_kernel,
        out_shape=shapes(az_message, az_message),
        in_specs=[vmem] * 3 + [anywhere],
        out_specs=(vmem,) * 2,
        name="pack_az",
    )(state, zone_id, resistance.reshape(1, ZONES), ht_first)
    ground = call(
        ground_kernel,
        out_shape=shapes((3, ROWS, NR))[0],
        in_specs=[smem] * 2 + [vmem] * 3,
        out_specs=vmem,
        name="ground",
    )(resistance, relax_rate, state, zone_id, ground_aux)
    def swap(x, start):
        pairs = [(i, i + 1) for i in range(start, 3, 2)]
        return lax.ppermute(x, HT, pairs + [(b, a) for a, b in pairs])

    rightward = [(i, (i + 1) % SECTORS) for i in range(SECTORS)]
    leftward = [(b, a) for a, b in rightward]
    left, right = lax.ppermute(to_right, AZ, rightward), lax.ppermute(to_left, AZ, leftward)
    ht_then, ht_first = swap(ht_then, 1), swap(ht_first, 0)

    def scratch(width):
        return [pltpu.VMEM((COMPS, ROWS + 2, HTS, width), f32), pltpu.VMEM((8, ROWS, width), f32)]

    halos = [pltpu.VMEM(ht_message, f32)] * 2
    packed, to_left, to_right = call(
        inner_kernel,
        mib=12,
        out_shape=shapes((COMPS * HTS * LONG, 128), (8, NR), (8, NR)),
        in_specs=[vmem] * 5,
        out_specs=(vmem,) * 3,
        scratch_shapes=halos + scratch(128),
        cost_estimate=pl.CostEstimate(flops=10**7, bytes_accessed=6 * 10**6, transcendentals=0),
        name="inner",
    )(state, left, ht_then, ht_first, ground)
    circle = lax.all_to_all(packed.reshape(PEERS, SETS * LONG, 1, 128), SPREAD, 0, 0, tiled=True)
    left_corner, right_corner = lax.ppermute(to_right, AZ, rightward), lax.ppermute(to_left, AZ, leftward)
    stepped = call(
        outer_kernel,
        mib=16,
        out_shape=shapes((COMPS, ROWS, HTS, NR))[0],
        in_specs=[vmem] * 5,
        out_specs=vmem,
        scratch_shapes=halos + scratch(NR),
        cost_estimate=pl.CostEstimate(flops=2 * 10**7, bytes_accessed=2 * 10**7, transcendentals=0),
        name="outer",
    )(state, ht_then, ht_first, left, ground)
    there, back, turns = jax.tree.map(jnp.asarray, mode_tables())
    sums = call(
        analysis_kernel,
        out_shape=shapes((2 * MODES, 128))[0],
        in_specs=[vmem] * 4,
        out_specs=vmem,
        scratch_shapes=[pltpu.VMEM((2, SETS, PEERS // 2 * LONG, 128), f32)],
        name="analysis",
    )(*there, turns, circle.reshape(PEERS * SETS * LONG, 128))
    other = lax.ppermute(sums, "x", [(0, 1), (1, 0)])
    kept = call(
        synthesis_kernel,
        out_shape=shapes((PEERS * SETS * HALF, 128))[0],
        in_specs=[vmem] * 6,
        out_specs=vmem,
        name="synthesis",
    )(*back, turns, cutoff.reshape(1, NI), sums, other)
    back = lax.all_to_all(kept.reshape(PEERS, SETS * HALF, 128), SPREAD, 0, 0, tiled=True)
    return call(
        merge_kernel,
        out_shape=jax.ShapeDtypeStruct(stepped.shape, f32),
        in_specs=[anywhere] + [vmem] * 5,
        out_specs=anywhere,
        scratch_shapes=[
            pltpu.VMEM((COMPS * HTS * HALF, 128), f32),
            pltpu.VMEM((COMPS, ROWS, HTS, 128), f32),
            pltpu.VMEM((COMPS, ROWS, HTS, 128), f32),
            pltpu.VMEM((EDGE_PLACES, HTS, 128), f32),
            pltpu.SemaphoreType.DMA((2, COMPS)),
            pltpu.SemaphoreType.DMA((2, EDGE_PLACES)),
        ],
        input_output_aliases={0: 0},
        name="merge",
    )(stepped, back.reshape(COMPS * HTS * HALF, 128), right, left_corner, right_corner, ground)


def solution(mesh):
    fine = Mesh(mesh.devices.reshape(4, 2, 8, 2, 2), AZ + HT)
    return jax.shard_map(
        per_device,
        mesh=fine,
        in_specs=(P(None, AZ, HT, None), P(AZ, None), P(AZ, None), P(), P(), P()),
        out_specs=P(None, AZ, HT, None),
        check_vma=False,
    )
```

```python
import functools
import math

import jax
import jax.numpy as jnp
import numpy as np
from jax import lax
from jax.experimental import pallas as pl
from jax.experimental.pallas import tpu as pltpu
from jax.sharding import Mesh, PartitionSpec as P

NA = 2048
NI = 64
MODES = 128
ZONES = 8
SECTORS = 64
ROWS = NA // SECTORS
HALF = ROWS // 2
LONG = HALF + 1
HTS = 16
NR = 256
COMPS = 4
DT = 0.4

AZ = ("y", "x", "z")
SPREAD = AZ
HT = ("hx", "core")


def mode_tables():
    first = np.arange(SECTORS // 2)[:, None] * ROWS
    there = (first - 1 + np.arange(LONG)[None, :]).reshape(-1)
    back = (first + np.arange(HALF)[None, :]).reshape(-1)
    tables = []
    for parity in range(2):
        modes = np.arange(parity, MODES, 2)
        waves = []
        for azimuth in (there, back):
            phase = (modes[:, None] * azimuth[None, :] % NA) * (2.0 * math.pi / NA)
            waves.append(np.concatenate([np.cos(phase), np.sin(phase)], 0))
        more = np.zeros((MODES // 2, 128))
        for k, by in enumerate((LONG, HALF)):
            turn = (modes * by % NA) * (2.0 * math.pi / NA)
            more[:, 2 * k] = np.cos(turn)
            more[:, 2 * k + 1] = np.sin(turn)
        more[:, 4] = np.where(modes == 0, 1.0, 2.0) / NA
        tables.append((*waves, more))
    there, back, turns = [np.stack(t).astype(np.float32) for t in zip(*tables)]
    return (*split(there), *split(back), turns)


def split(x):
    x = x.astype(np.float32) if isinstance(x, np.ndarray) else x
    large = x.astype(jnp.bfloat16)
    return large, (x - large.astype(jnp.float32)).astype(jnp.bfloat16)


def product(a, b, dims):
    dot = functools.partial(lax.dot_general, dimension_numbers=(dims, ((), ())), preferred_element_type=jnp.float32)
    return dot(a[0], b[0]) + (dot(a[0], b[1]) + dot(a[1], b[0]))


def radial_diff(x):
    n = x.shape[-1]
    lane = lax.broadcasted_iota(jnp.int32, (1, n), 1)
    after = jnp.where(lane == NR - 1, 0.0, 0.5)
    before = jnp.where(lane == 0, 0.0, 0.5)
    return after * pltpu.roll(x, n - 1, x.ndim - 1) - before * pltpu.roll(x, 1, x.ndim - 1)


def row_diff(x, low, high):
    up = jnp.concatenate([x[1:], high], 0)
    down = jnp.concatenate([low, x[:-1]], 0)
    return 0.5 * (up - down)


def radial_rates(n):
    lane = lax.broadcasted_iota(jnp.int32, (1, n), 1).astype(jnp.float32)
    inv_r = 1.0 / (NA / (2.0 * math.pi) + lane)
    return inv_r, 0.5 * (NA / (2.0 * math.pi)) * inv_r


def plane(state, comp, height, width=NR):
    return state[comp, :, height, 0:width]


def lookup(ids, table):
    out = jnp.zeros(ids.shape, jnp.float32)
    for k in range(ZONES):
        out = jnp.where(ids == k, table[k], out)
    return out


def odd_slab():
    return lax.axis_index("core") == 1


def odd_sector():
    return lax.rem(lax.axis_index("z"), 2) == 1


def lowest_slab():
    return lax.axis_index("hx") * 2 + lax.axis_index("core") == 0


def highest_slab():
    return lax.axis_index("hx") * 2 + lax.axis_index("core") == 3


HT_ROWS = 136
AZ_ROWS = 64
AZ_LONG = 144


def pack_kernel(state, az_then, ht_then, az_first, ht_first, up, down, to_left, to_right):
    inv_r, half_arc = radial_rates(NR)
    zero = jnp.zeros((1, NR), jnp.float32)
    for out, edge, inside, sign in ((up, HTS - 1, HTS - 2, 1.0), (down, 0, 1, -1.0)):
        p, w, u, v = [plane(state, i, edge) for i in (0, 3, 1, 2)]
        p_in, w_in = plane(state, 0, inside), plane(state, 3, inside)
        out[0:32] = p
        out[32:64] = w
        turn = 2.0 * row_diff(v, zero, zero) * half_arc
        out[64:96] = p - DT * (radial_diff(u) + u * inv_r + turn - (0.5 * sign) * w_in)
        out[96:128] = w + (0.5 * DT * sign) * p_in
        out[128:129] = v[0:1]
        out[129:130] = v[ROWS - 1 : ROWS]
        out[130:HT_ROWS] = jnp.zeros((HT_ROWS - 130, NR), jnp.float32)

    for out, j, inside, sign in ((to_right, ROWS - 1, ROWS - 2, 1.0), (to_left, 0, 1, -1.0)):
        p, u, v, w = [state[i, j] for i in range(4)]
        out[0:16] = p
        out[16:32] = v
        rate = radial_diff(u) + u * inv_r + row_diff(w, zero, zero) - sign * half_arc * state[2, inside]
        out[32:48] = p - DT * rate
        out[48:64] = v + (DT * sign) * half_arc * state[0, inside]

    for odd, one, two, ahead, behind in (
        (odd_slab(), ht_first, ht_then, up, down),
        (odd_sector(), az_first, az_then.at[0:AZ_ROWS], to_right, to_left),
    ):
        one[...] = jnp.where(odd, behind[...], ahead[...])
        two[...] = jnp.where(odd, ahead[...], behind[...])
    az_then[AZ_ROWS:AZ_LONG] = jnp.zeros((AZ_LONG - AZ_ROWS, NR), jnp.float32)


def ground_kernel(resistance, relax, state, zone, aux, ground):
    ids, q = zone[...], aux[...]
    p0, w0 = plane(state, 0, 0), plane(state, 3, 0)
    twice = 2.0 * (1.0 / lookup(ids, resistance))
    ground[0] = twice * (p0 - q) - w0
    ground[1] = twice
    ground[2] = q + DT * lookup(ids, relax) * (p0 - q)


def unswap(odd, first, then, behind, ahead):
    behind[...] = jnp.where(odd, first[...], then[...])
    ahead[...] = jnp.where(odd, then[...], first[...])


def two_stages(width, state, low, high, left, right, ground, mid, ghost):
    on_ground, on_top = lowest_slab(), highest_slab()
    inv_r, half_arc = radial_rates(width)
    cols = slice(0, width)
    turn = DT * half_arc

    p0, p1, u0, v0, w0, w1 = [plane(state, i, k, width) for i, k in ((0, 0), (0, 1), (1, 0), (2, 0), (3, 0), (3, 1))]
    p15, w15 = plane(state, 0, HTS - 1, width), plane(state, 3, HTS - 1, width)
    bp = jnp.where(on_ground, p0, low[0:32, cols])
    bw = jnp.where(on_ground, ground[0, :, cols], low[32:64, cols])
    ghost[0], ghost[1], ghost[2], ghost[3] = bp, bw, high[0:32, cols], high[32:64, cols]

    top_p = high[64:96, cols] + (0.5 * DT) * w15
    top_w = high[96:128, cols] + (0.5 * DT) * p15
    low_p = low[64:96, cols] - (0.5 * DT) * w0
    low_w = low[96:128, cols] - (0.5 * DT) * p0
    v_diff = 2.0 * row_diff(v0, left[16:17, cols], right[16:17, cols]) * half_arc
    mid_p0 = p0 - DT * (radial_diff(u0) + u0 * inv_r + v_diff + 0.5 * (w1 - bw))
    mid_w0 = w0 - (0.5 * DT) * (p1 - bp)
    ghost[4] = jnp.where(on_ground, mid_p0, low_p)
    ghost[5] = jnp.where(on_ground, ground[1, :, cols] * (mid_p0 - ground[2, :, cols]) - mid_w0, low_w)
    ghost[6] = jnp.where(on_top, 0.0, top_p)
    ghost[7] = jnp.where(on_top, 0.0, top_w)

    mid[0, 0] = left[32:48, cols] - turn * state[2, 0, :, cols]
    mid[2, 0] = left[48:64, cols] - turn * state[0, 0, :, cols]
    mid[0, ROWS + 1] = right[32:48, cols] + turn * state[2, ROWS - 1, :, cols]
    mid[2, ROWS + 1] = right[48:64, cols] + turn * state[0, ROWS - 1, :, cols]

    def rates(p, u, v_diff, p_diff, w, j, first):
        p_low, w_low, p_high, w_high = [ghost[first + i, pl.ds(j, 1)] for i in range(4)]
        return (
            radial_diff(u) + u * inv_r + v_diff * half_arc + row_diff(w, w_low, w_high),
            radial_diff(p),
            half_arc * p_diff,
            row_diff(p, p_low, p_high),
        )

    def first(j, p_diff, v_diff):
        p, u, v, w = [state[i, j, :, cols] for i in range(4)]
        for i, (s, rate) in enumerate(zip((p, u, v, w), rates(p, u, v_diff, p_diff, w, j, 0))):
            mid[i, j + 1] = s - DT * rate

    first(0, state[0, 1, :, cols] - left[0:16, cols], state[2, 1, :, cols] - left[16:32, cols])
    end = ROWS - 2
    first(ROWS - 1, right[0:16, cols] - state[0, end, :, cols], right[16:32, cols] - state[2, end, :, cols])

    @pl.loop(1, ROWS - 1, unroll=5)
    def _(j):
        first(
            j,
            state[0, j + 1, :, cols] - state[0, j - 1, :, cols],
            state[2, j + 1, :, cols] - state[2, j - 1, :, cols],
        )

    def second(j):
        p, u, v, w = [mid[i, j + 1] for i in range(4)]
        found = rates(p, u, mid[2, j + 2] - mid[2, j], mid[0, j + 2] - mid[0, j], w, j, 4)
        return [0.5 * (state[i, j, :, cols] + m - DT * r) for i, (m, r) in enumerate(zip((p, u, v, w), found))]

    return second


def corner_weight(width):
    return (0.5 * DT) * (0.5 * DT) * radial_rates(width)[1]


def inner_kernel(
    state, az_then, ht_then, az_first, ht_first, ground, packed, low, high, left, right, to_left, to_right, mid, ghost
):
    unswap(odd_slab(), ht_first, ht_then, low, high)
    unswap(odd_sector(), az_first, az_then.at[0:AZ_ROWS], left, right)
    near = lax.broadcasted_iota(jnp.int32, (HTS, 128), 1) < NI
    height = lax.broadcasted_iota(jnp.int32, (HTS, 128), 0)
    second = two_stages(128, state, low, high, left, right, ground, mid, ghost)

    def emit(r, one, two):
        for i in range(COMPS):
            both = jnp.where(near, one[i], pltpu.roll(two[i], NI, 1))
            packed[pl.ds(i * HTS * LONG + r, HTS, stride=LONG), :] = both

    @pl.loop(0, HALF - 1, unroll=3)
    def _(l):
        emit(l + 1, second(l), second(l + LONG))

    weight = corner_weight(128)

    def beyond(row):
        at, end = 32 + row * (ROWS - 1), row * (ROWS - 1)
        w_low = jnp.where(lowest_slab(), ground[0, end : end + 1], low[at : at + 1])
        return (w_low, high[at : at + 1]), (low[128 + row : 129 + row], high[128 + row : 129 + row])

    def owed(row, sign):
        out = [jnp.zeros((HTS, 128), jnp.float32)] * 2
        for below, above in beyond(row):
            below, above = [(by * weight) * x[:, 0:128] for by, x in ((-sign, below), (sign, above))]
            out.append(jnp.where(height == HTS - 1, above, jnp.where(height == 0, below, 0.0)))
        return out

    emit(0, owed(0, 1.0), second(HALF))
    emit(HALF, second(HALF - 1), owed(1, -1.0))

    for out, row in ((to_left, 0), (to_right, 1)):
        (w_low, w_high), (v_low, v_high) = beyond(row)
        out[...] = jnp.concatenate([w_low, w_high, v_low, v_high, jnp.zeros((4, NR), jnp.float32)], 0)


def outer_kernel(state, low, high, left, right, ground, stepped, mid, ghost):
    second = two_stages(NR, state, low, high, left, right, ground, mid, ghost)

    @pl.loop(0, ROWS, unroll=2)
    def _(j):
        for i, value in enumerate(second(j)):
            stepped[i, j] = value


def filter_kernel(there, there_small, back, back_small, turn, cutoff, x_ref, o_ref):
    n, m = NA // 4, SECTORS // 2 * LONG
    first, second = x_ref[:m], x_ref[m:]
    h = MODES // 2
    mode = lax.broadcasted_iota(jnp.int32, (h, 128), 0) * 2
    near = lax.broadcasted_iota(jnp.int32, (h, 128), 1) < NI
    limit = jnp.concatenate([cutoff[...], cutoff[...]], 1)
    outs = []
    for parity in range(2):
        folded = first + second if parity == 0 else first - second
        cs, sn, cs_back, sn_back, weight = [turn[parity, :, k : k + 1] for k in range(5)]
        coef = product((there[parity], there_small[parity]), split(folded), ((1,), (0,)))
        a, b = coef[:h], coef[h:]
        a_all = jnp.where(near, a, a * cs - b * sn)
        b_all = jnp.where(near, b, a * sn + b * cs)
        keep = jnp.where(mode + parity < limit, weight, 0.0)
        a_all = (a_all + pltpu.roll(a_all, NI, 1)) * keep
        b_all = (b_all + pltpu.roll(b_all, NI, 1)) * keep
        a_back = jnp.where(near, a_all, a_all * cs_back + b_all * sn_back)
        b_back = jnp.where(near, b_all, b_all * cs_back - a_all * sn_back)
        both = jnp.concatenate([a_back, b_back], 0)
        outs.append(product((back[parity], back_small[parity]), split(both), ((0,), (0,))))
    o_ref[:n] = outs[0] + outs[1]
    o_ref[n:] = outs[0] - outs[1]


def merge_kernel(stepped, back, left_corner, right_corner, out, rows, tile, beside, edges, sems, edge_sems):
    near = lax.broadcasted_iota(jnp.int32, (HTS, 128), 1) < NI
    height = lax.broadcasted_iota(jnp.int32, (HTS, NR), 0)
    loads = [
        pltpu.make_async_copy(stepped.at[i, :, :, pl.ds(0, 128)], beside.at[i], sems.at[0, i]) for i in range(COMPS)
    ]
    places = [(k, i, j) for k, (i, j) in enumerate(((2, 0), (2, ROWS - 1), (3, 0), (3, ROWS - 1)))]
    edge_loads = [
        pltpu.make_async_copy(stepped.at[i, j, :, pl.ds(128, 128)], edges.at[k], edge_sems.at[0, k]) for k, i, j in places
    ]
    for copy in loads + edge_loads:
        copy.start()

    weight = corner_weight(NR)
    owed = {}
    for k, i, j in places:
        corner, sign = (left_corner, -1.0) if j == 0 else (right_corner, 1.0)
        at = 2 * (i - 2)
        below, above = (-sign * weight) * corner[at : at + 1], (sign * weight) * corner[at + 1 : at + 2]
        owed[i, j] = jnp.where(height == HTS - 1, above, jnp.where(height == 0, below, 0.0))

    for i in range(COMPS * HTS):
        rows[pl.ds(i // HTS * HTS * HALF + i % HTS, HALF, stride=HTS), :] = back[i * HALF : (i + 1) * HALF]
    stores = []
    for i in range(COMPS):
        loads[i].wait()
        for j in (0, ROWS - 1):
            if i >= 2:
                beside[i, j] = beside[i, j] + owed[i, j][:, 0:128]
        for l in range(HALF):
            at = (i * HALF + l) * HTS
            both = rows[at : at + HTS]
            tile[i, l] = jnp.where(near, both, beside[i, l])
            tile[i, l + HALF] = jnp.where(near, pltpu.roll(both, NI, 1), beside[i, l + HALF])
        stores.append(pltpu.make_async_copy(tile.at[i], out.at[i, :, :, pl.ds(0, 128)], sems.at[1, i]))
        stores[i].start()
    for k, i, j in places:
        edge_loads[k].wait()
        edges[k] = edges[k] + owed[i, j][:, 128:NR]
        stores.append(pltpu.make_async_copy(edges.at[k], out.at[i, j, :, pl.ds(128, 128)], edge_sems.at[1, k]))
        stores[-1].start()
    for copy in stores:
        copy.wait()


def per_device(state, zone_id, ground_aux, resistance, relax_rate, cutoff):
    f32 = jnp.float32
    vmem = pl.BlockSpec(memory_space=pltpu.VMEM)
    smem = pl.BlockSpec(memory_space=pltpu.SMEM)
    anywhere = pl.BlockSpec(memory_space=pl.ANY)

    def call(kernel, mib=8, **more):
        return pl.pallas_call(kernel, compiler_params=pltpu.CompilerParams(vmem_limit_bytes=mib * 2**20), **more)

    def shapes(*dims):
        return tuple(jax.ShapeDtypeStruct(d, f32) for d in dims)

    ht_message, az_message = (HT_ROWS, NR), (AZ_ROWS, NR)
    az_then, ht_then, az_first, ht_first = call(
        pack_kernel,
        out_shape=shapes((AZ_LONG, NR), ht_message, az_message, ht_message),
        in_specs=[vmem],
        out_specs=(vmem,) * 4,
        scratch_shapes=[pltpu.VMEM(m, f32) for m in (ht_message, ht_message, az_message, az_message)],
        name="pack",
    )(state)
    ground = call(
        ground_kernel,
        out_shape=shapes((3, ROWS, NR))[0],
        in_specs=[smem] * 2 + [vmem] * 3,
        out_specs=vmem,
        name="ground",
    )(resistance, relax_rate, state, zone_id, ground_aux)
    def swap(x, axes, size, start, closed):
        pairs = [(i % size, (i + 1) % size) for i in range(start, size if closed else size - 1, 2)]
        return lax.ppermute(x, axes, pairs + [(b, a) for a, b in pairs])

    az_then = swap(az_then, AZ, SECTORS, 1, True)
    ht_then = swap(ht_then, HT, 4, 1, False)
    az_first = swap(az_first, AZ, SECTORS, 0, True)
    ht_first = swap(ht_first, HT, 4, 0, False)

    def scratch(width):
        return [pltpu.VMEM((COMPS, ROWS + 2, HTS, width), f32), pltpu.VMEM((8, ROWS, width), f32)]

    packed, low, high, left, right, to_left, to_right = call(
        inner_kernel,
        mib=12,
        out_shape=shapes(
            (COMPS * HTS * LONG, 128), ht_message, ht_message, az_message, az_message, (8, NR), (8, NR)
        ),
        in_specs=[vmem] * 6,
        out_specs=(vmem,) * 7,
        scratch_shapes=scratch(128),
        cost_estimate=pl.CostEstimate(flops=10**7, bytes_accessed=6 * 10**6, transcendentals=0),
        name="inner",
    )(state, az_then, ht_then, az_first, ht_first, ground)
    circle = lax.all_to_all(packed.reshape(SECTORS, LONG, 1, 128), SPREAD, 0, 0, tiled=True)
    left_corner = lax.ppermute(to_right, AZ, [(i, (i + 1) % SECTORS) for i in range(SECTORS)])
    right_corner = lax.ppermute(to_left, AZ, [((i + 1) % SECTORS, i) for i in range(SECTORS)])
    stepped = call(
        outer_kernel,
        mib=16,
        out_shape=shapes((COMPS, ROWS, HTS, NR))[0],
        in_specs=[vmem] * 6,
        out_specs=vmem,
        scratch_shapes=scratch(NR),
        cost_estimate=pl.CostEstimate(flops=2 * 10**7, bytes_accessed=2 * 10**7, transcendentals=0),
        name="outer",
    )(state, low, high, left, right, ground)
    kept = call(
        filter_kernel, out_shape=shapes((NA // 2, 128))[0], in_specs=[vmem] * 7, out_specs=vmem, name="filter"
    )(*map(jnp.asarray, mode_tables()), cutoff.reshape(1, NI), circle.reshape(SECTORS * LONG, 128))
    back = lax.all_to_all(kept.reshape(SECTORS, HALF, 128), SPREAD, 0, 0, tiled=True)
    return call(
        merge_kernel,
        out_shape=jax.ShapeDtypeStruct(stepped.shape, f32),
        in_specs=[anywhere] + [vmem] * 3,
        out_specs=anywhere,
        scratch_shapes=[
            pltpu.VMEM((COMPS * HTS * HALF, 128), f32),
            pltpu.VMEM((COMPS, ROWS, HTS, 128), f32),
            pltpu.VMEM((COMPS, ROWS, HTS, 128), f32),
            pltpu.VMEM((4, HTS, 128), f32),
            pltpu.SemaphoreType.DMA((2, COMPS)),
            pltpu.SemaphoreType.DMA((2, 4)),
        ],
        input_output_aliases={0: 0},
        name="merge",
    )(stepped, back.reshape(COMPS * HTS * HALF, 128), left_corner, right_corner)


def solution(mesh):
    fine = Mesh(mesh.devices.reshape(4, 2, 8, 2, 2), AZ + HT)
    return jax.shard_map(
        per_device,
        mesh=fine,
        in_specs=(P(None, AZ, HT, None), P(AZ, None), P(AZ, None), P(), P(), P()),
        out_specs=P(None, AZ, HT, None),
        check_vma=False,
    )
```

```python
import functools
import math

import jax
import jax.numpy as jnp
import numpy as np
from jax import lax
from jax.experimental import pallas as pl
from jax.experimental.pallas import tpu as pltpu
from jax.sharding import Mesh, PartitionSpec as P

NA = 2048
NI = 64
MODES = 128
ZONES = 8
SECTORS = 64
ROWS = NA // SECTORS
HALF = ROWS // 2
LONG = HALF + 1
HTS = 16
NR = 256
COMPS = 4
DT = 0.4

AZ = ("y", "x", "z")
SPREAD = AZ
HT = ("hx", "core")


def mode_tables():
    first = np.arange(SECTORS // 2)[:, None] * ROWS
    there = (first - 1 + np.arange(LONG)[None, :]).reshape(-1)
    back = (first + np.arange(HALF)[None, :]).reshape(-1)
    tables = []
    for parity in range(2):
        modes = np.arange(parity, MODES, 2)
        waves = []
        for azimuth in (there, back):
            phase = (modes[:, None] * azimuth[None, :] % NA) * (2.0 * math.pi / NA)
            waves.append(np.concatenate([np.cos(phase), np.sin(phase)], 0))
        more = np.zeros((MODES // 2, 128))
        for k, by in enumerate((LONG, HALF)):
            turn = (modes * by % NA) * (2.0 * math.pi / NA)
            more[:, 2 * k] = np.cos(turn)
            more[:, 2 * k + 1] = np.sin(turn)
        more[:, 4] = np.where(modes == 0, 1.0, 2.0) / NA
        tables.append((*waves, more))
    there, back, turns = [np.stack(t).astype(np.float32) for t in zip(*tables)]
    return (*split(there), *split(back), turns)


def split(x):
    x = x.astype(np.float32) if isinstance(x, np.ndarray) else x
    large = x.astype(jnp.bfloat16)
    return large, (x - large.astype(jnp.float32)).astype(jnp.bfloat16)


def product(a, b, dims):
    dot = functools.partial(lax.dot_general, dimension_numbers=(dims, ((), ())), preferred_element_type=jnp.float32)
    return dot(a[0], b[0]) + (dot(a[0], b[1]) + dot(a[1], b[0]))


def radial_diff(x):
    n = x.shape[-1]
    lane = lax.broadcasted_iota(jnp.int32, (1, n), 1)
    after = jnp.where(lane == NR - 1, 0.0, 0.5)
    before = jnp.where(lane == 0, 0.0, 0.5)
    return after * pltpu.roll(x, n - 1, x.ndim - 1) - before * pltpu.roll(x, 1, x.ndim - 1)


def row_diff(x, low, high):
    up = jnp.concatenate([x[1:], high], 0)
    down = jnp.concatenate([low, x[:-1]], 0)
    return 0.5 * (up - down)


def radial_rates(n):
    lane = lax.broadcasted_iota(jnp.int32, (1, n), 1).astype(jnp.float32)
    inv_r = 1.0 / (NA / (2.0 * math.pi) + lane)
    return inv_r, 0.5 * (NA / (2.0 * math.pi)) * inv_r


def plane(state, comp, height, width=NR):
    return state[comp, :, height, 0:width]


def lookup(ids, table):
    out = jnp.zeros(ids.shape, jnp.float32)
    for k in range(ZONES):
        out = jnp.where(ids == k, table[k], out)
    return out


def odd_slab():
    return lax.axis_index("core") == 1


def odd_sector():
    return lax.rem(lax.axis_index("z"), 2) == 1


def lowest_slab():
    return lax.axis_index("hx") * 2 + lax.axis_index("core") == 0


def highest_slab():
    return lax.axis_index("hx") * 2 + lax.axis_index("core") == 3


HT_ROWS = 136
AZ_ROWS = 64
AZ_LONG = 144


def pack_kernel(state, az_then, ht_first, az_first, ht_then, up, down, to_left, to_right):
    inv_r, half_arc = radial_rates(NR)
    zero = jnp.zeros((1, NR), jnp.float32)
    for out, edge, inside, sign in ((up, HTS - 1, HTS - 2, 1.0), (down, 0, 1, -1.0)):
        p, w, u, v = [plane(state, i, edge) for i in (0, 3, 1, 2)]
        p_in, w_in = plane(state, 0, inside), plane(state, 3, inside)
        out[0:32] = p
        out[32:64] = w
        turn = 2.0 * row_diff(v, zero, zero) * half_arc
        out[64:96] = p - DT * (radial_diff(u) + u * inv_r + turn - (0.5 * sign) * w_in)
        out[96:128] = w + (0.5 * DT * sign) * p_in
        out[128:129] = v[0:1]
        out[129:130] = v[ROWS - 1 : ROWS]
        out[130:HT_ROWS] = jnp.zeros((HT_ROWS - 130, NR), jnp.float32)

    for out, j, inside, sign in ((to_right, ROWS - 1, ROWS - 2, 1.0), (to_left, 0, 1, -1.0)):
        p, u, v, w = [state[i, j] for i in range(4)]
        out[0:16] = p
        out[16:32] = v
        rate = radial_diff(u) + u * inv_r + row_diff(w, zero, zero) - sign * half_arc * state[2, inside]
        out[32:48] = p - DT * rate
        out[48:64] = v + (DT * sign) * half_arc * state[0, inside]

    for odd, one, two, ahead, behind in (
        (odd_slab(), ht_first, ht_then, up, down),
        (odd_sector(), az_first, az_then.at[0:AZ_ROWS], to_right, to_left),
    ):
        one[...] = jnp.where(odd, behind[...], ahead[...])
        two[...] = jnp.where(odd, ahead[...], behind[...])
    az_then[AZ_ROWS:AZ_LONG] = jnp.zeros((AZ_LONG - AZ_ROWS, NR), jnp.float32)


def ground_kernel(resistance, relax, state, zone, aux, ground):
    ids, q = zone[...], aux[...]
    p0, w0 = plane(state, 0, 0), plane(state, 3, 0)
    twice = 2.0 * (1.0 / lookup(ids, resistance))
    ground[0] = twice * (p0 - q) - w0
    ground[1] = twice
    ground[2] = q + DT * lookup(ids, relax) * (p0 - q)


def unswap(odd, first, then, behind, ahead):
    behind[...] = jnp.where(odd, first[...], then[...])
    ahead[...] = jnp.where(odd, then[...], first[...])


def two_stages(width, state, low, high, left, right, ground, mid, ghost):
    on_ground, on_top = lowest_slab(), highest_slab()
    inv_r, half_arc = radial_rates(width)
    cols = slice(0, width)
    turn = DT * half_arc

    p0, p1, u0, v0, w0, w1 = [plane(state, i, k, width) for i, k in ((0, 0), (0, 1), (1, 0), (2, 0), (3, 0), (3, 1))]
    p15, w15 = plane(state, 0, HTS - 1, width), plane(state, 3, HTS - 1, width)
    bp = jnp.where(on_ground, p0, low[0:32, cols])
    bw = jnp.where(on_ground, ground[0, :, cols], low[32:64, cols])
    ghost[0], ghost[1], ghost[2], ghost[3] = bp, bw, high[0:32, cols], high[32:64, cols]

    top_p = high[64:96, cols] + (0.5 * DT) * w15
    top_w = high[96:128, cols] + (0.5 * DT) * p15
    low_p = low[64:96, cols] - (0.5 * DT) * w0
    low_w = low[96:128, cols] - (0.5 * DT) * p0
    v_diff = 2.0 * row_diff(v0, left[16:17, cols], right[16:17, cols]) * half_arc
    mid_p0 = p0 - DT * (radial_diff(u0) + u0 * inv_r + v_diff + 0.5 * (w1 - bw))
    mid_w0 = w0 - (0.5 * DT) * (p1 - bp)
    ghost[4] = jnp.where(on_ground, mid_p0, low_p)
    ghost[5] = jnp.where(on_ground, ground[1, :, cols] * (mid_p0 - ground[2, :, cols]) - mid_w0, low_w)
    ghost[6] = jnp.where(on_top, 0.0, top_p)
    ghost[7] = jnp.where(on_top, 0.0, top_w)

    mid[0, 0] = left[32:48, cols] - turn * state[2, 0, :, cols]
    mid[2, 0] = left[48:64, cols] - turn * state[0, 0, :, cols]
    mid[0, ROWS + 1] = right[32:48, cols] + turn * state[2, ROWS - 1, :, cols]
    mid[2, ROWS + 1] = right[48:64, cols] + turn * state[0, ROWS - 1, :, cols]

    def rates(p, u, v_diff, p_diff, w, j, first):
        p_low, w_low, p_high, w_high = [ghost[first + i, pl.ds(j, 1)] for i in range(4)]
        return (
            radial_diff(u) + u * inv_r + v_diff * half_arc + row_diff(w, w_low, w_high),
            radial_diff(p),
            half_arc * p_diff,
            row_diff(p, p_low, p_high),
        )

    def first(j, p_diff, v_diff):
        p, u, v, w = [state[i, j, :, cols] for i in range(4)]
        for i, (s, rate) in enumerate(zip((p, u, v, w), rates(p, u, v_diff, p_diff, w, j, 0))):
            mid[i, j + 1] = s - DT * rate

    first(0, state[0, 1, :, cols] - left[0:16, cols], state[2, 1, :, cols] - left[16:32, cols])
    end = ROWS - 2
    first(ROWS - 1, right[0:16, cols] - state[0, end, :, cols], right[16:32, cols] - state[2, end, :, cols])

    @pl.loop(1, ROWS - 1, unroll=5)
    def _(j):
        first(
            j,
            state[0, j + 1, :, cols] - state[0, j - 1, :, cols],
            state[2, j + 1, :, cols] - state[2, j - 1, :, cols],
        )

    def second(j):
        p, u, v, w = [mid[i, j + 1] for i in range(4)]
        found = rates(p, u, mid[2, j + 2] - mid[2, j], mid[0, j + 2] - mid[0, j], w, j, 4)
        return [0.5 * (state[i, j, :, cols] + m - DT * r) for i, (m, r) in enumerate(zip((p, u, v, w), found))]

    return second


def corner_weight(width):
    return (0.5 * DT) * (0.5 * DT) * radial_rates(width)[1]


def inner_kernel(
    state, az_then, ht_first, az_first, ht_then, ground, packed, low, high, left, right, to_left, to_right, mid, ghost
):
    unswap(odd_slab(), ht_first, ht_then, low, high)
    unswap(odd_sector(), az_first, az_then.at[0:AZ_ROWS], left, right)
    near = lax.broadcasted_iota(jnp.int32, (HTS, 128), 1) < NI
    height = lax.broadcasted_iota(jnp.int32, (HTS, 128), 0)
    second = two_stages(128, state, low, high, left, right, ground, mid, ghost)

    def emit(r, one, two):
        for i in range(COMPS):
            both = jnp.where(near, one[i], pltpu.roll(two[i], NI, 1))
            packed[pl.ds(i * HTS * LONG + r, HTS, stride=LONG), :] = both

    @pl.loop(0, HALF - 1, unroll=3)
    def _(l):
        emit(l + 1, second(l), second(l + LONG))

    weight = corner_weight(128)

    def beyond(row):
        at, end = 32 + row * (ROWS - 1), row * (ROWS - 1)
        w_low = jnp.where(lowest_slab(), ground[0, end : end + 1], low[at : at + 1])
        return (w_low, high[at : at + 1]), (low[128 + row : 129 + row], high[128 + row : 129 + row])

    def owed(row, sign):
        out = [jnp.zeros((HTS, 128), jnp.float32)] * 2
        for below, above in beyond(row):
            below, above = [(by * weight) * x[:, 0:128] for by, x in ((-sign, below), (sign, above))]
            out.append(jnp.where(height == HTS - 1, above, jnp.where(height == 0, below, 0.0)))
        return out

    emit(0, owed(0, 1.0), second(HALF))
    emit(HALF, second(HALF - 1), owed(1, -1.0))

    for out, row in ((to_left, 0), (to_right, 1)):
        (w_low, w_high), (v_low, v_high) = beyond(row)
        out[...] = jnp.concatenate([w_low, w_high, v_low, v_high, jnp.zeros((4, NR), jnp.float32)], 0)


def outer_kernel(state, low, high, left, right, ground, stepped, mid, ghost):
    second = two_stages(NR, state, low, high, left, right, ground, mid, ghost)

    @pl.loop(0, ROWS, unroll=2)
    def _(j):
        for i, value in enumerate(second(j)):
            stepped[i, j] = value


def filter_kernel(there, there_small, back, back_small, turn, cutoff, x_ref, o_ref):
    n, m = NA // 4, SECTORS // 2 * LONG
    first, second = x_ref[:m], x_ref[m:]
    h = MODES // 2
    mode = lax.broadcasted_iota(jnp.int32, (h, 128), 0) * 2
    near = lax.broadcasted_iota(jnp.int32, (h, 128), 1) < NI
    limit = jnp.concatenate([cutoff[...], cutoff[...]], 1)
    outs = []
    for parity in range(2):
        folded = first + second if parity == 0 else first - second
        cs, sn, cs_back, sn_back, weight = [turn[parity, :, k : k + 1] for k in range(5)]
        coef = product((there[parity], there_small[parity]), split(folded), ((1,), (0,)))
        a, b = coef[:h], coef[h:]
        a_all = jnp.where(near, a, a * cs - b * sn)
        b_all = jnp.where(near, b, a * sn + b * cs)
        keep = jnp.where(mode + parity < limit, weight, 0.0)
        a_all = (a_all + pltpu.roll(a_all, NI, 1)) * keep
        b_all = (b_all + pltpu.roll(b_all, NI, 1)) * keep
        a_back = jnp.where(near, a_all, a_all * cs_back + b_all * sn_back)
        b_back = jnp.where(near, b_all, b_all * cs_back - a_all * sn_back)
        both = jnp.concatenate([a_back, b_back], 0)
        outs.append(product((back[parity], back_small[parity]), split(both), ((0,), (0,))))
    o_ref[:n] = outs[0] + outs[1]
    o_ref[n:] = outs[0] - outs[1]


def merge_kernel(stepped, back, left_corner, right_corner, out, rows, tile, beside, edges, sems, edge_sems):
    near = lax.broadcasted_iota(jnp.int32, (HTS, 128), 1) < NI
    height = lax.broadcasted_iota(jnp.int32, (HTS, NR), 0)
    loads = [
        pltpu.make_async_copy(stepped.at[i, :, :, pl.ds(0, 128)], beside.at[i], sems.at[0, i]) for i in range(COMPS)
    ]
    places = [(k, i, j) for k, (i, j) in enumerate(((2, 0), (2, ROWS - 1), (3, 0), (3, ROWS - 1)))]
    edge_loads = [
        pltpu.make_async_copy(stepped.at[i, j, :, pl.ds(128, 128)], edges.at[k], edge_sems.at[0, k]) for k, i, j in places
    ]
    for copy in loads + edge_loads:
        copy.start()

    weight = corner_weight(NR)
    owed = {}
    for k, i, j in places:
        corner, sign = (left_corner, -1.0) if j == 0 else (right_corner, 1.0)
        at = 2 * (i - 2)
        below, above = (-sign * weight) * corner[at : at + 1], (sign * weight) * corner[at + 1 : at + 2]
        owed[i, j] = jnp.where(height == HTS - 1, above, jnp.where(height == 0, below, 0.0))

    for i in range(COMPS * HTS):
        rows[pl.ds(i // HTS * HTS * HALF + i % HTS, HALF, stride=HTS), :] = back[i * HALF : (i + 1) * HALF]
    stores = []
    for i in range(COMPS):
        loads[i].wait()
        for j in (0, ROWS - 1):
            if i >= 2:
                beside[i, j] = beside[i, j] + owed[i, j][:, 0:128]
        for l in range(HALF):
            at = (i * HALF + l) * HTS
            both = rows[at : at + HTS]
            tile[i, l] = jnp.where(near, both, beside[i, l])
            tile[i, l + HALF] = jnp.where(near, pltpu.roll(both, NI, 1), beside[i, l + HALF])
        stores.append(pltpu.make_async_copy(tile.at[i], out.at[i, :, :, pl.ds(0, 128)], sems.at[1, i]))
        stores[i].start()
    for k, i, j in places:
        edge_loads[k].wait()
        edges[k] = edges[k] + owed[i, j][:, 128:NR]
        stores.append(pltpu.make_async_copy(edges.at[k], out.at[i, j, :, pl.ds(128, 128)], edge_sems.at[1, k]))
        stores[-1].start()
    for copy in stores:
        copy.wait()


def per_device(state, zone_id, ground_aux, resistance, relax_rate, cutoff):
    f32 = jnp.float32
    vmem = pl.BlockSpec(memory_space=pltpu.VMEM)
    smem = pl.BlockSpec(memory_space=pltpu.SMEM)
    anywhere = pl.BlockSpec(memory_space=pl.ANY)

    def call(kernel, mib=8, **more):
        return pl.pallas_call(kernel, compiler_params=pltpu.CompilerParams(vmem_limit_bytes=mib * 2**20), **more)

    def shapes(*dims):
        return tuple(jax.ShapeDtypeStruct(d, f32) for d in dims)

    ht_message, az_message = (HT_ROWS, NR), (AZ_ROWS, NR)
    az_then, ht_first, az_first, ht_then = call(
        pack_kernel,
        out_shape=shapes((AZ_LONG, NR), ht_message, az_message, ht_message),
        in_specs=[vmem],
        out_specs=(vmem,) * 4,
        scratch_shapes=[pltpu.VMEM(m, f32) for m in (ht_message, ht_message, az_message, az_message)],
        name="pack",
    )(state)
    ground = call(
        ground_kernel,
        out_shape=shapes((3, ROWS, NR))[0],
        in_specs=[smem] * 2 + [vmem] * 3,
        out_specs=vmem,
        name="ground",
    )(resistance, relax_rate, state, zone_id, ground_aux)
    def swap(x, axes, size, start, closed):
        pairs = [(i % size, (i + 1) % size) for i in range(start, size if closed else size - 1, 2)]
        return lax.ppermute(x, axes, pairs + [(b, a) for a, b in pairs])

    az_then = swap(az_then, AZ, SECTORS, 1, True)
    ht_then = swap(ht_then, HT, 4, 1, False)
    az_first = swap(az_first, AZ, SECTORS, 0, True)
    ht_first = swap(ht_first, HT, 4, 0, False)

    def scratch(width):
        return [pltpu.VMEM((COMPS, ROWS + 2, HTS, width), f32), pltpu.VMEM((8, ROWS, width), f32)]

    packed, low, high, left, right, to_left, to_right = call(
        inner_kernel,
        mib=12,
        out_shape=shapes(
            (COMPS * HTS * LONG, 128), ht_message, ht_message, az_message, az_message, (8, NR), (8, NR)
        ),
        in_specs=[vmem] * 6,
        out_specs=(vmem,) * 7,
        scratch_shapes=scratch(128),
        cost_estimate=pl.CostEstimate(flops=10**7, bytes_accessed=6 * 10**6, transcendentals=0),
        name="inner",
    )(state, az_then, ht_first, az_first, ht_then, ground)
    circle = lax.all_to_all(packed.reshape(SECTORS, LONG, 1, 128), SPREAD, 0, 0, tiled=True)
    left_corner = lax.ppermute(to_right, AZ, [(i, (i + 1) % SECTORS) for i in range(SECTORS)])
    right_corner = lax.ppermute(to_left, AZ, [((i + 1) % SECTORS, i) for i in range(SECTORS)])
    stepped = call(
        outer_kernel,
        mib=16,
        out_shape=shapes((COMPS, ROWS, HTS, NR))[0],
        in_specs=[vmem] * 6,
        out_specs=vmem,
        scratch_shapes=scratch(NR),
        cost_estimate=pl.CostEstimate(flops=2 * 10**7, bytes_accessed=2 * 10**7, transcendentals=0),
        name="outer",
    )(state, low, high, left, right, ground)
    kept = call(
        filter_kernel, out_shape=shapes((NA // 2, 128))[0], in_specs=[vmem] * 7, out_specs=vmem, name="filter"
    )(*map(jnp.asarray, mode_tables()), cutoff.reshape(1, NI), circle.reshape(SECTORS * LONG, 128))
    back = lax.all_to_all(kept.reshape(SECTORS, HALF, 128), SPREAD, 0, 0, tiled=True)
    return call(
        merge_kernel,
        out_shape=jax.ShapeDtypeStruct(stepped.shape, f32),
        in_specs=[anywhere] + [vmem] * 3,
        out_specs=anywhere,
        scratch_shapes=[
            pltpu.VMEM((COMPS * HTS * HALF, 128), f32),
            pltpu.VMEM((COMPS, ROWS, HTS, 128), f32),
            pltpu.VMEM((COMPS, ROWS, HTS, 128), f32),
            pltpu.VMEM((4, HTS, 128), f32),
            pltpu.SemaphoreType.DMA((2, COMPS)),
            pltpu.SemaphoreType.DMA((2, 4)),
        ],
        input_output_aliases={0: 0},
        name="merge",
    )(stepped, back.reshape(COMPS * HTS * HALF, 128), left_corner, right_corner)


def solution(mesh):
    fine = Mesh(mesh.devices.reshape(4, 2, 8, 2, 2), AZ + HT)
    return jax.shard_map(
        per_device,
        mesh=fine,
        in_specs=(P(None, AZ, HT, None), P(AZ, None), P(AZ, None), P(), P(), P()),
        out_specs=P(None, AZ, HT, None),
        check_vma=False,
    )
```

```python
import functools
import math

import jax
import jax.numpy as jnp
import numpy as np
from jax import lax
from jax.experimental import pallas as pl
from jax.experimental.pallas import tpu as pltpu
from jax.sharding import Mesh, PartitionSpec as P

NA = 2048
NI = 64
MODES = 128
ZONES = 8
SECTORS = 64
ROWS = NA // SECTORS
HALF = ROWS // 2
LONG = HALF + 1
HTS = 16
NR = 256
COMPS = 4
DT = 0.4

AZ = ("y", "x", "z")
SPREAD = AZ
HT = ("hx", "core")


def mode_tables():
    first = np.arange(SECTORS // 2)[:, None] * ROWS
    there = (first - 1 + np.arange(LONG)[None, :]).reshape(-1)
    back = (first + np.arange(HALF)[None, :]).reshape(-1)
    tables = []
    for parity in range(2):
        modes = np.arange(parity, MODES, 2)
        waves = []
        for azimuth in (there, back):
            phase = (modes[:, None] * azimuth[None, :] % NA) * (2.0 * math.pi / NA)
            waves.append(np.concatenate([np.cos(phase), np.sin(phase)], 0))
        more = np.zeros((MODES // 2, 128))
        for k, by in enumerate((LONG, HALF)):
            turn = (modes * by % NA) * (2.0 * math.pi / NA)
            more[:, 2 * k] = np.cos(turn)
            more[:, 2 * k + 1] = np.sin(turn)
        more[:, 4] = np.where(modes == 0, 1.0, 2.0) / NA
        tables.append((*waves, more))
    there, back, turns = [np.stack(t).astype(np.float32) for t in zip(*tables)]
    return (*split(there), *split(back), turns)


def split(x):
    x = x.astype(np.float32) if isinstance(x, np.ndarray) else x
    large = x.astype(jnp.bfloat16)
    return large, (x - large.astype(jnp.float32)).astype(jnp.bfloat16)


def product(a, b, dims):
    dot = functools.partial(lax.dot_general, dimension_numbers=(dims, ((), ())), preferred_element_type=jnp.float32)
    return dot(a[0], b[0]) + (dot(a[0], b[1]) + dot(a[1], b[0]))


def radial_diff(x):
    n = x.shape[-1]
    lane = lax.broadcasted_iota(jnp.int32, (1, n), 1)
    after = jnp.where(lane == NR - 1, 0.0, 0.5)
    before = jnp.where(lane == 0, 0.0, 0.5)
    return after * pltpu.roll(x, n - 1, x.ndim - 1) - before * pltpu.roll(x, 1, x.ndim - 1)


def row_diff(x, low, high):
    up = jnp.concatenate([x[1:], high], 0)
    down = jnp.concatenate([low, x[:-1]], 0)
    return 0.5 * (up - down)


def radial_rates(n):
    lane = lax.broadcasted_iota(jnp.int32, (1, n), 1).astype(jnp.float32)
    inv_r = 1.0 / (NA / (2.0 * math.pi) + lane)
    return inv_r, 0.5 * (NA / (2.0 * math.pi)) * inv_r


def plane(state, comp, height, width=NR):
    return state[comp, :, height, 0:width]


def lookup(ids, table):
    out = jnp.zeros(ids.shape, jnp.float32)
    for k in range(ZONES):
        out = jnp.where(ids == k, table[k], out)
    return out


def odd_slab():
    return lax.axis_index("core") == 1


def odd_sector():
    return lax.rem(lax.axis_index("z"), 2) == 1


def lowest_slab():
    return lax.axis_index("hx") * 2 + lax.axis_index("core") == 0


def highest_slab():
    return lax.axis_index("hx") * 2 + lax.axis_index("core") == 3


HT_ROWS = 136
AZ_ROWS = 64
AZ_LONG = 144


def pack_kernel(state, az_first, az_then, ht_then, ht_first, up, down, to_left, to_right):
    inv_r, half_arc = radial_rates(NR)
    zero = jnp.zeros((1, NR), jnp.float32)
    for out, edge, inside, sign in ((up, HTS - 1, HTS - 2, 1.0), (down, 0, 1, -1.0)):
        p, w, u, v = [plane(state, i, edge) for i in (0, 3, 1, 2)]
        p_in, w_in = plane(state, 0, inside), plane(state, 3, inside)
        out[0:32] = p
        out[32:64] = w
        turn = 2.0 * row_diff(v, zero, zero) * half_arc
        out[64:96] = p - DT * (radial_diff(u) + u * inv_r + turn - (0.5 * sign) * w_in)
        out[96:128] = w + (0.5 * DT * sign) * p_in
        out[128:129] = v[0:1]
        out[129:130] = v[ROWS - 1 : ROWS]
        out[130:HT_ROWS] = jnp.zeros((HT_ROWS - 130, NR), jnp.float32)

    for out, j, inside, sign in ((to_right, ROWS - 1, ROWS - 2, 1.0), (to_left, 0, 1, -1.0)):
        p, u, v, w = [state[i, j] for i in range(4)]
        out[0:16] = p
        out[16:32] = v
        rate = radial_diff(u) + u * inv_r + row_diff(w, zero, zero) - sign * half_arc * state[2, inside]
        out[32:48] = p - DT * rate
        out[48:64] = v + (DT * sign) * half_arc * state[0, inside]

    for odd, one, two, ahead, behind in (
        (odd_slab(), ht_first, ht_then, up, down),
        (odd_sector(), az_first.at[0:AZ_ROWS], az_then.at[0:AZ_ROWS], to_right, to_left),
    ):
        one[...] = jnp.where(odd, behind[...], ahead[...])
        two[...] = jnp.where(odd, ahead[...], behind[...])
    for out in (az_first, az_then):
        out[AZ_ROWS:AZ_LONG] = jnp.zeros((AZ_LONG - AZ_ROWS, NR), jnp.float32)


def ground_kernel(resistance, relax, state, zone, aux, ground):
    ids, q = zone[...], aux[...]
    p0, w0 = plane(state, 0, 0), plane(state, 3, 0)
    twice = 2.0 * (1.0 / lookup(ids, resistance))
    ground[0] = twice * (p0 - q) - w0
    ground[1] = twice
    ground[2] = q + DT * lookup(ids, relax) * (p0 - q)


def unswap(odd, first, then, behind, ahead):
    behind[...] = jnp.where(odd, first[...], then[...])
    ahead[...] = jnp.where(odd, then[...], first[...])


def two_stages(width, state, low, high, left, right, ground, mid, ghost):
    on_ground, on_top = lowest_slab(), highest_slab()
    inv_r, half_arc = radial_rates(width)
    cols = slice(0, width)
    turn = DT * half_arc

    p0, p1, u0, v0, w0, w1 = [plane(state, i, k, width) for i, k in ((0, 0), (0, 1), (1, 0), (2, 0), (3, 0), (3, 1))]
    p15, w15 = plane(state, 0, HTS - 1, width), plane(state, 3, HTS - 1, width)
    bp = jnp.where(on_ground, p0, low[0:32, cols])
    bw = jnp.where(on_ground, ground[0, :, cols], low[32:64, cols])
    ghost[0], ghost[1], ghost[2], ghost[3] = bp, bw, high[0:32, cols], high[32:64, cols]

    top_p = high[64:96, cols] + (0.5 * DT) * w15
    top_w = high[96:128, cols] + (0.5 * DT) * p15
    low_p = low[64:96, cols] - (0.5 * DT) * w0
    low_w = low[96:128, cols] - (0.5 * DT) * p0
    v_diff = 2.0 * row_diff(v0, left[16:17, cols], right[16:17, cols]) * half_arc
    mid_p0 = p0 - DT * (radial_diff(u0) + u0 * inv_r + v_diff + 0.5 * (w1 - bw))
    mid_w0 = w0 - (0.5 * DT) * (p1 - bp)
    ghost[4] = jnp.where(on_ground, mid_p0, low_p)
    ghost[5] = jnp.where(on_ground, ground[1, :, cols] * (mid_p0 - ground[2, :, cols]) - mid_w0, low_w)
    ghost[6] = jnp.where(on_top, 0.0, top_p)
    ghost[7] = jnp.where(on_top, 0.0, top_w)

    mid[0, 0] = left[32:48, cols] - turn * state[2, 0, :, cols]
    mid[2, 0] = left[48:64, cols] - turn * state[0, 0, :, cols]
    mid[0, ROWS + 1] = right[32:48, cols] + turn * state[2, ROWS - 1, :, cols]
    mid[2, ROWS + 1] = right[48:64, cols] + turn * state[0, ROWS - 1, :, cols]

    def rates(p, u, v_diff, p_diff, w, j, first):
        p_low, w_low, p_high, w_high = [ghost[first + i, pl.ds(j, 1)] for i in range(4)]
        return (
            radial_diff(u) + u * inv_r + v_diff * half_arc + row_diff(w, w_low, w_high),
            radial_diff(p),
            half_arc * p_diff,
            row_diff(p, p_low, p_high),
        )

    def first(j, p_diff, v_diff):
        p, u, v, w = [state[i, j, :, cols] for i in range(4)]
        for i, (s, rate) in enumerate(zip((p, u, v, w), rates(p, u, v_diff, p_diff, w, j, 0))):
            mid[i, j + 1] = s - DT * rate

    first(0, state[0, 1, :, cols] - left[0:16, cols], state[2, 1, :, cols] - left[16:32, cols])
    end = ROWS - 2
    first(ROWS - 1, right[0:16, cols] - state[0, end, :, cols], right[16:32, cols] - state[2, end, :, cols])

    @pl.loop(1, ROWS - 1, unroll=5)
    def _(j):
        first(
            j,
            state[0, j + 1, :, cols] - state[0, j - 1, :, cols],
            state[2, j + 1, :, cols] - state[2, j - 1, :, cols],
        )

    def second(j):
        p, u, v, w = [mid[i, j + 1] for i in range(4)]
        found = rates(p, u, mid[2, j + 2] - mid[2, j], mid[0, j + 2] - mid[0, j], w, j, 4)
        return [0.5 * (state[i, j, :, cols] + m - DT * r) for i, (m, r) in enumerate(zip((p, u, v, w), found))]

    return second


def corner_weight(width):
    return (0.5 * DT) * (0.5 * DT) * radial_rates(width)[1]


def inner_kernel(
    state, az_first, az_then, ht_then, ht_first, ground, packed, low, high, left, right, to_left, to_right, mid, ghost
):
    unswap(odd_slab(), ht_first, ht_then, low, high)
    unswap(odd_sector(), az_first.at[0:AZ_ROWS], az_then.at[0:AZ_ROWS], left, right)
    near = lax.broadcasted_iota(jnp.int32, (HTS, 128), 1) < NI
    height = lax.broadcasted_iota(jnp.int32, (HTS, 128), 0)
    second = two_stages(128, state, low, high, left, right, ground, mid, ghost)

    def emit(r, one, two):
        for i in range(COMPS):
            both = jnp.where(near, one[i], pltpu.roll(two[i], NI, 1))
            packed[pl.ds(i * HTS * LONG + r, HTS, stride=LONG), :] = both

    @pl.loop(0, HALF - 1, unroll=3)
    def _(l):
        emit(l + 1, second(l), second(l + LONG))

    weight = corner_weight(128)

    def beyond(row):
        at, end = 32 + row * (ROWS - 1), row * (ROWS - 1)
        w_low = jnp.where(lowest_slab(), ground[0, end : end + 1], low[at : at + 1])
        return (w_low, high[at : at + 1]), (low[128 + row : 129 + row], high[128 + row : 129 + row])

    def owed(row, sign):
        out = [jnp.zeros((HTS, 128), jnp.float32)] * 2
        for below, above in beyond(row):
            below, above = [(by * weight) * x[:, 0:128] for by, x in ((-sign, below), (sign, above))]
            out.append(jnp.where(height == HTS - 1, above, jnp.where(height == 0, below, 0.0)))
        return out

    emit(0, owed(0, 1.0), second(HALF))
    emit(HALF, second(HALF - 1), owed(1, -1.0))

    for out, row in ((to_left, 0), (to_right, 1)):
        (w_low, w_high), (v_low, v_high) = beyond(row)
        out[...] = jnp.concatenate([w_low, w_high, v_low, v_high, jnp.zeros((4, NR), jnp.float32)], 0)


def outer_kernel(state, low, high, left, right, ground, stepped, mid, ghost):
    second = two_stages(NR, state, low, high, left, right, ground, mid, ghost)

    @pl.loop(0, ROWS, unroll=2)
    def _(j):
        for i, value in enumerate(second(j)):
            stepped[i, j] = value


def filter_kernel(there, there_small, back, back_small, turn, cutoff, x_ref, o_ref):
    n, m = NA // 4, SECTORS // 2 * LONG
    first, second = x_ref[:m], x_ref[m:]
    h = MODES // 2
    mode = lax.broadcasted_iota(jnp.int32, (h, 128), 0) * 2
    near = lax.broadcasted_iota(jnp.int32, (h, 128), 1) < NI
    limit = jnp.concatenate([cutoff[...], cutoff[...]], 1)
    outs = []
    for parity in range(2):
        folded = first + second if parity == 0 else first - second
        cs, sn, cs_back, sn_back, weight = [turn[parity, :, k : k + 1] for k in range(5)]
        coef = product((there[parity], there_small[parity]), split(folded), ((1,), (0,)))
        a, b = coef[:h], coef[h:]
        a_all = jnp.where(near, a, a * cs - b * sn)
        b_all = jnp.where(near, b, a * sn + b * cs)
        keep = jnp.where(mode + parity < limit, weight, 0.0)
        a_all = (a_all + pltpu.roll(a_all, NI, 1)) * keep
        b_all = (b_all + pltpu.roll(b_all, NI, 1)) * keep
        a_back = jnp.where(near, a_all, a_all * cs_back + b_all * sn_back)
        b_back = jnp.where(near, b_all, b_all * cs_back - a_all * sn_back)
        both = jnp.concatenate([a_back, b_back], 0)
        outs.append(product((back[parity], back_small[parity]), split(both), ((0,), (0,))))
    o_ref[:n] = outs[0] + outs[1]
    o_ref[n:] = outs[0] - outs[1]


def merge_kernel(stepped, back, left_corner, right_corner, out, rows, tile, beside, edges, sems, edge_sems):
    near = lax.broadcasted_iota(jnp.int32, (HTS, 128), 1) < NI
    height = lax.broadcasted_iota(jnp.int32, (HTS, NR), 0)
    loads = [
        pltpu.make_async_copy(stepped.at[i, :, :, pl.ds(0, 128)], beside.at[i], sems.at[0, i]) for i in range(COMPS)
    ]
    places = [(k, i, j) for k, (i, j) in enumerate(((2, 0), (2, ROWS - 1), (3, 0), (3, ROWS - 1)))]
    edge_loads = [
        pltpu.make_async_copy(stepped.at[i, j, :, pl.ds(128, 128)], edges.at[k], edge_sems.at[0, k]) for k, i, j in places
    ]
    for copy in loads + edge_loads:
        copy.start()

    weight = corner_weight(NR)
    owed = {}
    for k, i, j in places:
        corner, sign = (left_corner, -1.0) if j == 0 else (right_corner, 1.0)
        at = 2 * (i - 2)
        below, above = (-sign * weight) * corner[at : at + 1], (sign * weight) * corner[at + 1 : at + 2]
        owed[i, j] = jnp.where(height == HTS - 1, above, jnp.where(height == 0, below, 0.0))

    for i in range(COMPS * HTS):
        rows[pl.ds(i // HTS * HTS * HALF + i % HTS, HALF, stride=HTS), :] = back[i * HALF : (i + 1) * HALF]
    stores = []
    for i in range(COMPS):
        loads[i].wait()
        for j in (0, ROWS - 1):
            if i >= 2:
                beside[i, j] = beside[i, j] + owed[i, j][:, 0:128]
        for l in range(HALF):
            at = (i * HALF + l) * HTS
            both = rows[at : at + HTS]
            tile[i, l] = jnp.where(near, both, beside[i, l])
            tile[i, l + HALF] = jnp.where(near, pltpu.roll(both, NI, 1), beside[i, l + HALF])
        stores.append(pltpu.make_async_copy(tile.at[i], out.at[i, :, :, pl.ds(0, 128)], sems.at[1, i]))
        stores[i].start()
    for k, i, j in places:
        edge_loads[k].wait()
        edges[k] = edges[k] + owed[i, j][:, 128:NR]
        stores.append(pltpu.make_async_copy(edges.at[k], out.at[i, j, :, pl.ds(128, 128)], edge_sems.at[1, k]))
        stores[-1].start()
    for copy in stores:
        copy.wait()


def per_device(state, zone_id, ground_aux, resistance, relax_rate, cutoff):
    f32 = jnp.float32
    vmem = pl.BlockSpec(memory_space=pltpu.VMEM)
    smem = pl.BlockSpec(memory_space=pltpu.SMEM)
    anywhere = pl.BlockSpec(memory_space=pl.ANY)

    def call(kernel, mib=8, **more):
        return pl.pallas_call(kernel, compiler_params=pltpu.CompilerParams(vmem_limit_bytes=mib * 2**20), **more)

    def shapes(*dims):
        return tuple(jax.ShapeDtypeStruct(d, f32) for d in dims)

    ht_message, az_message = (HT_ROWS, NR), (AZ_ROWS, NR)
    az_first, az_then, ht_then, ht_first = call(
        pack_kernel,
        out_shape=shapes((AZ_LONG, NR), (AZ_LONG, NR), ht_message, ht_message),
        in_specs=[vmem],
        out_specs=(vmem,) * 4,
        scratch_shapes=[pltpu.VMEM(m, f32) for m in (ht_message, ht_message, az_message, az_message)],
        name="pack",
    )(state)
    ground = call(
        ground_kernel,
        out_shape=shapes((3, ROWS, NR))[0],
        in_specs=[smem] * 2 + [vmem] * 3,
        out_specs=vmem,
        name="ground",
    )(resistance, relax_rate, state, zone_id, ground_aux)
    def swap(x, axes, size, start, closed):
        pairs = [(i % size, (i + 1) % size) for i in range(start, size if closed else size - 1, 2)]
        return lax.ppermute(x, axes, pairs + [(b, a) for a, b in pairs])

    az_then = swap(az_then, AZ, SECTORS, 1, True)
    ht_then = swap(ht_then, HT, 4, 1, False)
    az_first = swap(az_first, AZ, SECTORS, 0, True)
    ht_first = swap(ht_first, HT, 4, 0, False)

    def scratch(width):
        return [pltpu.VMEM((COMPS, ROWS + 2, HTS, width), f32), pltpu.VMEM((8, ROWS, width), f32)]

    packed, low, high, left, right, to_left, to_right = call(
        inner_kernel,
        mib=12,
        out_shape=shapes(
            (COMPS * HTS * LONG, 128), ht_message, ht_message, az_message, az_message, (8, NR), (8, NR)
        ),
        in_specs=[vmem] * 6,
        out_specs=(vmem,) * 7,
        scratch_shapes=scratch(128),
        cost_estimate=pl.CostEstimate(flops=10**7, bytes_accessed=6 * 10**6, transcendentals=0),
        name="inner",
    )(state, az_first, az_then, ht_then, ht_first, ground)
    circle = lax.all_to_all(packed.reshape(SECTORS, LONG, 1, 128), SPREAD, 0, 0, tiled=True)
    left_corner = lax.ppermute(to_right, AZ, [(i, (i + 1) % SECTORS) for i in range(SECTORS)])
    right_corner = lax.ppermute(to_left, AZ, [((i + 1) % SECTORS, i) for i in range(SECTORS)])
    stepped = call(
        outer_kernel,
        mib=16,
        out_shape=shapes((COMPS, ROWS, HTS, NR))[0],
        in_specs=[vmem] * 6,
        out_specs=vmem,
        scratch_shapes=scratch(NR),
        cost_estimate=pl.CostEstimate(flops=2 * 10**7, bytes_accessed=2 * 10**7, transcendentals=0),
        name="outer",
    )(state, low, high, left, right, ground)
    kept = call(
        filter_kernel, out_shape=shapes((NA // 2, 128))[0], in_specs=[vmem] * 7, out_specs=vmem, name="filter"
    )(*map(jnp.asarray, mode_tables()), cutoff.reshape(1, NI), circle.reshape(SECTORS * LONG, 128))
    back = lax.all_to_all(kept.reshape(SECTORS, HALF, 128), SPREAD, 0, 0, tiled=True)
    return call(
        merge_kernel,
        out_shape=jax.ShapeDtypeStruct(stepped.shape, f32),
        in_specs=[anywhere] + [vmem] * 3,
        out_specs=anywhere,
        scratch_shapes=[
            pltpu.VMEM((COMPS * HTS * HALF, 128), f32),
            pltpu.VMEM((COMPS, ROWS, HTS, 128), f32),
            pltpu.VMEM((COMPS, ROWS, HTS, 128), f32),
            pltpu.VMEM((4, HTS, 128), f32),
            pltpu.SemaphoreType.DMA((2, COMPS)),
            pltpu.SemaphoreType.DMA((2, 4)),
        ],
        input_output_aliases={0: 0},
        name="merge",
    )(stepped, back.reshape(COMPS * HTS * HALF, 128), left_corner, right_corner)


def solution(mesh):
    fine = Mesh(mesh.devices.reshape(4, 2, 8, 2, 2), AZ + HT)
    return jax.shard_map(
        per_device,
        mesh=fine,
        in_specs=(P(None, AZ, HT, None), P(AZ, None), P(AZ, None), P(), P(), P()),
        out_specs=P(None, AZ, HT, None),
        check_vma=False,
    )
```
